32 devices in a mesh: row: 4 (over y, core), col: 8 (over z, x).
Axes of the slice: x: 2, y: 2, z: 4, core: 2. Of those that a mesh axis runs over, the one named last changes fastest.
Arguments:
- positions: float32 [3, 32768], P(None, ('col', 'row')), may hold values from 0 to 16
- velocity: float32 [3, 32768], P(None, ('col', 'row')), may hold values from -6 to 6
- applied: float32 [3, 32768], P(None, ('col', 'row')), may hold values from -12 to 12
- suscept: float32 [32768], P(('col', 'row')), may hold values from 0.05 to 0.3
- contact_owner: int32 [8, 4, 8, 512], P('col', 'row'), may hold values from 0 to 1023
- contact_partner: int32 [8, 4, 8, 512], P('col', 'row'), may hold values from 0 to 1023
- contact_count: int32 [8, 4, 8], P('col', 'row'), may hold values from 1 to 512, as said below
Outputs:
- moments: float32 [3, 32768], P(None, ('col', 'row'))
- forces: float32 [3, 32768], P(None, ('col', 'row'))
The draws below stay inside these ranges and needn't reach their ends.
Inputs may be any that keep to these rules, and one draw needn't show every extreme that they name: `contact_count`: in every draw one column receives full blocks of 512 live slots from every device; the other columns' blocks are filled to different depths.
All inputs are finite; a program needn't handle non-finite values.
Results may differ from the reference program's by a relative error of at most 0.0003.
Values sent between devices are 32-bit elements; how exact they have to be, the bound alone decides.
No kernel may reach another device: no remote copies, remote signals or barrier semaphores. Data moves between devices by JAX's collectives and lax.ppermute only.
A program may use at most 64 MiB of HBM per device.

```python
import math
import jax
import jax.numpy as jnp
from jax import lax

PART_DEV = 1024
ITERS = 2
CAP = 512
NPART = 32768
N_ROW = 4
N_COL = 8


def draw_contact_count(key, part):
    key_heavy, key_upper, key_counts = jax.random.split(jax.random.fold_in(key, 17), 3)
    heavy_col = jax.random.randint(key_heavy, (), 0, N_COL)
    upper_bound = jax.random.randint(key_upper, (N_COL,), CAP // 2, CAP + 1)
    drawn_counts = jax.random.randint(key_counts, (N_COL, N_ROW, N_COL), 1, upper_bound[None, None, :] + 1)
    col_ids = jnp.arange(N_COL)
    return jnp.where((col_ids == heavy_col)[None, None, :], CAP, drawn_counts).astype(jnp.int32)


def plant(drawn, own_key, low, top_value):
    extent = drawn.shape
    index_at = [jax.random.randint(jax.random.fold_in(own_key, axis), (), 0, extent[axis]) for axis in range(len(extent))]
    drawn = drawn.at[tuple(index_at)].set(low)
    longest = extent.index(max(extent))
    index_at[longest] = (index_at[longest] + 1) % extent[longest]
    return drawn.at[tuple(index_at)].set(top_value)


def levels(stream_key, extent, cuts, smallest, largest):
    gain = 1.0
    for axis_at, parts in cuts:
        steps = jax.random.uniform(jax.random.fold_in(jax.random.fold_in(stream_key, 6), axis_at), (parts,), jnp.float32, smallest / len(cuts), largest / len(cuts))
        gain = gain * jnp.repeat(jnp.exp(steps), extent[axis_at] // parts).reshape((-1,) + (1,) * (len(extent) - 1 - axis_at))
    return gain


def normal_values(own_key, extent, scale, bound, pieces=(), held_as=jnp.bfloat16):
    drawn = scale * jax.random.normal(own_key, extent, jnp.float32)
    if pieces:
        drawn = drawn * levels(own_key, extent, pieces, -0.22, 0.18)
    return jnp.clip(drawn, -bound, bound).astype(held_as)


def setup_inputs(seed: int = 0) -> dict:
    keys = jax.random.split(jax.random.key(seed), 8)
    return {
        "positions": jnp.clip(16.0 * jax.random.uniform(keys[0], (3, NPART), jnp.float32) ** levels(keys[0], (3, NPART), ((1, 32),), -0.2, 0.2), 0.0, 16.0),
        "velocity": normal_values(keys[1], (3, NPART), 1.0, 6.0, ((1, 32),), jnp.float32),
        "applied": normal_values(keys[2], (3, NPART), 2.0, 12.0, ((1, 32),), jnp.float32),
        "suscept": jnp.clip(jnp.exp(math.log(0.3) - 1.7917595 * jax.random.uniform(keys[3], (NPART,), jnp.float32) ** levels(keys[3], (NPART,), ((0, 32),), -0.2, 0.2)), 0.05, 0.3),
        "contact_owner": plant(jax.random.randint(keys[4], (N_COL, N_ROW, N_COL, CAP), 0, PART_DEV), jax.random.fold_in(keys[4], 1), 0, PART_DEV - 1).astype(jnp.int32),
        "contact_partner": plant(jax.random.randint(keys[5], (N_COL, N_ROW, N_COL, CAP), 0, PART_DEV), jax.random.fold_in(keys[5], 1), 0, PART_DEV - 1).astype(jnp.int32),
        "contact_count": draw_contact_count(jax.random.fold_in(keys[7], 71), 0),
    }


def dipole_block(target_pos, target_ids, source_pos, source_mom, source_ids):
    offset = target_pos[:, :, None] - source_pos[:, None, :]
    radius_sq = lax.optimization_barrier(jnp.sum(offset * offset, axis=0)) + 1.0
    inverse_r = lax.rsqrt(radius_sq)
    inverse_cube = inverse_r * inverse_r * inverse_r
    inverse_fifth = inverse_cube * inverse_r * inverse_r
    keep_mask = target_ids[:, None] != source_ids[None, :]
    projection = lax.optimization_barrier(jnp.sum(offset * source_mom[:, None, :], axis=0))
    radial_coef = jnp.where(keep_mask, 3.0 * projection * inverse_fifth, 0.0)
    direct_coef = jnp.where(keep_mask, inverse_cube, 0.0)
    return lax.optimization_barrier(jnp.sum(radial_coef[None] * offset, axis=2)) - lax.optimization_barrier(jnp.sum(direct_coef[None] * source_mom[:, None, :], axis=2))

def column_field(column_pos, column_mom):
    column_len = column_pos.shape[1]
    block_len = math.gcd(column_len, 512)
    nblocks = column_len // block_len
    all_ids = jnp.arange(column_len, dtype=jnp.int32)
    target_blocks = (column_pos.reshape(3, nblocks, block_len).transpose(1, 0, 2), all_ids.reshape(nblocks, block_len))

    def per_block(target_block):
        return dipole_block(target_block[0], target_block[1], column_pos, column_mom, all_ids)
    result_blocks = lax.map(per_block, target_blocks)
    return result_blocks.transpose(1, 0, 2).reshape(3, column_len)

def pair_force(one_side, other_side):
    separation = one_side[0:3] - other_side[0:3]
    distance = jnp.sqrt(lax.optimization_barrier(jnp.sum(separation * separation, axis=0)) + 1.0)
    normal = separation / distance
    mom_one = one_side[6:9]
    mom_other = other_side[6:9]
    along_one = lax.optimization_barrier(jnp.sum(mom_one * normal, axis=0))
    along_other = lax.optimization_barrier(jnp.sum(mom_other * normal, axis=0))
    mom_dot = lax.optimization_barrier(jnp.sum(mom_one * mom_other, axis=0))
    magnetic = 3.0 * (along_one * mom_other + along_other * mom_one + (mom_dot - 5.0 * along_one * along_other) * normal)
    spring = -0.03 * (distance - 1.0) * normal
    rel_speed = lax.optimization_barrier(jnp.sum((one_side[3:6] - other_side[3:6]) * normal, axis=0))
    damping = -0.5 * rel_speed * normal
    return magnetic + spring + damping

def reference(positions, velocity, applied, suscept, contact_owner, contact_partner, contact_count):
    column_len = PART_DEV * N_ROW
    pos_cols = positions.reshape(3, N_COL, column_len).transpose(1, 0, 2)
    moments = suscept[None, :] * applied
    for iteration in range(ITERS):
        mom_cols = moments.reshape(3, N_COL, column_len).transpose(1, 0, 2)
        field_cols = lax.map(lambda pair_cols: column_field(pair_cols[0], pair_cols[1]), (pos_cols, mom_cols))
        field_sum = field_cols.transpose(1, 0, 2).reshape(3, N_COL * column_len)
        moments = suscept[None, :] * (applied + field_sum)
    col_ids = jnp.arange(N_COL, dtype=jnp.int32)
    row_ids = jnp.arange(N_ROW, dtype=jnp.int32)
    owner_global = (col_ids[:, None, None, None] * N_ROW + row_ids[None, :, None, None]) * PART_DEV + contact_owner
    partner_global = (col_ids[None, None, :, None] * N_ROW + row_ids[None, :, None, None]) * PART_DEV + contact_partner
    slot_ids = jnp.arange(CAP, dtype=jnp.int32)
    live_mask = (slot_ids[None, None, None, :] < contact_count[:, :, :, None]).astype(jnp.float32).reshape(-1)
    state_rows = jnp.concatenate([positions, velocity, moments], axis=0)
    owner_flat = owner_global.reshape(-1).astype(jnp.int32)
    partner_flat = partner_global.reshape(-1).astype(jnp.int32)
    owner_rows = jnp.take(state_rows, owner_flat, axis=1)
    partner_rows = jnp.take(state_rows, partner_flat, axis=1)
    slot_force = pair_force(owner_rows, partner_rows) * live_mask[None, :]
    forces = jnp.zeros_like(positions).at[:, owner_flat].add(slot_force).at[:, partner_flat].add(-slot_force)
    return (moments, forces)
```

```python
import functools
import math

import jax
import jax.numpy as jnp
from jax import lax
from jax.experimental import pallas as pl
from jax.experimental.pallas import tpu as pltpu
from jax.sharding import PartitionSpec as P

ITERS = 2
LANES = 128
SUBS = 8
FEATURES = 16
KEEP_BYTES = 20 * 2**20
F32 = jnp.float32
BF16 = jnp.bfloat16
VMEM = pl.BlockSpec(memory_space=pltpu.VMEM)
SMEM = pl.BlockSpec(memory_space=pltpu.SMEM)


def split3(value):
    high = value.astype(BF16)
    rest = value - high.astype(F32)
    middle = rest.astype(BF16)
    return high, middle, (rest - middle.astype(F32)).astype(BF16)


def norm_sq(pos):
    return pos[0:1] * pos[0:1] + pos[1:2] * pos[1:2] + pos[2:3] * pos[2:3]


def distance_rows(pos):
    high, middle, low = split3(pos)
    norms = split3(norm_sq(pos))
    ones = tuple(jnp.ones_like(n) for n in norms)
    target = jnp.concatenate((high, high, middle, middle, high, low) + norms + ones, axis=0)
    doubled = tuple((-2.0 * p.astype(F32)).astype(BF16) for p in (high, middle, high, middle, low, high))
    source = jnp.concatenate(doubled + ones + norms, axis=0)
    return target, source


def moment_rows(pos, mom):
    outer = [mom[a : a + 1] * pos[b : b + 1] for a in range(3) for b in range(3)]
    along = outer[0] + outer[4] + outer[8]
    square = norm_sq(pos)
    mixed = [3.0 * along * pos[a : a + 1] - square * mom[a : a + 1] for a in range(3)]
    rows = jnp.concatenate([mom] + outer + mixed + [along], axis=0)
    return jnp.concatenate(split3(rows), axis=0)


def field_from_sums(sums, pos, mom):
    total = sums[0:FEATURES] + sums[FEATURES : 2 * FEATURES] + sums[2 * FEATURES : 3 * FEATURES]
    x = [pos[a : a + 1] for a in range(3)]
    m = [total[a : a + 1] for a in range(3)]

    def outer(a, b):
        return total[3 + 3 * a + b : 4 + 3 * a + b]

    trace = outer(0, 0) + outer(1, 1) + outer(2, 2)
    scale_sq = norm_sq(pos) + 1.0
    along = m[0] * x[0] + m[1] * x[1] + m[2] * x[2] - trace
    parts = []
    for a in range(3):
        by_column = outer(0, a) * x[0] + outer(1, a) * x[1] + outer(2, a) * x[2]
        by_row = outer(a, 0) * x[0] + outer(a, 1) * x[1] + outer(a, 2) * x[2]
        parts.append(
            3.0 * (along * x[a] - by_column)
            + 2.0 * by_row
            + total[12 + a : 13 + a]
            - scale_sq * m[a]
            + mom[a : a + 1]
        )
    return jnp.concatenate(parts, axis=0)


def pair_coefficient(radius_sq):
    inverse = lax.rsqrt(radius_sq)
    square = inverse * inverse
    fifth = square * square * inverse
    high = fifth.astype(BF16)
    return high, (fifth - high.astype(F32)).astype(BF16)


def center_of(pos):
    return jnp.sum(pos, axis=1, keepdims=True) * (1.0 / pos.shape[1])


def add_blocks(target_pos, source_pos, source_mom, block, high_ref, low_ref, make):
    if make:
        target_rows, unused = distance_rows(target_pos)
        unused, source_rows = distance_rows(source_pos)
    moments = moment_rows(source_pos, source_mom)
    sums = None
    for start in range(0, source_pos.shape[1], block):
        part = slice(start, start + block)
        if make:
            radius_sq = (
                lax.dot_general(
                    source_rows[:, part],
                    target_rows,
                    (((0,), (0,)), ((), ())),
                    preferred_element_type=F32,
                )
                + 1.0
            )
            high, low = pair_coefficient(radius_sq)
            if high_ref is not None:
                high_ref[part, :] = high
                low_ref[part, :] = low
        else:
            high, low = high_ref[part, :], low_ref[part, :]
        here = jnp.dot(moments[:, part], high, preferred_element_type=F32) + jnp.dot(
            moments[:, part], low, preferred_element_type=F32
        )
        sums = here if sums is None else sums + here
    return sums


def pack_kernel(pos, vel, applied, suscept, owner, partner, count, send, row_send):
    groups = pos.shape[1] // LANES
    slots = owner.shape[1] // LANES
    columns = owner.shape[0]
    row_send[0:3, :] = pos[...]
    row_send[3:6, :] = suscept[...] * applied[...]
    row_send[6:8, :] = jnp.zeros_like(row_send[6:8, :])
    for c in range(3):
        for g in range(groups):
            lanes = slice(g * LANES, (g + 1) * LANES)
            send[0, c * groups + g : c * groups + g + 1, :] = pos[c : c + 1, lanes]
            row = (3 + c) * groups + g
            send[0, row : row + 1, :] = vel[c : c + 1, lanes]
    for e in range(1, columns):
        send[e, 0 : 6 * groups, :] = send[0, 0 : 6 * groups, :]
    for q in range(slots):
        lanes = slice(q * LANES, (q + 1) * LANES)
        send[:, 6 * groups + q, :] = owner[:, lanes].astype(F32)
        send[:, 6 * groups + slots + q, :] = partner[:, lanes].astype(F32)
    tail = 6 * groups + 2 * slots
    for e in range(columns):
        send[e, tail:, :] = jnp.full((send.shape[1] - tail, LANES), count[e].astype(F32))


def first_kernel(block, own, sources, applied, suscept, moments, *kept):
    center = center_of(own[0:3, :])
    target = own[0:3, :] - center
    high_ref, low_ref = kept if kept else (None, None)
    sums = add_blocks(target, sources[0:3, :] - center, sources[3:6, :], block, high_ref, low_ref, True)
    field = field_from_sums(sums, target, own[3:6, :])
    moments[...] = suscept[...] * (applied[...] + field)


def second_kernel(block, own, sources, own_mom, source_mom, applied, suscept, *rest):
    kept, (moments, send) = rest[:-2], rest[-2:]
    center = center_of(own[0:3, :])
    target = own[0:3, :] - center
    high_ref, low_ref = kept if kept else (None, None)
    sums = add_blocks(
        target, sources[0:3, :] - center, source_mom[...], block, high_ref, low_ref, not kept
    )
    result = suscept[...] * (applied[...] + field_from_sums(sums, target, own_mom[...]))
    moments[...] = result
    groups = own.shape[1] // LANES
    for c in range(3):
        for g in range(groups):
            row = c * groups + g
            send[0, row : row + 1, :] = result[c : c + 1, g * LANES : (g + 1) * LANES]
    for e in range(1, send.shape[0]):
        send[e, :, :] = send[0, :, :]


def look_up(tables, index):
    lane = index & (LANES - 1)
    group = index >> (LANES.bit_length() - 1)
    found = None
    for g, table in enumerate(tables):
        here = jnp.take_along_axis(table, lane, axis=1, mode="promise_in_bounds")
        found = here if found is None else jnp.where(group == g, here, found)
    return found


def own_tables(ref, first, groups):
    return [
        jnp.broadcast_to(ref[0, first + g : first + g + 1, :], (SUBS, LANES)) for g in range(groups)
    ]


def their_tables(ref, rows, first, groups):
    return [ref[rows, first + g, :] for g in range(groups)]


def slot_index(sent, received, kind, rows, q, groups, slots):
    owner_row = 6 * groups + q
    partner_row = 6 * groups + slots + q
    ref = received if kind else sent
    owner = ref[rows, owner_row, :].astype(jnp.int32)
    partner = ref[rows, partner_row, :].astype(jnp.int32)
    return (partner, owner) if kind else (owner, partner)


def contact_blocks(columns, slots):
    return [
        (kind, slice(first, first + SUBS), q)
        for kind in range(2)
        for first in range(0, columns, SUBS)
        for q in range(slots)
    ]


def geometry_kernel(slots, sent, received, mom_sent, out):
    columns = sent.shape[0]
    groups = mom_sent.shape[1] // 3
    count_row = 6 * groups + 2 * slots
    for at, (kind, rows, q) in enumerate(contact_blocks(columns, slots)):
        mine, other = slot_index(sent, received, kind, rows, q, groups, slots)
        count = (received if kind else sent)[rows, count_row, :]
        slot = (lax.broadcasted_iota(jnp.int32, (SUBS, LANES), 1) + q * LANES).astype(F32)
        live = slot < count
        gap = []
        for c in range(6):
            gap.append(
                look_up(own_tables(sent, c * groups, groups), mine)
                - look_up(their_tables(received, rows, c * groups, groups), other)
            )
        radius_sq = gap[0] * gap[0] + gap[1] * gap[1] + gap[2] * gap[2] + 1.0
        inverse = lax.rsqrt(radius_sq)
        distance = radius_sq * inverse
        normal = [jnp.where(live, gap[c] * inverse, 0.0) for c in range(3)]
        speed = gap[3] * normal[0] + gap[4] * normal[1] + gap[5] * normal[2]
        for c in range(3):
            out[at, c] = normal[c]
            out[at, 4 + c] = look_up(own_tables(mom_sent, c * groups, groups), mine)
        out[at, 3] = -0.03 * (distance - 1.0) - 0.5 * speed


def force_kernel(slots, geometry, sent, received, mom_received, forces):
    columns = sent.shape[0]
    groups = mom_received.shape[1] // 3
    total = None
    for at, (kind, rows, q) in enumerate(contact_blocks(columns, slots)):
        mine, other = slot_index(sent, received, kind, rows, q, groups, slots)
        normal = [geometry[at, c] for c in range(3)]
        own = [geometry[at, 4 + c] for c in range(3)]
        their = [look_up(their_tables(mom_received, rows, c * groups, groups), other) for c in range(3)]
        along_own = own[0] * normal[0] + own[1] * normal[1] + own[2] * normal[2]
        along_their = their[0] * normal[0] + their[1] * normal[1] + their[2] * normal[2]
        product = own[0] * their[0] + own[1] * their[1] + own[2] * their[2]
        radial = 3.0 * (product - 5.0 * along_own * along_their) + geometry[at, 3]
        force = [
            3.0 * (along_own * their[c] + along_their * own[c]) + radial * normal[c] for c in range(3)
        ]
        group_of = mine >> (LANES.bit_length() - 1)
        lane_of = mine & (LANES - 1)
        for s in range(SUBS):
            place = group_of[s : s + 1, :] == lax.broadcasted_iota(jnp.int32, (groups, LANES), 0)
            rows_f32 = jnp.concatenate(
                [jnp.where(place, force[c][s : s + 1, :], 0.0) for c in range(3)], axis=0
            )
            values = jnp.concatenate(split3(rows_f32), axis=0)
            lane_hot = lane_of[s : s + 1, :] == lax.broadcasted_iota(jnp.int32, (LANES, LANES), 0)
            here = lax.dot_general(
                values,
                jnp.where(lane_hot, 1.0, 0.0).astype(BF16),
                (((1,), (1,)), ((), ())),
                preferred_element_type=F32,
            )
            total = here if total is None else total + here
    height = 3 * groups
    summed = total[0:height] + total[height : 2 * height] + total[2 * height : 3 * height]
    for c in range(3):
        for g in range(groups):
            row = c * groups + g
            forces[c : c + 1, g * LANES : (g + 1) * LANES] = summed[row : row + 1, :]


def call(kernel, name, outs, *args, scalars=(), limit=None):
    specs = [SMEM if at in scalars else VMEM for at in range(len(args))]
    many = isinstance(outs, tuple)
    return pl.pallas_call(
        kernel,
        out_shape=outs,
        in_specs=specs,
        out_specs=tuple(VMEM for _ in outs) if many else VMEM,
        compiler_params=pltpu.CompilerParams(vmem_limit_bytes=limit or 40 * 2**20),
        name=name,
    )(*args)


def shape(*dims, dtype=F32):
    return jax.ShapeDtypeStruct(dims, dtype)


def on_device(positions, velocity, applied, suscept, contact_owner, contact_partner, contact_count):
    count = positions.shape[1]
    columns, slot_len = contact_owner.shape[2:]
    groups, slots = count // LANES, slot_len // LANES
    suscept = suscept.reshape(1, count)
    send_rows = 6 * groups + 2 * slots + 1
    send_rows += -send_rows % SUBS
    sent, row_send = call(
        pack_kernel,
        "pack",
        (shape(columns, send_rows, LANES), shape(8, count)),
        positions,
        velocity,
        applied,
        suscept,
        contact_owner.reshape(columns, slot_len),
        contact_partner.reshape(columns, slot_len),
        contact_count.reshape(columns),
        scalars=(6,),
    )
    received = lax.all_to_all(sent, "col", split_axis=0, concat_axis=0, tiled=True)
    sources = lax.all_gather(row_send, "row", axis=1, tiled=True)
    length = sources.shape[1]
    block = math.gcd(length, 512)
    keep = 4 * length * count <= KEEP_BYTES
    kept_shape = (shape(length, count, dtype=BF16),) * 2 if keep else ()
    moments, *kept = call(
        functools.partial(first_kernel, block),
        "first_field",
        (shape(3, count),) + kept_shape,
        row_send,
        sources,
        applied,
        suscept,
    )
    for iteration in range(1, ITERS):
        source_mom = lax.all_gather(moments, "row", axis=1, tiled=True)
        moments, mom_sent = call(
            functools.partial(second_kernel, block),
            "next_field",
            (shape(3, count), shape(columns, 3 * groups, LANES)),
            row_send,
            sources,
            moments,
            source_mom,
            applied,
            suscept,
            *kept,
        )
    mom_received = lax.all_to_all(mom_sent, "col", split_axis=0, concat_axis=0, tiled=True)
    blocks = len(contact_blocks(columns, slots))
    geometry = call(
        functools.partial(geometry_kernel, slots),
        "contact_geometry",
        shape(blocks, 7, SUBS, LANES),
        sent,
        received,
        mom_sent,
    )
    forces = call(
        functools.partial(force_kernel, slots),
        "contact_force",
        shape(3, count),
        geometry,
        sent,
        received,
        mom_received,
    )
    return (moments, forces)


def solution(mesh):
    placed = (
        P(None, ("col", "row")),
        P(None, ("col", "row")),
        P(None, ("col", "row")),
        P(("col", "row")),
        P("col", "row", None, None),
        P("col", "row", None, None),
        P("col", "row", None),
    )
    return jax.shard_map(
        on_device,
        mesh=mesh,
        in_specs=placed,
        out_specs=(P(None, ("col", "row")), P(None, ("col", "row"))),
        check_vma=False,
    )
```

```python
import functools
import math

import jax
import jax.numpy as jnp
from jax import lax
from jax.experimental import pallas as pl
from jax.experimental.pallas import tpu as pltpu
from jax.sharding import PartitionSpec as P

ITERS = 2
LANES = 128
SUBS = 8
FEATURES = 16
PAIR_ROWS = 24
KEEP_BYTES = 20 * 2**20
BLOCK = 512
F32 = jnp.float32
BF16 = jnp.bfloat16
VMEM = pl.BlockSpec(memory_space=pltpu.VMEM)
HBM = pl.BlockSpec(memory_space=pltpu.HBM)


def split3(value):
    high = value.astype(BF16).astype(F32)
    rest = value - high
    middle = rest.astype(BF16).astype(F32)
    return high, middle, rest - middle


def norm_sq(pos):
    return pos[0] * pos[0] + pos[1] * pos[1] + pos[2] * pos[2]


def to_rows(vectors, held, out, first, columns):
    groups = held.shape[1]
    for f, vector in enumerate(vectors):
        held[f] = vector
    for g in range(groups):
        lanes = slice(columns + g * LANES, columns + (g + 1) * LANES)
        out[first : first + len(vectors), lanes] = held[0 : len(vectors), g, :].astype(BF16)


def moment_rows(pos, mom, held, out, columns):
    outer = [mom[a] * pos[b] for a in range(3) for b in range(3)]
    along = outer[0] + outer[4] + outer[8]
    square = norm_sq(pos)
    mixed = [3.0 * along * pos[a] - square * mom[a] for a in range(3)]
    pieces = [split3(v) for v in list(mom) + outer + mixed + [along]]
    for k in range(3):
        to_rows([p[k] for p in pieces], held, out, k * FEATURES, columns)


def target_rows(pos, held, out):
    high, middle, low = zip(*(split3(p) for p in pos))
    norms = split3(norm_sq(pos) + 1.0)
    ones = (jnp.ones_like(pos[0]),) * 3
    to_rows(high + high + middle + middle + high + low + norms + ones, held, out, 0, 0)


def source_rows(pos, held, out, columns):
    high, middle, low = zip(*(split3(p) for p in pos))
    norms = split3(norm_sq(pos))
    ones = (jnp.ones_like(pos[0]),) * 3
    doubled = tuple(-2.0 * p for p in high + middle + high + middle + low + high)
    to_rows(doubled + ones + norms, held, out, 3 * FEATURES, columns)


def field_from_sums(sums, held, pos, mom):
    groups = held.shape[1]
    for g in range(groups):
        lanes = slice(g * LANES, (g + 1) * LANES)
        held[0:FEATURES, g, :] = (
            sums[0:FEATURES, lanes]
            + sums[FEATURES : 2 * FEATURES, lanes]
            + sums[2 * FEATURES : 3 * FEATURES, lanes]
        )
    m = [held[a] for a in range(3)]
    outer = [[held[3 + 3 * a + b] for b in range(3)] for a in range(3)]
    trace = outer[0][0] + outer[1][1] + outer[2][2]
    scale_sq = norm_sq(pos) + 1.0
    along = m[0] * pos[0] + m[1] * pos[1] + m[2] * pos[2] - trace
    parts = []
    for a in range(3):
        by_column = outer[0][a] * pos[0] + outer[1][a] * pos[1] + outer[2][a] * pos[2]
        by_row = outer[a][0] * pos[0] + outer[a][1] * pos[1] + outer[a][2] * pos[2]
        parts.append(
            3.0 * (along * pos[a] - by_column)
            + 2.0 * by_row
            + held[12 + a]
            - scale_sq * m[a]
            + mom[a]
        )
    return parts


def pair_coefficient(radius_sq):
    inverse = lax.rsqrt(radius_sq)
    square = inverse * inverse
    fifth = square * square * inverse
    high = fifth.astype(BF16)
    return high, (fifth - high.astype(F32)).astype(BF16)


def vectors_of(ref, first, groups):
    return [ref[first + c * groups : first + (c + 1) * groups, :] for c in range(3)]


def about(pos, center):
    return [p - c for p, c in zip(pos, center)]


def field_kernel(has_mom, has_kept, has_before, is_last, columns, *refs):
    refs = list(refs)
    own, source = refs.pop(0), refs.pop(0)
    own_mom, source_mom = (refs.pop(0), refs.pop(0)) if has_mom else (None, None)
    kept = (refs.pop(0), refs.pop(0)) if has_kept else None
    before = refs.pop(0) if has_before else None
    outs, (held, target, feats, sums) = refs[:-4], refs[-4:]
    made = outs[1:] if len(outs) == 3 else None
    blocks = source.shape[0]
    groups = held.shape[1]
    count = groups * LANES
    own_pos = vectors_of(own, 0, groups)
    center = [jnp.sum(p, keepdims=True) * (1.0 / count) for p in own_pos]
    pos = about(own_pos, center)
    if not has_kept:
        target_rows(pos, held, target)
    sums[...] = before[...] if has_before else jnp.zeros_like(sums)
    for k in range(blocks):
        there = source.at[k]
        their_pos = about(vectors_of(there, 0, groups), center)
        if has_mom:
            their_mom = vectors_of(source_mom.at[k], 0, groups)
        else:
            chi = there[6 * groups : 7 * groups, :]
            their_mom = [chi * v for v in vectors_of(there, 3 * groups, groups)]
        moment_rows(their_pos, their_mom, held, feats, k * count)
        if not has_kept:
            source_rows(their_pos, held, feats, k * count)
    block = math.gcd(count, BLOCK)
    for start in range(0, blocks * count, block):
        part = slice(start, start + block)
        if has_kept:
            high, low = kept[0][part, :], kept[1][part, :]
        else:
            radius_sq = lax.dot_general(
                feats[3 * FEATURES :, part],
                target[...],
                (((0,), (0,)), ((), ())),
                preferred_element_type=F32,
            )
            high, low = pair_coefficient(radius_sq)
            if made:
                made[0][part, :] = high
                made[1][part, :] = low
        moments = feats[0 : 3 * FEATURES, part]
        sums[...] += jnp.dot(moments, high, preferred_element_type=F32) + jnp.dot(
            moments, low, preferred_element_type=F32
        )
    if not is_last:
        outs[0][...] = sums[...]
        return
    applied = vectors_of(own, 3 * groups, groups)
    chi = own[6 * groups : 7 * groups, :]
    own_now = vectors_of(own_mom, 0, groups) if has_mom else [chi * v for v in applied]
    field = field_from_sums(sums, held, pos, own_now)
    result = [chi * (applied[a] + field[a]) for a in range(3)]
    if not columns:
        for a in range(3):
            outs[0][a * groups : (a + 1) * groups, :] = result[a]
        return
    for a in range(3):
        for e in range(columns):
            outs[1][e, a * groups : (a + 1) * groups, :] = result[a]
        for g in range(groups):
            outs[0][a : a + 1, g * LANES : (g + 1) * LANES] = result[a][g : g + 1, :]


def pack_kernel(*refs):
    inputs, (send, payload), (pos, vel, field, chi, owner, partner, counts, done) = (
        refs[0:7],
        refs[7:9],
        refs[9:],
    )
    held = (pos, vel, field, chi, owner, partner, counts)
    copies = [
        pltpu.make_async_copy(src, dst, done.at[k]) for k, (src, dst) in enumerate(zip(inputs, held))
    ]
    for copy in copies:
        copy.start()
    for copy in copies:
        copy.wait()
    groups = pos.shape[1] // LANES
    slots = owner.shape[1] // LANES
    columns = owner.shape[0]
    for g in range(groups):
        lanes = slice(g * LANES, (g + 1) * LANES)
        for c in range(3):
            row = slice(c * groups + g, c * groups + g + 1)
            payload[row, :] = pos[c : c + 1, lanes]
            row = slice((3 + c) * groups + g, (3 + c) * groups + g + 1)
            payload[row, :] = field[c : c + 1, lanes]
            send[0, row, :] = vel[c : c + 1, lanes]
        payload[6 * groups + g : 6 * groups + g + 1, :] = chi[:, lanes]
    send[0, 0 : 3 * groups, :] = payload[0 : 3 * groups, :]
    for e in range(1, columns):
        send[e, 0 : 6 * groups, :] = send[0, 0 : 6 * groups, :]
    for q in range(slots):
        lanes = slice(q * LANES, (q + 1) * LANES)
        send[:, 6 * groups + q, :] = owner[:, lanes].astype(F32)
        send[:, 6 * groups + slots + q, :] = partner[:, lanes].astype(F32)
    tail = 6 * groups + 2 * slots
    for e in range(columns):
        send[e, tail:, :] = jnp.full((send.shape[1] - tail, LANES), counts[0, e].astype(F32))


def split_index(index):
    return index & (LANES - 1), index >> (LANES.bit_length() - 1)


def look_up(tables, lane, bits):
    found = [jnp.take_along_axis(t, lane, axis=1, mode="promise_in_bounds") for t in tables]
    for bit in bits:
        found = [
            jnp.where(bit, found[k + 1], found[k]) if k + 1 < len(found) else found[k]
            for k in range(0, len(found), 2)
        ]
    return found[0]


def bits_of(group, groups):
    return [(group >> k) & 1 == 1 for k in range((groups - 1).bit_length())]


def own_tables(ref, first, groups):
    return [
        jnp.broadcast_to(ref[first + g : first + g + 1, :], (SUBS, LANES)) for g in range(groups)
    ]


def their_tables(ref, rows, first, groups):
    return [ref[rows, first + g, :] for g in range(groups)]


def slot_index(sent, received, kind, rows, q, groups, slots):
    ref = received if kind else sent
    owner = ref[rows, 6 * groups + q, :].astype(jnp.int32)
    partner = ref[rows, 6 * groups + slots + q, :].astype(jnp.int32)
    return (partner, owner) if kind else (owner, partner)


def contact_blocks(columns, slots):
    return [
        (kind, slice(first, first + SUBS), q)
        for kind in range(2)
        for first in range(0, columns, SUBS)
        for q in range(slots)
    ]


def geometry_kernel(slots, groups, sent, received, out):
    columns = sent.shape[0]
    count_row = 6 * groups + 2 * slots
    for at, (kind, rows, q) in enumerate(contact_blocks(columns, slots)):
        mine, other = slot_index(sent, received, kind, rows, q, groups, slots)
        count = (received if kind else sent)[rows, count_row, :]
        slot = (lax.broadcasted_iota(jnp.int32, (SUBS, LANES), 1) + q * LANES).astype(F32)
        live = slot < count
        lane, group = split_index(mine)
        bits = bits_of(group, groups)
        their_lane, their_group = split_index(other)
        their_bits = bits_of(their_group, groups)
        gap = []
        for c in range(6):
            gap.append(
                look_up(own_tables(sent.at[0], c * groups, groups), lane, bits)
                - look_up(
                    their_tables(received, rows, c * groups, groups), their_lane, their_bits
                )
            )
        radius_sq = gap[0] * gap[0] + gap[1] * gap[1] + gap[2] * gap[2] + 1.0
        inverse = lax.rsqrt(radius_sq)
        normal = [jnp.where(live, gap[c] * inverse, 0.0) for c in range(3)]
        speed = gap[3] * normal[0] + gap[4] * normal[1] + gap[5] * normal[2]
        for c in range(3):
            out[at, c] = normal[c]
        out[at, 3] = -0.03 * (radius_sq * inverse - 1.0) - 0.5 * speed


def force_kernel(slots, geometry, sent, received, mom_sent, mom_received, forces, places, pieces):
    columns = sent.shape[0]
    groups = mom_received.shape[1] // 3
    for at, (kind, rows, q) in enumerate(contact_blocks(columns, slots)):
        mine, other = slot_index(sent, received, kind, rows, q, groups, slots)
        lane, group = split_index(mine)
        bits = bits_of(group, groups)
        their_lane, their_group = split_index(other)
        their_bits = bits_of(their_group, groups)
        normal = [geometry[at, c] for c in range(3)]
        own = [look_up(own_tables(mom_sent.at[0], c * groups, groups), lane, bits) for c in range(3)]
        their = [
            look_up(their_tables(mom_received, rows, c * groups, groups), their_lane, their_bits)
            for c in range(3)
        ]
        along_own = own[0] * normal[0] + own[1] * normal[1] + own[2] * normal[2]
        along_their = their[0] * normal[0] + their[1] * normal[1] + their[2] * normal[2]
        product = own[0] * their[0] + own[1] * their[1] + own[2] * their[2]
        radial = 3.0 * (product - 5.0 * along_own * along_their) + geometry[at, 3]
        lanes = slice(q * LANES, (q + 1) * LANES)
        places[kind, 0, rows, lanes] = group
        places[kind, 1, rows, lanes] = lane
        for c in range(3):
            force = 3.0 * (along_own * their[c] + along_their * own[c]) + radial * normal[c]
            for k, piece in enumerate(split3(force)):
                pieces[kind, k * 3 + c, rows, lanes] = piece
    width = slots * LANES
    row_of = lax.broadcasted_iota(jnp.int32, (groups, width), 0)
    lane_of = lax.broadcasted_iota(jnp.int32, (LANES, width), 0)
    total = None
    for kind in range(2):
        for e in range(columns):
            here = places[kind, 0, e : e + 1, :] == row_of
            values = jnp.concatenate(
                [jnp.where(here, pieces[kind, k, e : e + 1, :], 0.0) for k in range(9)], axis=0
            ).astype(BF16)
            hot = jnp.where(places[kind, 1, e : e + 1, :] == lane_of, 1.0, 0.0).astype(BF16)
            summed = lax.dot_general(
                values, hot, (((1,), (1,)), ((), ())), preferred_element_type=F32
            )
            total = summed if total is None else total + summed
    height = 3 * groups
    total = total[0:height] + total[height : 2 * height] + total[2 * height : 3 * height]
    for c in range(3):
        for g in range(groups):
            row = c * groups + g
            forces[c : c + 1, g * LANES : (g + 1) * LANES] = total[row : row + 1, :]


def call(kernel, name, outs, *args, specs=None, scratch=(), limit=24):
    many = isinstance(outs, tuple)
    return pl.pallas_call(
        kernel,
        out_shape=outs,
        in_specs=specs or [VMEM] * len(args),
        out_specs=tuple(VMEM for _ in outs) if many else VMEM,
        scratch_shapes=scratch,
        compiler_params=pltpu.CompilerParams(vmem_limit_bytes=limit * 2**20),
        name=name,
    )(*args)


def shape(*dims, dtype=F32):
    return jax.ShapeDtypeStruct(dims, dtype)


def exchange(block, axis, size):
    if size & (size - 1):
        every = lambda k: lax.ppermute(block, axis, [(i, (i + k) % size) for i in range(size)])
        return [every(k)[None] for k in range(1, size)]
    held, rounds = block[None], []
    for k in range(size.bit_length() - 1):
        arrived = lax.ppermute(held, axis, [(i, i ^ (1 << k)) for i in range(size)])
        rounds.append(arrived)
        if k + 2 < size.bit_length():
            held = jnp.concatenate([held, arrived], axis=0)
    return rounds


def add_fields(payload, payloads, mom, moms, kept, columns, keep):
    count = payload.shape[0] // SUBS * LANES
    groups = count // LANES
    sums, made = None, []
    for k, source in enumerate(payloads):
        is_last = k == len(payloads) - 1
        length = source.shape[0] * count
        args = [payload, source]
        if mom is not None:
            args += [mom, moms[k]]
        if kept:
            args += kept[k]
        if sums is not None:
            args.append(sums)
        if not is_last:
            outs = (shape(3 * FEATURES, count),)
        elif columns:
            outs = (shape(3, count), shape(columns, 3 * groups, LANES))
        else:
            outs = (shape(3 * groups, LANES),)
        if keep:
            outs += (shape(length, count, dtype=BF16),) * 2
        results = call(
            functools.partial(
                field_kernel, mom is not None, bool(kept), sums is not None, is_last, columns
            ),
            "field_sums",
            outs,
            *args,
            scratch=[
                pltpu.VMEM((PAIR_ROWS, groups, LANES), F32),
                pltpu.VMEM((PAIR_ROWS, count), BF16),
                pltpu.VMEM((3 * FEATURES + PAIR_ROWS, length), BF16),
                pltpu.VMEM((3 * FEATURES, count), F32),
            ],
        )
        sums = results[0]
        if keep:
            made.append(results[1:])
    return results, made


def on_device(row_size, positions, velocity, applied, suscept, owner, partner, contact_count):
    count = positions.shape[1]
    columns, slot_len = owner.shape[2:]
    groups, slots = count // LANES, slot_len // LANES
    send_rows = 6 * groups + 2 * slots + 1
    send_rows += -send_rows % SUBS
    inputs = (
        positions,
        velocity,
        applied,
        suscept.reshape(1, count),
        owner.reshape(columns, slot_len),
        partner.reshape(columns, slot_len),
        contact_count.reshape(1, columns),
    )
    sent, payload = call(
        pack_kernel,
        "pack",
        (shape(columns, send_rows, LANES), shape(8 * groups, LANES)),
        *(pltpu.with_memory_space_constraint(v, pltpu.HBM) for v in inputs),
        specs=[HBM] * 7,
        scratch=[pltpu.VMEM(v.shape, v.dtype) for v in inputs[:-1]]
        + [pltpu.SMEM((1, columns), jnp.int32), pltpu.SemaphoreType.DMA((7,))],
    )
    payloads = [payload[None]] + exchange(payload, "row", row_size)
    received = lax.all_to_all(sent, "col", split_axis=0, concat_axis=0, tiled=True)
    keep = 4 * row_size * count * count <= KEEP_BYTES
    (mom, *unused), kept = add_fields(payload, payloads, None, None, None, 0, keep)
    geometry = call(
        functools.partial(geometry_kernel, slots, groups),
        "contact_geometry",
        shape(len(contact_blocks(columns, slots)), 4, SUBS, LANES),
        sent,
        received,
    )
    for iteration in range(1, ITERS):
        is_last = iteration == ITERS - 1
        moms = [mom[None]] + exchange(mom, "row", row_size)
        results, unused = add_fields(
            payload, payloads, mom, moms, kept, columns if is_last else 0, False
        )
        mom = results[0]
    moments, mom_sent = results
    mom_received = lax.all_to_all(mom_sent, "col", split_axis=0, concat_axis=0, tiled=True)
    forces = call(
        functools.partial(force_kernel, slots),
        "contact_force",
        shape(3, count),
        geometry,
        sent,
        received,
        mom_sent,
        mom_received,
        scratch=[
            pltpu.VMEM((2, 2, columns, slot_len), jnp.int32),
            pltpu.VMEM((2, 9, columns, slot_len), F32),
        ],
    )
    return (moments, forces)


def solution(mesh):
    placed = (
        P(None, ("col", "row")),
        P(None, ("col", "row")),
        P(None, ("col", "row")),
        P(("col", "row")),
        P("col", "row", None, None),
        P("col", "row", None, None),
        P("col", "row", None),
    )
    return jax.shard_map(
        functools.partial(on_device, mesh.shape["row"]),
        mesh=mesh,
        in_specs=placed,
        out_specs=(P(None, ("col", "row")), P(None, ("col", "row"))),
        check_vma=False,
    )
```

```python
import functools
import math

import jax
import jax.numpy as jnp
from jax import lax
from jax.experimental import pallas as pl
from jax.experimental.pallas import tpu as pltpu
from jax.sharding import PartitionSpec as P

ITERS = 2
LANES = 128
SUBS = 8
FEATURES = 16
PAIR_ROWS = 24
KEEP_BYTES = 20 * 2**20
BLOCK = 512
WIDTH = 256
F32 = jnp.float32
BF16 = jnp.bfloat16
VMEM = pl.BlockSpec(memory_space=pltpu.VMEM)
HBM = pl.BlockSpec(memory_space=pltpu.HBM)


def split3(value):
    high = value.astype(BF16).astype(F32)
    rest = value - high
    middle = rest.astype(BF16).astype(F32)
    return high, middle, rest - middle


def norm_sq(pos):
    return pos[0] * pos[0] + pos[1] * pos[1] + pos[2] * pos[2]


def to_rows(vectors, held, out, first, columns):
    groups = held.shape[1]
    for f, vector in enumerate(vectors):
        held[f] = vector
    for g in range(groups):
        lanes = slice(columns + g * LANES, columns + (g + 1) * LANES)
        out[first : first + len(vectors), lanes] = held[0 : len(vectors), g, :].astype(BF16)


def moment_rows(pos, mom, held, out, columns):
    outer = [mom[a] * pos[b] for a in range(3) for b in range(3)]
    along = outer[0] + outer[4] + outer[8]
    square = norm_sq(pos)
    mixed = [3.0 * along * pos[a] - square * mom[a] for a in range(3)]
    pieces = [split3(v) for v in list(mom) + outer + mixed + [along]]
    for k in range(3):
        to_rows([p[k] for p in pieces], held, out, k * FEATURES, columns)


def target_rows(pos, held, out):
    high, middle, low = zip(*(split3(p) for p in pos))
    norms = split3(norm_sq(pos) + 1.0)
    ones = (jnp.ones_like(pos[0]),) * 3
    to_rows(high + high + middle + middle + high + low + norms + ones, held, out, 0, 0)


def source_rows(pos, held, out, columns):
    high, middle, low = zip(*(split3(p) for p in pos))
    norms = split3(norm_sq(pos))
    ones = (jnp.ones_like(pos[0]),) * 3
    doubled = tuple(-2.0 * p for p in high + middle + high + middle + low + high)
    to_rows(doubled + ones + norms, held, out, 3 * FEATURES, columns)


def field_from_sums(sums, held, pos, mom):
    groups = held.shape[1]
    for g in range(groups):
        lanes = slice(g * LANES, (g + 1) * LANES)
        held[0:FEATURES, g, :] = (
            sums[0:FEATURES, lanes]
            + sums[FEATURES : 2 * FEATURES, lanes]
            + sums[2 * FEATURES : 3 * FEATURES, lanes]
        )
    m = [held[a] for a in range(3)]
    outer = [[held[3 + 3 * a + b] for b in range(3)] for a in range(3)]
    trace = outer[0][0] + outer[1][1] + outer[2][2]
    scale_sq = norm_sq(pos) + 1.0
    along = m[0] * pos[0] + m[1] * pos[1] + m[2] * pos[2] - trace
    parts = []
    for a in range(3):
        by_column = outer[0][a] * pos[0] + outer[1][a] * pos[1] + outer[2][a] * pos[2]
        by_row = outer[a][0] * pos[0] + outer[a][1] * pos[1] + outer[a][2] * pos[2]
        parts.append(
            3.0 * (along * pos[a] - by_column)
            + 2.0 * by_row
            + held[12 + a]
            - scale_sq * m[a]
            + mom[a]
        )
    return parts


def pair_coefficient(radius_sq):
    inverse = lax.rsqrt(radius_sq)
    square = inverse * inverse
    fifth = square * square * inverse
    high = fifth.astype(BF16)
    return high, (fifth - high.astype(F32)).astype(BF16)


def vectors_of(ref, first, groups):
    return [ref[first + c * groups : first + (c + 1) * groups, :] for c in range(3)]


def about(pos, center):
    return [p - c for p, c in zip(pos, center)]


def field_kernel(sources, with_mom, kept_at, has_before, is_last, columns, *refs):
    refs = list(refs)
    own = refs.pop(0)
    blocks = [ref.at[k] for ref in refs[:sources] for k in range(ref.shape[0])]
    refs = refs[sources:]
    if with_mom:
        own_mom = refs.pop(0)
        mom_blocks = [ref.at[k] for ref in refs[:sources] for k in range(ref.shape[0])]
        refs = refs[sources:]
    has_kept = kept_at is not None
    kept = (refs.pop(0), refs.pop(0)) if has_kept else None
    before = refs.pop(0) if has_before else None
    outs, (held, target, feats, sums) = refs[:-4], refs[-4:]
    made = outs[1:] if len(outs) == 3 else None
    groups = held.shape[1]
    count = groups * LANES
    own_pos = vectors_of(own, 0, groups)
    center = [jnp.sum(p, keepdims=True) * (1.0 / count) for p in own_pos]
    pos = about(own_pos, center)
    if not has_kept:
        target_rows(pos, held, target)
    sums[...] = before[...] if has_before else jnp.zeros_like(sums)
    for k, there in enumerate(blocks):
        their_pos = about(vectors_of(there, 0, groups), center)
        if with_mom:
            their_mom = vectors_of(mom_blocks[k], 0, groups)
        else:
            chi = there[6 * groups : 7 * groups, :]
            their_mom = [chi * v for v in vectors_of(there, 3 * groups, groups)]
        moment_rows(their_pos, their_mom, held, feats, k * count)
        if not has_kept:
            source_rows(their_pos, held, feats, k * count)
    height, width = math.gcd(count, BLOCK), math.gcd(count, WIDTH)
    tiles = [
        (slice(a, a + height), slice(b, b + width))
        for a in range(0, len(blocks) * count, height)
        for b in range(0, count, width)
    ]

    def radius_of(tile):
        return lax.dot_general(
            feats[3 * FEATURES :, tile[0]],
            target[:, tile[1]],
            (((0,), (0,)), ((), ())),
            preferred_element_type=F32,
        )

    def add(tile, high, low):
        moments = feats[0 : 3 * FEATURES, tile[0]]
        sums[:, tile[1]] += jnp.dot(moments, high, preferred_element_type=F32) + jnp.dot(
            moments, low, preferred_element_type=F32
        )

    if has_kept:
        for a, b in tiles:
            rows = slice(kept_at + a.start, kept_at + a.stop)
            add((a, b), kept[0][rows, b], kept[1][rows, b])
    else:
        radius_sq, ready = radius_of(tiles[0]), None
        for at, tile in enumerate(tiles):
            following = radius_of(tiles[at + 1]) if at + 1 < len(tiles) else None
            high, low = pair_coefficient(radius_sq)
            if made:
                made[0][tile] = high
                made[1][tile] = low
            if ready is not None:
                add(*ready)
            ready, radius_sq = (tile, high, low), following
        add(*ready)
    if not is_last:
        outs[0][...] = sums[...]
        return
    applied = vectors_of(own, 3 * groups, groups)
    chi = own[6 * groups : 7 * groups, :]
    own_now = vectors_of(own_mom, 0, groups) if with_mom else [chi * v for v in applied]
    field = field_from_sums(sums, held, pos, own_now)
    for a in range(3):
        result = chi * (applied[a] + field[a])
        rows = slice(a * groups, (a + 1) * groups)
        if columns:
            for e in range(columns):
                outs[0][e, rows, :] = result
        else:
            outs[0][rows, :] = result


def copy_in(inputs, held, done):
    copies = [
        pltpu.make_async_copy(src, dst, done.at[k]) for k, (src, dst) in enumerate(zip(inputs, held))
    ]
    for copy in copies:
        copy.start()
    for copy in copies:
        copy.wait()


def row_pack_kernel(*refs):
    inputs, payload, (pos, field, chi, done) = refs[0:3], refs[3], refs[4:]
    copy_in(inputs, (pos, field, chi), done)
    groups = pos.shape[1] // LANES
    for g in range(groups):
        lanes = slice(g * LANES, (g + 1) * LANES)
        for c in range(3):
            payload[c * groups + g : c * groups + g + 1, :] = pos[c : c + 1, lanes]
            row = (3 + c) * groups + g
            payload[row : row + 1, :] = field[c : c + 1, lanes]
        payload[6 * groups + g : 6 * groups + g + 1, :] = chi[:, lanes]
    payload[7 * groups :, :] = jnp.zeros_like(payload[7 * groups :, :])


def column_pack_kernel(*refs):
    inputs, payload, send, (vel, owner, partner, counts, done) = refs[0:4], refs[4], refs[5], refs[6:]
    copy_in(inputs, (vel, owner, partner, counts), done)
    groups = vel.shape[1] // LANES
    slots = owner.shape[1] // LANES
    columns = owner.shape[0]
    send[0, 0 : 3 * groups, :] = payload[0 : 3 * groups, :]
    for g in range(groups):
        for c in range(3):
            row = (3 + c) * groups + g
            send[0, row : row + 1, :] = vel[c : c + 1, g * LANES : (g + 1) * LANES]
    for e in range(1, columns):
        send[e, 0 : 6 * groups, :] = send[0, 0 : 6 * groups, :]
    for q in range(slots):
        lanes = slice(q * LANES, (q + 1) * LANES)
        send[:, 6 * groups + q, :] = owner[:, lanes].astype(F32)
        send[:, 6 * groups + slots + q, :] = partner[:, lanes].astype(F32)
    tail = 6 * groups + 2 * slots
    for e in range(columns):
        send[e, tail:, :] = jnp.full((send.shape[1] - tail, LANES), counts[0, e].astype(F32))


def split_index(index):
    return index & (LANES - 1), index >> (LANES.bit_length() - 1)


def look_up(tables, lane, bits):
    found = [jnp.take_along_axis(t, lane, axis=1, mode="promise_in_bounds") for t in tables]
    for bit in bits:
        found = [
            jnp.where(bit, found[k + 1], found[k]) if k + 1 < len(found) else found[k]
            for k in range(0, len(found), 2)
        ]
    return found[0]


def bits_of(group, groups):
    return [(group >> k) & 1 == 1 for k in range((groups - 1).bit_length())]


def own_tables(ref, first, groups):
    return [
        jnp.broadcast_to(ref[first + g : first + g + 1, :], (SUBS, LANES)) for g in range(groups)
    ]


def their_tables(ref, rows, first, groups):
    return [ref[rows, first + g, :] for g in range(groups)]


def slot_index(sent, received, kind, rows, q, groups, slots):
    ref = received if kind else sent
    owner = ref[rows, 6 * groups + q, :].astype(jnp.int32)
    partner = ref[rows, 6 * groups + slots + q, :].astype(jnp.int32)
    return (partner, owner) if kind else (owner, partner)


def contact_blocks(columns, slots):
    return [
        (kind, slice(first, first + SUBS), q)
        for kind in range(2)
        for first in range(0, columns, SUBS)
        for q in range(slots)
    ]


def geometry_kernel(slots, sent, received, mom_sent, moments, out, places, hot):
    columns = sent.shape[0]
    groups = mom_sent.shape[1] // 3
    count_row = 6 * groups + 2 * slots
    for c in range(3):
        for g in range(groups):
            lanes = slice(g * LANES, (g + 1) * LANES)
            moments[c : c + 1, lanes] = mom_sent[0, c * groups + g : c * groups + g + 1, :]
    for at, (kind, rows, q) in enumerate(contact_blocks(columns, slots)):
        mine, other = slot_index(sent, received, kind, rows, q, groups, slots)
        count = (received if kind else sent)[rows, count_row, :]
        slot = (lax.broadcasted_iota(jnp.int32, (SUBS, LANES), 1) + q * LANES).astype(F32)
        live = slot < count
        lane, group = split_index(mine)
        bits = bits_of(group, groups)
        their_lane, their_group = split_index(other)
        their_bits = bits_of(their_group, groups)
        gap = []
        for c in range(6):
            gap.append(
                look_up(own_tables(sent.at[0], c * groups, groups), lane, bits)
                - look_up(
                    their_tables(received, rows, c * groups, groups), their_lane, their_bits
                )
            )
        radius_sq = gap[0] * gap[0] + gap[1] * gap[1] + gap[2] * gap[2] + 1.0
        inverse = lax.rsqrt(radius_sq)
        normal = [jnp.where(live, gap[c] * inverse, 0.0) for c in range(3)]
        speed = gap[3] * normal[0] + gap[4] * normal[1] + gap[5] * normal[2]
        own = [look_up(own_tables(mom_sent.at[0], c * groups, groups), lane, bits) for c in range(3)]
        for c in range(3):
            out[at, c] = normal[c]
            out[at, 3 + c] = own[c]
        out[at, 6] = -0.03 * (radius_sq * inverse - 1.0) - 0.5 * speed
        out[at, 7] = own[0] * normal[0] + own[1] * normal[1] + own[2] * normal[2]
        lanes = slice(q * LANES, (q + 1) * LANES)
        places[kind, 0, rows, lanes] = group
        places[kind, 1, rows, lanes] = lane
    lane_of = lax.broadcasted_iota(jnp.int32, (LANES, slots * LANES), 0)
    for kind in range(2):
        for e in range(columns):
            here = places[kind, 1, e : e + 1, :] == lane_of
            hot[kind * columns + e] = jnp.where(here, 1.0, 0.0).astype(BF16)


def force_kernel(slots, geometry, places, hot, sent, received, mom_received, forces, pieces):
    columns = sent.shape[0]
    groups = mom_received.shape[1] // 3
    for at, (kind, rows, q) in enumerate(contact_blocks(columns, slots)):
        unused, other = slot_index(sent, received, kind, rows, q, groups, slots)
        their_lane, their_group = split_index(other)
        their_bits = bits_of(their_group, groups)
        normal = [geometry[at, c] for c in range(3)]
        own = [geometry[at, 3 + c] for c in range(3)]
        along_own = geometry[at, 7]
        their = [
            look_up(their_tables(mom_received, rows, c * groups, groups), their_lane, their_bits)
            for c in range(3)
        ]
        along_their = their[0] * normal[0] + their[1] * normal[1] + their[2] * normal[2]
        product = own[0] * their[0] + own[1] * their[1] + own[2] * their[2]
        radial = 3.0 * (product - 5.0 * along_own * along_their) + geometry[at, 6]
        lanes = slice(q * LANES, (q + 1) * LANES)
        for c in range(3):
            force = 3.0 * (along_own * their[c] + along_their * own[c]) + radial * normal[c]
            for k, piece in enumerate(split3(force)):
                pieces[kind, k * 3 + c, rows, lanes] = piece
    row_of = lax.broadcasted_iota(jnp.int32, (groups, slots * LANES), 0)
    total = None
    for kind in range(2):
        for e in range(columns):
            here = places[kind, 0, e : e + 1, :] == row_of
            values = jnp.concatenate(
                [jnp.where(here, pieces[kind, k, e : e + 1, :], 0.0) for k in range(9)], axis=0
            ).astype(BF16)
            summed = lax.dot_general(
                values,
                hot[kind * columns + e],
                (((1,), (1,)), ((), ())),
                preferred_element_type=F32,
            )
            total = summed if total is None else total + summed
    height = 3 * groups
    total = total[0:height] + total[height : 2 * height] + total[2 * height : 3 * height]
    for c in range(3):
        for g in range(groups):
            row = c * groups + g
            forces[c : c + 1, g * LANES : (g + 1) * LANES] = total[row : row + 1, :]


def call(kernel, name, outs, *args, specs=None, scratch=(), limit=24):
    many = isinstance(outs, tuple)
    return pl.pallas_call(
        kernel,
        out_shape=outs,
        in_specs=specs or [VMEM] * len(args),
        out_specs=tuple(VMEM for _ in outs) if many else VMEM,
        scratch_shapes=scratch,
        compiler_params=pltpu.CompilerParams(vmem_limit_bytes=limit * 2**20),
        name=name,
    )(*args)


def shape(*dims, dtype=F32):
    return jax.ShapeDtypeStruct(dims, dtype)


def exchange(block, axis, size):
    if size & (size - 1):
        every = lambda k: lax.ppermute(block, axis, [(i, (i + k) % size) for i in range(size)])
        return [every(k)[None] for k in range(1, size)]
    held, rounds = block[None], []
    for k in range(size.bit_length() - 1):
        arrived = lax.ppermute(held, axis, [(i, i ^ (1 << k)) for i in range(size)])
        rounds.append(arrived)
        if k + 2 < size.bit_length():
            held = jnp.concatenate([held, arrived], axis=0)
    return rounds


def add_fields(payload, payloads, mom, moms, kept, columns, keep):
    count = payload.shape[0] // SUBS * LANES
    groups = count // LANES
    sums, made = None, []
    for k, sources in enumerate(payloads):
        is_last = k == len(payloads) - 1
        length = sum(a.shape[0] for a in sources) * count
        args = [payload, *sources]
        if mom is not None:
            args += [mom, *moms[k]]
        if kept:
            args += kept[k][1]
        if sums is not None:
            args.append(sums)
        if not is_last:
            outs = (shape(3 * FEATURES, count),)
        elif columns:
            outs = (shape(columns, 3 * groups, LANES),)
        else:
            outs = (shape(3 * groups, LANES),)
        if keep:
            outs += (shape(length, count, dtype=BF16),) * 2
        sums, *now = call(
            functools.partial(
                field_kernel,
                len(sources),
                mom is not None,
                kept[k][0] if kept else None,
                sums is not None,
                is_last,
                columns,
            ),
            "field_sums",
            outs,
            *args,
            scratch=[
                pltpu.VMEM((PAIR_ROWS, groups, LANES), F32),
                pltpu.VMEM((PAIR_ROWS, count), BF16),
                pltpu.VMEM((3 * FEATURES + PAIR_ROWS, length), BF16),
                pltpu.VMEM((3 * FEATURES, count), F32),
            ],
        )
        made.append(now)
    return sums, made


def on_device(row_size, positions, velocity, applied, suscept, owner, partner, contact_count):
    count = positions.shape[1]
    columns, slot_len = owner.shape[2:]
    groups, slots = count // LANES, slot_len // LANES
    send_rows = 6 * groups + 2 * slots + 1
    send_rows += -send_rows % SUBS
    def in_hbm(*arrays):
        return [pltpu.with_memory_space_constraint(v, pltpu.HBM) for v in arrays]

    inputs = in_hbm(positions, applied, suscept.reshape(1, count))
    payload = call(
        row_pack_kernel,
        "row_pack",
        shape(8 * groups, LANES),
        *inputs,
        specs=[HBM] * 3,
        scratch=[pltpu.VMEM(v.shape, v.dtype) for v in inputs] + [pltpu.SemaphoreType.DMA((3,))],
    )
    inputs = in_hbm(
        velocity,
        owner.reshape(columns, slot_len),
        partner.reshape(columns, slot_len),
        contact_count.reshape(1, columns),
    )
    sent = call(
        column_pack_kernel,
        "column_pack",
        shape(columns, send_rows, LANES),
        *inputs,
        payload,
        specs=[HBM] * 4 + [VMEM],
        scratch=[pltpu.VMEM(v.shape, v.dtype) for v in inputs[:-1]]
        + [pltpu.SMEM((1, columns), jnp.int32), pltpu.SemaphoreType.DMA((4,))],
    )
    rounds = exchange(payload, "row", row_size)
    first, sent = lax.optimization_barrier((rounds[0], sent))
    payloads = [[payload[None], first]] + [[r] for r in rounds[1:]]
    received = lax.all_to_all(sent, "col", split_axis=0, concat_axis=0, tiled=True)
    keep = 4 * row_size * count * count <= KEEP_BYTES
    mom, made = add_fields(payload, payloads, None, None, None, 0, keep)
    payloads = [[payload[None]], [first]] + payloads[1:]
    kept = [(0, made[0]), (count, made[0])] + [(0, m) for m in made[1:]] if keep else None
    for iteration in range(1, ITERS):
        is_last = iteration == ITERS - 1
        moms = [[mom[None]]] + [[r] for r in exchange(mom, "row", row_size)]
        mom, unused = add_fields(
            payload, payloads, mom, moms, kept, columns if is_last else 0, False
        )
    mom_received = lax.all_to_all(mom, "col", split_axis=0, concat_axis=0, tiled=True)
    moments, geometry, places, hot = call(
        functools.partial(geometry_kernel, slots),
        "contact_geometry",
        (
            shape(3, count),
            shape(len(contact_blocks(columns, slots)), 8, SUBS, LANES),
            shape(2, 2, columns, slot_len, dtype=jnp.int32),
            shape(2 * columns, LANES, slot_len, dtype=BF16),
        ),
        sent,
        received,
        mom,
    )
    forces = call(
        functools.partial(force_kernel, slots),
        "contact_force",
        shape(3, count),
        geometry,
        places,
        hot,
        sent,
        received,
        mom_received,
        scratch=[pltpu.VMEM((2, 9, columns, slot_len), F32)],
    )
    return (moments, forces)


def solution(mesh):
    placed = (
        P(None, ("col", "row")),
        P(None, ("col", "row")),
        P(None, ("col", "row")),
        P(("col", "row")),
        P("col", "row", None, None),
        P("col", "row", None, None),
        P("col", "row", None),
    )
    return jax.shard_map(
        functools.partial(on_device, mesh.shape["row"]),
        mesh=mesh,
        in_specs=placed,
        out_specs=(P(None, ("col", "row")), P(None, ("col", "row"))),
        check_vma=False,
    )
```

```python
import functools
import math

import jax
import jax.numpy as jnp
from jax import lax
from jax.experimental import pallas as pl
from jax.experimental.pallas import tpu as pltpu
from jax.sharding import PartitionSpec as P

ITERS = 2
LANES = 128
SUBS = 8
FEATURES = 16
PAIR_ROWS = 48
KEEP_BYTES = 20 * 2**20
BLOCK = 512
WIDTH = 256
F32 = jnp.float32
BF16 = jnp.bfloat16
VMEM = pl.BlockSpec(memory_space=pltpu.VMEM)
HBM = pl.BlockSpec(memory_space=pltpu.HBM)


def split3(value):
    high = value.astype(BF16).astype(F32)
    rest = value - high
    middle = rest.astype(BF16).astype(F32)
    return high, middle, rest - middle


def norm_sq(pos):
    return pos[0] * pos[0] + pos[1] * pos[1] + pos[2] * pos[2]


def to_rows(vectors, held):
    for f, vector in enumerate(vectors):
        held[f] = vector
    return [held[0 : len(vectors), g, :] for g in range(held.shape[1])]


def put_pieces(rows, out, first, columns, order):
    for g, row in enumerate(rows):
        pieces = split3(row)
        lanes = slice(columns + g * LANES, columns + (g + 1) * LANES)
        out[first : first + len(order) * row.shape[0], lanes] = jnp.concatenate(
            [pieces[k] for k in order], axis=0
        ).astype(BF16)


def moment_rows(pos, mom, held, out, columns):
    outer = [mom[a] * pos[b] for a in range(3) for b in range(3)]
    along = outer[0] + outer[4] + outer[8]
    square = norm_sq(pos)
    mixed = [3.0 * along * pos[a] - square * mom[a] for a in range(3)]
    put_pieces(to_rows(list(mom) + outer + mixed + [along], held), out, 0, columns, (0, 1, 2))


TARGET_ORDER = (0, 1, 0, 1, 2, 0)
SOURCE_ORDER = (0, 0, 1, 1, 0, 2)


def target_rows(pos, held, out):
    one, zero = jnp.ones_like(pos[0]), jnp.zeros_like(pos[0])
    rows = list(pos) + [one, norm_sq(pos) + 1.0, zero, zero, zero]
    put_pieces(to_rows(rows, held), out, 0, 0, TARGET_ORDER)


def source_rows(pos, held, out, columns):
    one, zero = jnp.ones_like(pos[0]), jnp.zeros_like(pos[0])
    rows = [-2.0 * p for p in pos] + [norm_sq(pos), one, zero, zero, zero]
    put_pieces(to_rows(rows, held), out, 3 * FEATURES, columns, SOURCE_ORDER)


def field_from_sums(sums, held, pos, mom):
    groups = held.shape[1]
    for g in range(groups):
        lanes = slice(g * LANES, (g + 1) * LANES)
        held[0:FEATURES, g, :] = (
            sums[0:FEATURES, lanes]
            + sums[FEATURES : 2 * FEATURES, lanes]
            + sums[2 * FEATURES : 3 * FEATURES, lanes]
        )
    m = [held[a] for a in range(3)]
    outer = [[held[3 + 3 * a + b] for b in range(3)] for a in range(3)]
    trace = outer[0][0] + outer[1][1] + outer[2][2]
    scale_sq = norm_sq(pos) + 1.0
    along = m[0] * pos[0] + m[1] * pos[1] + m[2] * pos[2] - trace
    parts = []
    for a in range(3):
        by_column = outer[0][a] * pos[0] + outer[1][a] * pos[1] + outer[2][a] * pos[2]
        by_row = outer[a][0] * pos[0] + outer[a][1] * pos[1] + outer[a][2] * pos[2]
        parts.append(
            3.0 * (along * pos[a] - by_column)
            + 2.0 * by_row
            + held[12 + a]
            - scale_sq * m[a]
            + mom[a]
        )
    return parts


def pair_coefficient(radius_sq):
    inverse = lax.rsqrt(radius_sq)
    square = inverse * inverse
    fifth = square * square * inverse
    high = fifth.astype(BF16)
    return high, (fifth - high.astype(F32)).astype(BF16)


def vectors_of(ref, first, groups):
    return [ref[first + c * groups : first + (c + 1) * groups, :] for c in range(3)]


def about(pos, center):
    return [p - c for p, c in zip(pos, center)]


def field_kernel(sources, with_mom, kept_at, has_before, is_last, columns, *refs):
    refs = list(refs)
    own = refs.pop(0)
    blocks = [ref.at[k] for ref in refs[:sources] for k in range(ref.shape[0])]
    refs = refs[sources:]
    if with_mom:
        own_mom = refs.pop(0)
        mom_blocks = [ref.at[k] for ref in refs[:sources] for k in range(ref.shape[0])]
        refs = refs[sources:]
    has_kept = kept_at is not None
    kept = (refs.pop(0), refs.pop(0)) if has_kept else None
    before = refs.pop(0) if has_before else None
    outs, (held, target, feats, sums) = refs[:-4], refs[-4:]
    made = outs[1:3] if len(outs) == 3 else None
    groups = held.shape[1]
    count = groups * LANES
    own_pos = vectors_of(own, 0, groups)
    center = [jnp.sum(p, keepdims=True) * (1.0 / count) for p in own_pos]
    pos = about(own_pos, center)
    if not has_kept:
        target_rows(pos, held, target)
    sums[...] = before[...] if has_before else jnp.zeros_like(sums)
    for k, there in enumerate(blocks):
        their_pos = about(vectors_of(there, 0, groups), center)
        if with_mom:
            their_mom = vectors_of(mom_blocks[k], 0, groups)
        else:
            chi = there[6 * groups : 7 * groups, :]
            their_mom = [chi * v for v in vectors_of(there, 3 * groups, groups)]
        moment_rows(their_pos, their_mom, held, feats, k * count)
        if not has_kept:
            source_rows(their_pos, held, feats, k * count)
    height, width = math.gcd(count, BLOCK), math.gcd(count, WIDTH)
    tiles = [
        (slice(a, a + height), slice(b, b + width))
        for a in range(0, len(blocks) * count, height)
        for b in range(0, count, width)
    ]

    def radius_of(tile):
        return lax.dot_general(
            feats[3 * FEATURES :, tile[0]],
            target[:, tile[1]],
            (((0,), (0,)), ((), ())),
            preferred_element_type=F32,
        )

    def add(tile, high, low):
        moments = feats[0 : 3 * FEATURES, tile[0]]
        sums[:, tile[1]] += jnp.dot(moments, high, preferred_element_type=F32) + jnp.dot(
            moments, low, preferred_element_type=F32
        )

    if has_kept:
        for a, b in tiles:
            rows = slice(kept_at + a.start, kept_at + a.stop)
            add((a, b), kept[0][rows, b], kept[1][rows, b])
    else:
        radius_sq, ready = radius_of(tiles[0]), None
        for at, tile in enumerate(tiles):
            following = radius_of(tiles[at + 1]) if at + 1 < len(tiles) else None
            high, low = pair_coefficient(radius_sq)
            if made:
                made[0][tile] = high
                made[1][tile] = low
            if ready is not None:
                add(*ready)
            ready, radius_sq = (tile, high, low), following
        add(*ready)
    if not is_last:
        outs[0][...] = sums[...]
        return
    applied = vectors_of(own, 3 * groups, groups)
    chi = own[6 * groups : 7 * groups, :]
    own_now = vectors_of(own_mom, 0, groups) if with_mom else [chi * v for v in applied]
    field = field_from_sums(sums, held, pos, own_now)
    for a in range(3):
        result = chi * (applied[a] + field[a])
        rows = slice(a * groups, (a + 1) * groups)
        outs[0][rows, :] = result
        for e in range(columns):
            outs[1][e, rows, :] = result


def copy_in(inputs, held, done):
    copies = [
        pltpu.make_async_copy(src, dst, done.at[k]) for k, (src, dst) in enumerate(zip(inputs, held))
    ]
    for copy in copies:
        copy.start()
    for copy in copies:
        copy.wait()


def row_pack_kernel(*refs):
    inputs, payload, (pos, field, chi, done) = refs[0:3], refs[3], refs[4:]
    copy_in(inputs, (pos, field, chi), done)
    groups = pos.shape[1] // LANES
    for g in range(groups):
        lanes = slice(g * LANES, (g + 1) * LANES)
        for c in range(3):
            payload[c * groups + g : c * groups + g + 1, :] = pos[c : c + 1, lanes]
            row = (3 + c) * groups + g
            payload[row : row + 1, :] = field[c : c + 1, lanes]
        payload[6 * groups + g : 6 * groups + g + 1, :] = chi[:, lanes]
    payload[7 * groups :, :] = jnp.zeros_like(payload[7 * groups :, :])


def column_pack_kernel(*refs):
    inputs, payload, (send, table, listed), (vel, owner, partner, counts, done) = (
        refs[0:4],
        refs[4],
        refs[5:8],
        refs[8:],
    )
    copy_in(inputs, (vel, owner, partner, counts), done)
    groups = vel.shape[1] // LANES
    slots = owner.shape[1] // LANES
    columns = owner.shape[0]
    table[0 : 3 * groups, :] = payload[0 : 3 * groups, :]
    for g in range(groups):
        for c in range(3):
            row = (3 + c) * groups + g
            table[row : row + 1, :] = vel[c : c + 1, g * LANES : (g + 1) * LANES]
    for e in range(columns):
        send[e, 0 : 6 * groups, :] = table[...]
        live = jnp.full((send.shape[1] - 6 * groups - 2 * slots, LANES), counts[0, e])
        send[e, 6 * groups + 2 * slots :, :] = live.astype(F32)
        listed[2 * slots, e : e + 1, :] = live[0:1]
    for q in range(slots):
        lanes = slice(q * LANES, (q + 1) * LANES)
        for k, index in enumerate((owner[:, lanes], partner[:, lanes])):
            send[:, 6 * groups + k * slots + q, :] = index.astype(F32)
            listed[k * slots + q] = index


def split_index(index):
    return index & (LANES - 1), index >> (LANES.bit_length() - 1)


def look_up(tables, lane, bits):
    found = [jnp.take_along_axis(t, lane, axis=1, mode="promise_in_bounds") for t in tables]
    for bit in bits:
        found = [
            jnp.where(bit, found[k + 1], found[k]) if k + 1 < len(found) else found[k]
            for k in range(0, len(found), 2)
        ]
    return found[0]


def bits_of(group, groups):
    return [(group >> k) & 1 == 1 for k in range((groups - 1).bit_length())]


def own_tables(ref, first, groups):
    return [
        jnp.broadcast_to(ref[first + g : first + g + 1, :], (SUBS, LANES)) for g in range(groups)
    ]


def their_tables(ref, rows, first, groups):
    return [ref[rows, first + g, :] for g in range(groups)]


def slot_index(listed, received, kind, rows, q, groups, slots):
    if kind:
        first = 6 * groups + q
        owner, partner, count = (
            received[rows, row, :].astype(jnp.int32)
            for row in (first, first + slots, 6 * groups + 2 * slots)
        )
    else:
        owner, partner, count = (listed[row, rows, :] for row in (q, slots + q, 2 * slots))
    live = lax.broadcasted_iota(jnp.int32, (SUBS, LANES), 1) + q * LANES < count
    return (partner, owner, live) if kind else (owner, partner, live)


def contact_blocks(columns, slots):
    return [
        (kind, slice(first, first + SUBS), q)
        for kind in range(2)
        for first in range(0, columns, SUBS)
        for q in range(slots)
    ]


def geometry_kernel(slots, table, listed, received, mom, moments, out, places, hot):
    columns = received.shape[0]
    groups = mom.shape[0] // 3
    for c in range(3):
        for g in range(groups):
            lanes = slice(g * LANES, (g + 1) * LANES)
            moments[c : c + 1, lanes] = mom[c * groups + g : c * groups + g + 1, :]
    for at, (kind, rows, q) in enumerate(contact_blocks(columns, slots)):
        mine, other, live = slot_index(listed, received, kind, rows, q, groups, slots)
        lane, group = split_index(mine)
        bits = bits_of(group, groups)
        their_lane, their_group = split_index(other)
        their_bits = bits_of(their_group, groups)
        gap = []
        for c in range(6):
            gap.append(
                look_up(own_tables(table, c * groups, groups), lane, bits)
                - look_up(
                    their_tables(received, rows, c * groups, groups), their_lane, their_bits
                )
            )
        radius_sq = gap[0] * gap[0] + gap[1] * gap[1] + gap[2] * gap[2] + 1.0
        inverse = lax.rsqrt(radius_sq)
        normal = [jnp.where(live, gap[c] * inverse, 0.0) for c in range(3)]
        speed = gap[3] * normal[0] + gap[4] * normal[1] + gap[5] * normal[2]
        own = [look_up(own_tables(mom, c * groups, groups), lane, bits) for c in range(3)]
        for c in range(3):
            out[at, c] = normal[c]
            out[at, 3 + c] = own[c]
        out[at, 6] = -0.03 * (radius_sq * inverse - 1.0) - 0.5 * speed
        out[at, 7] = own[0] * normal[0] + own[1] * normal[1] + own[2] * normal[2]
        lanes = slice(q * LANES, (q + 1) * LANES)
        places[kind, 0, rows, lanes] = group
        places[kind, 1, rows, lanes] = lane
        places[kind, 2, rows, lanes] = other
    lane_of = lax.broadcasted_iota(jnp.int32, (LANES, slots * LANES), 0)
    for kind in range(2):
        for e in range(columns):
            here = places[kind, 1, e : e + 1, :] == lane_of
            hot[kind * columns + e] = jnp.where(here, 1.0, 0.0).astype(BF16)


def force_kernel(slots, geometry, places, hot, mom_received, forces, pieces):
    columns = mom_received.shape[0]
    groups = mom_received.shape[1] // 3
    for at, (kind, rows, q) in enumerate(contact_blocks(columns, slots)):
        lanes = slice(q * LANES, (q + 1) * LANES)
        their_lane, their_group = split_index(places[kind, 2, rows, lanes])
        their_bits = bits_of(their_group, groups)
        normal = [geometry[at, c] for c in range(3)]
        own = [geometry[at, 3 + c] for c in range(3)]
        along_own = geometry[at, 7]
        their = [
            look_up(their_tables(mom_received, rows, c * groups, groups), their_lane, their_bits)
            for c in range(3)
        ]
        along_their = their[0] * normal[0] + their[1] * normal[1] + their[2] * normal[2]
        product = own[0] * their[0] + own[1] * their[1] + own[2] * their[2]
        radial = 3.0 * (product - 5.0 * along_own * along_their) + geometry[at, 6]
        for c in range(3):
            force = 3.0 * (along_own * their[c] + along_their * own[c]) + radial * normal[c]
            for k, piece in enumerate(split3(force)):
                pieces[kind, k * 3 + c, rows, lanes] = piece
    row_of = lax.broadcasted_iota(jnp.int32, (groups, slots * LANES), 0)
    total = None
    for kind in range(2):
        for e in range(columns):
            here = places[kind, 0, e : e + 1, :] == row_of
            values = jnp.concatenate(
                [jnp.where(here, pieces[kind, k, e : e + 1, :], 0.0) for k in range(9)], axis=0
            ).astype(BF16)
            summed = lax.dot_general(
                values,
                hot[kind * columns + e],
                (((1,), (1,)), ((), ())),
                preferred_element_type=F32,
            )
            total = summed if total is None else total + summed
    height = 3 * groups
    total = total[0:height] + total[height : 2 * height] + total[2 * height : 3 * height]
    for c in range(3):
        for g in range(groups):
            row = c * groups + g
            forces[c : c + 1, g * LANES : (g + 1) * LANES] = total[row : row + 1, :]


def call(kernel, name, outs, *args, specs=None, scratch=(), limit=24):
    many = isinstance(outs, tuple)
    return pl.pallas_call(
        kernel,
        out_shape=outs,
        in_specs=specs or [VMEM] * len(args),
        out_specs=tuple(VMEM for _ in outs) if many else VMEM,
        scratch_shapes=scratch,
        compiler_params=pltpu.CompilerParams(vmem_limit_bytes=limit * 2**20),
        name=name,
    )(*args)


def shape(*dims, dtype=F32):
    return jax.ShapeDtypeStruct(dims, dtype)


def exchange(block, axis, size):
    if size & (size - 1):
        every = lambda k: lax.ppermute(block, axis, [(i, (i + k) % size) for i in range(size)])
        return [every(k)[None] for k in range(1, size)]
    held, rounds = block[None], []
    for k in range(size.bit_length() - 1):
        arrived = lax.ppermute(held, axis, [(i, i ^ (1 << k)) for i in range(size)])
        rounds.append(arrived)
        if k + 2 < size.bit_length():
            held = jnp.concatenate([held, arrived], axis=0)
    return rounds


def add_fields(payload, payloads, mom, moms, kept, columns, keep):
    count = payload.shape[0] // SUBS * LANES
    groups = count // LANES
    sums, made = None, []
    for k, sources in enumerate(payloads):
        is_last = k == len(payloads) - 1
        length = sum(a.shape[0] for a in sources) * count
        args = [payload, *sources]
        if mom is not None:
            args += [mom, *moms[k]]
        if kept:
            args += kept[k][1]
        if sums is not None:
            args.append(sums)
        if not is_last:
            outs = (shape(3 * FEATURES, count),)
        else:
            outs = (shape(3 * groups, LANES),)
            outs += (shape(columns, 3 * groups, LANES),) if columns else ()
        if keep:
            outs += (shape(length, count, dtype=BF16),) * 2
        sums, *now = call(
            functools.partial(
                field_kernel,
                len(sources),
                mom is not None,
                kept[k][0] if kept else None,
                sums is not None,
                is_last,
                columns,
            ),
            "field_sums",
            outs,
            *args,
            scratch=[
                pltpu.VMEM((FEATURES, groups, LANES), F32),
                pltpu.VMEM((PAIR_ROWS, count), BF16),
                pltpu.VMEM((3 * FEATURES + PAIR_ROWS, length), BF16),
                pltpu.VMEM((3 * FEATURES, count), F32),
            ],
        )
        made.append(now)
    return sums, made


def on_device(row_size, positions, velocity, applied, suscept, owner, partner, contact_count):
    count = positions.shape[1]
    columns, slot_len = owner.shape[2:]
    groups, slots = count // LANES, slot_len // LANES
    send_rows = 6 * groups + 2 * slots + 1
    send_rows += -send_rows % SUBS
    def in_hbm(*arrays):
        return [pltpu.with_memory_space_constraint(v, pltpu.HBM) for v in arrays]

    inputs = in_hbm(positions, applied, suscept.reshape(1, count))
    payload = call(
        row_pack_kernel,
        "row_pack",
        shape(8 * groups, LANES),
        *inputs,
        specs=[HBM] * 3,
        scratch=[pltpu.VMEM(v.shape, v.dtype) for v in inputs] + [pltpu.SemaphoreType.DMA((3,))],
    )
    inputs = in_hbm(
        velocity,
        owner.reshape(columns, slot_len),
        partner.reshape(columns, slot_len),
        contact_count.reshape(1, columns),
    )
    sent, table, listed = call(
        column_pack_kernel,
        "column_pack",
        (
            shape(columns, send_rows, LANES),
            shape(6 * groups, LANES),
            shape(2 * slots + 1, columns, LANES, dtype=jnp.int32),
        ),
        *inputs,
        payload,
        specs=[HBM] * 4 + [VMEM],
        scratch=[pltpu.VMEM(v.shape, v.dtype) for v in inputs[:-1]]
        + [pltpu.SMEM((1, columns), jnp.int32), pltpu.SemaphoreType.DMA((4,))],
    )
    rounds = exchange(payload, "row", row_size)
    first, sent = lax.optimization_barrier((rounds[0], sent))
    payloads = [[payload[None], first]] + [[r] for r in rounds[1:]]
    received = lax.all_to_all(sent, "col", split_axis=0, concat_axis=0, tiled=True)
    keep = 4 * row_size * count * count <= KEEP_BYTES
    mom, made = add_fields(payload, payloads, None, None, None, 0, keep)
    kept = [(0, m) for m in made] if keep else None
    for iteration in range(1, ITERS):
        is_last = iteration == ITERS - 1
        arrived = exchange(mom, "row", row_size)
        moms = [[mom[None], arrived[0]]] + [[r] for r in arrived[1:]]
        mom, made = add_fields(
            payload, payloads, mom, moms, kept, columns if is_last else 0, False
        )
    (mom_sent,) = made[-1]
    mom_received = lax.all_to_all(mom_sent, "col", split_axis=0, concat_axis=0, tiled=True)
    moments, geometry, places, hot = call(
        functools.partial(geometry_kernel, slots),
        "contact_geometry",
        (
            shape(3, count),
            shape(len(contact_blocks(columns, slots)), 8, SUBS, LANES),
            shape(2, 3, columns, slot_len, dtype=jnp.int32),
            shape(2 * columns, LANES, slot_len, dtype=BF16),
        ),
        table,
        listed,
        received,
        mom,
    )
    forces = call(
        functools.partial(force_kernel, slots),
        "contact_force",
        shape(3, count),
        geometry,
        places,
        hot,
        mom_received,
        scratch=[pltpu.VMEM((2, 9, columns, slot_len), F32)],
    )
    return (moments, forces)


def solution(mesh):
    placed = (
        P(None, ("col", "row")),
        P(None, ("col", "row")),
        P(None, ("col", "row")),
        P(("col", "row")),
        P("col", "row", None, None),
        P("col", "row", None, None),
        P("col", "row", None),
    )
    return jax.shard_map(
        functools.partial(on_device, mesh.shape["row"]),
        mesh=mesh,
        in_specs=placed,
        out_specs=(P(None, ("col", "row")), P(None, ("col", "row"))),
        check_vma=False,
    )
```

```python
import functools
import math

import jax
import jax.numpy as jnp
from jax import lax
from jax.experimental import pallas as pl
from jax.experimental.pallas import tpu as pltpu
from jax.sharding import PartitionSpec as P

ITERS = 2
LANES = 128
SUBS = 8
FEATURES = 16
PAIR_ROWS = 48
KEEP_BYTES = 20 * 2**20
BLOCK = 512
WIDTH = 256
F32 = jnp.float32
BF16 = jnp.bfloat16
VMEM = pl.BlockSpec(memory_space=pltpu.VMEM)
HBM = pl.BlockSpec(memory_space=pltpu.HBM)


def split3(value):
    high = value.astype(BF16).astype(F32)
    rest = value - high
    middle = rest.astype(BF16).astype(F32)
    return high, middle, rest - middle


def norm_sq(pos):
    return pos[0] * pos[0] + pos[1] * pos[1] + pos[2] * pos[2]


def to_rows(vectors, held):
    for f, vector in enumerate(vectors):
        held[f] = vector
    return [held[0 : len(vectors), g, :] for g in range(held.shape[1])]


def put_pieces(rows, out, first, columns, order):
    for g, row in enumerate(rows):
        pieces = split3(row)
        lanes = slice(columns + g * LANES, columns + (g + 1) * LANES)
        out[first : first + len(order) * row.shape[0], lanes] = jnp.concatenate(
            [pieces[k] for k in order], axis=0
        ).astype(BF16)


def moment_rows(pos, mom, held, out, columns):
    outer = [mom[a] * pos[b] for a in range(3) for b in range(3)]
    along = outer[0] + outer[4] + outer[8]
    square = norm_sq(pos)
    mixed = [3.0 * along * pos[a] - square * mom[a] for a in range(3)]
    put_pieces(to_rows(list(mom) + outer + mixed + [along], held), out, 0, columns, (0, 1, 2))


TARGET_ORDER = (0, 1, 0, 1, 2, 0)
SOURCE_ORDER = (0, 0, 1, 1, 0, 2)


def target_rows(pos, held, out):
    one, zero = jnp.ones_like(pos[0]), jnp.zeros_like(pos[0])
    rows = list(pos) + [one, norm_sq(pos) + 1.0, zero, zero, zero]
    put_pieces(to_rows(rows, held), out, 0, 0, TARGET_ORDER)


def source_rows(pos, held, out, columns):
    one, zero = jnp.ones_like(pos[0]), jnp.zeros_like(pos[0])
    rows = [-2.0 * p for p in pos] + [norm_sq(pos), one, zero, zero, zero]
    put_pieces(to_rows(rows, held), out, 3 * FEATURES, columns, SOURCE_ORDER)


def field_from_sums(sums, held, pos, mom):
    groups = held.shape[1]
    for g in range(groups):
        lanes = slice(g * LANES, (g + 1) * LANES)
        held[0:FEATURES, g, :] = (
            sums[0:FEATURES, lanes]
            + sums[FEATURES : 2 * FEATURES, lanes]
            + sums[2 * FEATURES : 3 * FEATURES, lanes]
        )
    m = [held[a] for a in range(3)]
    outer = [[held[3 + 3 * a + b] for b in range(3)] for a in range(3)]
    trace = outer[0][0] + outer[1][1] + outer[2][2]
    scale_sq = norm_sq(pos) + 1.0
    along = m[0] * pos[0] + m[1] * pos[1] + m[2] * pos[2] - trace
    parts = []
    for a in range(3):
        by_column = outer[0][a] * pos[0] + outer[1][a] * pos[1] + outer[2][a] * pos[2]
        by_row = outer[a][0] * pos[0] + outer[a][1] * pos[1] + outer[a][2] * pos[2]
        parts.append(
            3.0 * (along * pos[a] - by_column)
            + 2.0 * by_row
            + held[12 + a]
            - scale_sq * m[a]
            + mom[a]
        )
    return parts


def pair_coefficient(radius_sq):
    inverse = lax.rsqrt(radius_sq)
    square = inverse * inverse
    fifth = square * square * inverse
    high = fifth.astype(BF16)
    return high, (fifth - high.astype(F32)).astype(BF16)


def vectors_of(ref, first, groups):
    return [ref[first + c * groups : first + (c + 1) * groups, :] for c in range(3)]


def about(pos, center):
    return [p - c for p, c in zip(pos, center)]


def field_kernel(sources, with_mom, kept_at, has_before, is_last, columns, *refs):
    refs = list(refs)
    own = refs.pop(0)
    blocks = [ref.at[k] for ref in refs[:sources] for k in range(ref.shape[0])]
    refs = refs[sources:]
    if with_mom:
        own_mom = refs.pop(0)
        mom_blocks = [ref.at[k] for ref in refs[:sources] for k in range(ref.shape[0])]
        refs = refs[sources:]
    has_kept = kept_at is not None
    kept = (refs.pop(0), refs.pop(0)) if has_kept else None
    before = refs.pop(0) if has_before else None
    outs, (held, target, feats, sums) = refs[:-4], refs[-4:]
    made = outs[1:3] if len(outs) == 3 else None
    groups = held.shape[1]
    count = groups * LANES
    own_pos = vectors_of(own, 0, groups)
    center = [jnp.sum(p, keepdims=True) * (1.0 / count) for p in own_pos]
    pos = about(own_pos, center)
    if not has_kept:
        target_rows(pos, held, target)
    sums[...] = before[...] if has_before else jnp.zeros_like(sums)
    for k, there in enumerate(blocks):
        their_pos = about(vectors_of(there, 0, groups), center)
        if with_mom:
            their_mom = vectors_of(mom_blocks[k], 0, groups)
        else:
            chi = there[6 * groups : 7 * groups, :]
            their_mom = [chi * v for v in vectors_of(there, 3 * groups, groups)]
        moment_rows(their_pos, their_mom, held, feats, k * count)
        if not has_kept:
            source_rows(their_pos, held, feats, k * count)
    height, width = math.gcd(count, BLOCK), math.gcd(count, WIDTH)
    tiles = [
        (slice(a, a + height), slice(b, b + width))
        for a in range(0, len(blocks) * count, height)
        for b in range(0, count, width)
    ]

    def radius_of(tile):
        return lax.dot_general(
            feats[3 * FEATURES :, tile[0]],
            target[:, tile[1]],
            (((0,), (0,)), ((), ())),
            preferred_element_type=F32,
        )

    def add(tile, high, low):
        moments = feats[0 : 3 * FEATURES, tile[0]]
        sums[:, tile[1]] += jnp.dot(moments, high, preferred_element_type=F32) + jnp.dot(
            moments, low, preferred_element_type=F32
        )

    if has_kept:
        for a, b in tiles:
            rows = slice(kept_at + a.start, kept_at + a.stop)
            add((a, b), kept[0][rows, b], kept[1][rows, b])
    else:
        radius_sq, ready = radius_of(tiles[0]), None
        for at, tile in enumerate(tiles):
            following = radius_of(tiles[at + 1]) if at + 1 < len(tiles) else None
            high, low = pair_coefficient(radius_sq)
            if made:
                made[0][tile] = high
                made[1][tile] = low
            if ready is not None:
                add(*ready)
            ready, radius_sq = (tile, high, low), following
        add(*ready)
    if not is_last:
        outs[0][...] = sums[...]
        return
    applied = vectors_of(own, 3 * groups, groups)
    chi = own[6 * groups : 7 * groups, :]
    own_now = vectors_of(own_mom, 0, groups) if with_mom else [chi * v for v in applied]
    field = field_from_sums(sums, held, pos, own_now)
    for a in range(3):
        result = chi * (applied[a] + field[a])
        rows = slice(a * groups, (a + 1) * groups)
        outs[0][rows, :] = result
        for e in range(columns):
            outs[1][e, rows, :] = result


def copy_in(inputs, held, done):
    copies = [
        pltpu.make_async_copy(src, dst, done.at[k]) for k, (src, dst) in enumerate(zip(inputs, held))
    ]
    for copy in copies:
        copy.start()
    for copy in copies:
        copy.wait()


def column_order(columns):
    return [(k + columns // 2) % columns for k in range(columns)]


def to_columns(blocks):
    return lax.all_to_all(
        blocks,
        "col",
        split_axis=0,
        concat_axis=0,
        axis_index_groups=[column_order(blocks.shape[0])],
        tiled=True,
    )


def row_pack_kernel(*refs):
    inputs, payload, (pos, field, chi, done) = refs[0:3], refs[3], refs[4:]
    copy_in(inputs, (pos, field, chi), done)
    groups = pos.shape[1] // LANES
    for g in range(groups):
        lanes = slice(g * LANES, (g + 1) * LANES)
        for c in range(3):
            payload[c * groups + g : c * groups + g + 1, :] = pos[c : c + 1, lanes]
            row = (3 + c) * groups + g
            payload[row : row + 1, :] = field[c : c + 1, lanes]
        payload[6 * groups + g : 6 * groups + g + 1, :] = chi[:, lanes]
    payload[7 * groups :, :] = jnp.zeros_like(payload[7 * groups :, :])


def column_pack_kernel(*refs):
    inputs, payload, (send, table, listed), (vel, owner, partner, counts, done) = (
        refs[0:4],
        refs[4],
        refs[5:8],
        refs[8:],
    )
    copy_in(inputs, (vel, owner, partner, counts), done)
    groups = vel.shape[1] // LANES
    slots = owner.shape[1] // LANES
    columns = owner.shape[0]
    table[0 : 3 * groups, :] = payload[0 : 3 * groups, :]
    for g in range(groups):
        for c in range(3):
            row = (3 + c) * groups + g
            table[row : row + 1, :] = vel[c : c + 1, g * LANES : (g + 1) * LANES]
    for e in range(columns):
        send[e, 0 : 6 * groups, :] = table[...]
        live = jnp.full(
            (send.shape[1] - 6 * groups - 2 * slots, LANES), counts[0, column_order(columns)[e]]
        )
        send[e, 6 * groups + 2 * slots :, :] = live.astype(F32)
        listed[2 * slots, e : e + 1, :] = live[0:1]
    for q in range(slots):
        lanes = slice(q * LANES, (q + 1) * LANES)
        for k, ref in enumerate((owner, partner)):
            half = columns // 2
            index = jnp.concatenate([ref[half:, lanes], ref[:half, lanes]], axis=0)
            send[:, 6 * groups + k * slots + q, :] = index.astype(F32)
            listed[k * slots + q] = index


def split_index(index):
    return index & (LANES - 1), index >> (LANES.bit_length() - 1)


def look_up(tables, lane, bits):
    found = [jnp.take_along_axis(t, lane, axis=1, mode="promise_in_bounds") for t in tables]
    for bit in bits:
        found = [
            jnp.where(bit, found[k + 1], found[k]) if k + 1 < len(found) else found[k]
            for k in range(0, len(found), 2)
        ]
    return found[0]


def bits_of(group, groups):
    return [(group >> k) & 1 == 1 for k in range((groups - 1).bit_length())]


def own_tables(ref, first, groups):
    return [
        jnp.broadcast_to(ref[first + g : first + g + 1, :], (SUBS, LANES)) for g in range(groups)
    ]


def their_tables(ref, rows, first, groups):
    return [ref[rows, first + g, :] for g in range(groups)]


def slot_index(listed, received, kind, rows, q, groups, slots):
    if kind:
        first = 6 * groups + q
        owner, partner, count = (
            received[rows, row, :].astype(jnp.int32)
            for row in (first, first + slots, 6 * groups + 2 * slots)
        )
    else:
        owner, partner, count = (listed[row, rows, :] for row in (q, slots + q, 2 * slots))
    live = lax.broadcasted_iota(jnp.int32, (SUBS, LANES), 1) + q * LANES < count
    return (partner, owner, live) if kind else (owner, partner, live)


def contact_blocks(columns, slots):
    return [
        (kind, slice(first, first + SUBS), q)
        for kind in range(2)
        for first in range(0, columns, SUBS)
        for q in range(slots)
    ]


def geometry_kernel(slots, table, listed, received, mom, moments, out, places, hot):
    columns = received.shape[0]
    groups = mom.shape[0] // 3
    for c in range(3):
        for g in range(groups):
            lanes = slice(g * LANES, (g + 1) * LANES)
            moments[c : c + 1, lanes] = mom[c * groups + g : c * groups + g + 1, :]
    for at, (kind, rows, q) in enumerate(contact_blocks(columns, slots)):
        mine, other, live = slot_index(listed, received, kind, rows, q, groups, slots)
        lane, group = split_index(mine)
        bits = bits_of(group, groups)
        their_lane, their_group = split_index(other)
        their_bits = bits_of(their_group, groups)
        gap = []
        for c in range(6):
            gap.append(
                look_up(own_tables(table, c * groups, groups), lane, bits)
                - look_up(
                    their_tables(received, rows, c * groups, groups), their_lane, their_bits
                )
            )
        radius_sq = gap[0] * gap[0] + gap[1] * gap[1] + gap[2] * gap[2] + 1.0
        inverse = lax.rsqrt(radius_sq)
        normal = [jnp.where(live, gap[c] * inverse, 0.0) for c in range(3)]
        speed = gap[3] * normal[0] + gap[4] * normal[1] + gap[5] * normal[2]
        own = [look_up(own_tables(mom, c * groups, groups), lane, bits) for c in range(3)]
        for c in range(3):
            out[at, c] = normal[c]
            out[at, 3 + c] = own[c]
        out[at, 6] = -0.03 * (radius_sq * inverse - 1.0) - 0.5 * speed
        out[at, 7] = own[0] * normal[0] + own[1] * normal[1] + own[2] * normal[2]
        lanes = slice(q * LANES, (q + 1) * LANES)
        places[kind, 0, rows, lanes] = group
        places[kind, 1, rows, lanes] = lane
        places[kind, 2, rows, lanes] = other
    lane_of = lax.broadcasted_iota(jnp.int32, (LANES, slots * LANES), 0)
    for kind in range(2):
        for e in range(columns):
            here = places[kind, 1, e : e + 1, :] == lane_of
            hot[kind * columns + e] = jnp.where(here, 1.0, 0.0).astype(BF16)


def force_kernel(slots, geometry, places, hot, mom_received, forces, pieces):
    columns = mom_received.shape[0]
    groups = mom_received.shape[1] // 3
    for at, (kind, rows, q) in enumerate(contact_blocks(columns, slots)):
        lanes = slice(q * LANES, (q + 1) * LANES)
        their_lane, their_group = split_index(places[kind, 2, rows, lanes])
        their_bits = bits_of(their_group, groups)
        normal = [geometry[at, c] for c in range(3)]
        own = [geometry[at, 3 + c] for c in range(3)]
        along_own = geometry[at, 7]
        their = [
            look_up(their_tables(mom_received, rows, c * groups, groups), their_lane, their_bits)
            for c in range(3)
        ]
        along_their = their[0] * normal[0] + their[1] * normal[1] + their[2] * normal[2]
        product = own[0] * their[0] + own[1] * their[1] + own[2] * their[2]
        radial = 3.0 * (product - 5.0 * along_own * along_their) + geometry[at, 6]
        for c in range(3):
            force = 3.0 * (along_own * their[c] + along_their * own[c]) + radial * normal[c]
            for k, piece in enumerate(split3(force)):
                pieces[kind, k * 3 + c, rows, lanes] = piece
    row_of = lax.broadcasted_iota(jnp.int32, (groups, slots * LANES), 0)
    total = None
    for kind in range(2):
        for e in range(columns):
            here = places[kind, 0, e : e + 1, :] == row_of
            values = jnp.concatenate(
                [jnp.where(here, pieces[kind, k, e : e + 1, :], 0.0) for k in range(9)], axis=0
            ).astype(BF16)
            summed = lax.dot_general(
                values,
                hot[kind * columns + e],
                (((1,), (1,)), ((), ())),
                preferred_element_type=F32,
            )
            total = summed if total is None else total + summed
    height = 3 * groups
    total = total[0:height] + total[height : 2 * height] + total[2 * height : 3 * height]
    for c in range(3):
        for g in range(groups):
            row = c * groups + g
            forces[c : c + 1, g * LANES : (g + 1) * LANES] = total[row : row + 1, :]


def call(kernel, name, outs, *args, specs=None, scratch=(), limit=24):
    many = isinstance(outs, tuple)
    return pl.pallas_call(
        kernel,
        out_shape=outs,
        in_specs=specs or [VMEM] * len(args),
        out_specs=tuple(VMEM for _ in outs) if many else VMEM,
        scratch_shapes=scratch,
        compiler_params=pltpu.CompilerParams(vmem_limit_bytes=limit * 2**20),
        name=name,
    )(*args)


def shape(*dims, dtype=F32):
    return jax.ShapeDtypeStruct(dims, dtype)


def exchange(block, axis, size):
    if size & (size - 1):
        every = lambda k: lax.ppermute(block, axis, [(i, (i + k) % size) for i in range(size)])
        return [every(k)[None] for k in range(1, size)]
    held, rounds = block[None], []
    for k in range(size.bit_length() - 1):
        arrived = lax.ppermute(held, axis, [(i, i ^ (1 << k)) for i in range(size)])
        rounds.append(arrived)
        if k + 2 < size.bit_length():
            held = jnp.concatenate([held, arrived], axis=0)
    return rounds


def add_fields(payload, payloads, mom, moms, kept, columns, keep):
    count = payload.shape[0] // SUBS * LANES
    groups = count // LANES
    sums, made = None, []
    for k, sources in enumerate(payloads):
        is_last = k == len(payloads) - 1
        length = sum(a.shape[0] for a in sources) * count
        args = [payload, *sources]
        if mom is not None:
            args += [mom, *moms[k]]
        if kept:
            args += kept[k][1]
        if sums is not None:
            args.append(sums)
        if not is_last:
            outs = (shape(3 * FEATURES, count),)
        else:
            outs = (shape(3 * groups, LANES),)
            outs += (shape(columns, 3 * groups, LANES),) if columns else ()
        if keep:
            outs += (shape(length, count, dtype=BF16),) * 2
        sums, *now = call(
            functools.partial(
                field_kernel,
                len(sources),
                mom is not None,
                kept[k][0] if kept else None,
                sums is not None,
                is_last,
                columns,
            ),
            "field_sums",
            outs,
            *args,
            scratch=[
                pltpu.VMEM((FEATURES, groups, LANES), F32),
                pltpu.VMEM((PAIR_ROWS, count), BF16),
                pltpu.VMEM((3 * FEATURES + PAIR_ROWS, length), BF16),
                pltpu.VMEM((3 * FEATURES, count), F32),
            ],
        )
        made.append(now)
    return sums, made


def on_device(row_size, positions, velocity, applied, suscept, owner, partner, contact_count):
    count = positions.shape[1]
    columns, slot_len = owner.shape[2:]
    groups, slots = count // LANES, slot_len // LANES
    send_rows = 6 * groups + 2 * slots + 1
    send_rows += -send_rows % SUBS
    def in_hbm(*arrays):
        return [pltpu.with_memory_space_constraint(v, pltpu.HBM) for v in arrays]

    inputs = in_hbm(positions, applied, suscept.reshape(1, count))
    payload = call(
        row_pack_kernel,
        "row_pack",
        shape(8 * groups, LANES),
        *inputs,
        specs=[HBM] * 3,
        scratch=[pltpu.VMEM(v.shape, v.dtype) for v in inputs] + [pltpu.SemaphoreType.DMA((3,))],
    )
    inputs = in_hbm(
        velocity,
        owner.reshape(columns, slot_len),
        partner.reshape(columns, slot_len),
        contact_count.reshape(1, columns),
    )
    sent, table, listed = call(
        column_pack_kernel,
        "column_pack",
        (
            shape(columns, send_rows, LANES),
            shape(6 * groups, LANES),
            shape(2 * slots + 1, columns, LANES, dtype=jnp.int32),
        ),
        *inputs,
        payload,
        specs=[HBM] * 4 + [VMEM],
        scratch=[pltpu.VMEM(v.shape, v.dtype) for v in inputs[:-1]]
        + [pltpu.SMEM((1, columns), jnp.int32), pltpu.SemaphoreType.DMA((4,))],
    )
    rounds = exchange(payload, "row", row_size)
    first, sent = lax.optimization_barrier((rounds[0], sent))
    payloads = [[payload[None], first]] + [[r] for r in rounds[1:]]
    received = to_columns(sent)
    keep = 4 * row_size * count * count <= KEEP_BYTES
    mom, made = add_fields(payload, payloads, None, None, None, 0, keep)
    kept = [(0, m) for m in made] if keep else None
    for iteration in range(1, ITERS):
        is_last = iteration == ITERS - 1
        arrived = exchange(mom, "row", row_size)
        moms = [[mom[None], arrived[0]]] + [[r] for r in arrived[1:]]
        mom, made = add_fields(
            payload, payloads, mom, moms, kept, columns if is_last else 0, False
        )
    (mom_sent,) = made[-1]
    mom_received = to_columns(mom_sent)
    moments, geometry, places, hot = call(
        functools.partial(geometry_kernel, slots),
        "contact_geometry",
        (
            shape(3, count),
            shape(len(contact_blocks(columns, slots)), 8, SUBS, LANES),
            shape(2, 3, columns, slot_len, dtype=jnp.int32),
            shape(2 * columns, LANES, slot_len, dtype=BF16),
        ),
        table,
        listed,
        received,
        mom,
    )
    forces = call(
        functools.partial(force_kernel, slots),
        "contact_force",
        shape(3, count),
        geometry,
        places,
        hot,
        mom_received,
        scratch=[pltpu.VMEM((2, 9, columns, slot_len), F32)],
    )
    return (moments, forces)


def solution(mesh):
    placed = (
        P(None, ("col", "row")),
        P(None, ("col", "row")),
        P(None, ("col", "row")),
        P(("col", "row")),
        P("col", "row", None, None),
        P("col", "row", None, None),
        P("col", "row", None),
    )
    return jax.shard_map(
        functools.partial(on_device, mesh.shape["row"]),
        mesh=mesh,
        in_specs=placed,
        out_specs=(P(None, ("col", "row")), P(None, ("col", "row"))),
        check_vma=False,
    )
```

```python
import functools
import math

import jax
import jax.numpy as jnp
from jax import lax
from jax.experimental import pallas as pl
from jax.experimental.pallas import tpu as pltpu
from jax.sharding import PartitionSpec as P

ITERS = 2
LANES = 128
SUBS = 8
FEATURES = 16
PAIR_ROWS = 48
KEEP_BYTES = 20 * 2**20
BLOCK = 512
WIDTH = 256
F32 = jnp.float32
BF16 = jnp.bfloat16
VMEM = pl.BlockSpec(memory_space=pltpu.VMEM)
HBM = pl.BlockSpec(memory_space=pltpu.HBM)


def split3(value):
    high = value.astype(BF16).astype(F32)
    rest = value - high
    middle = rest.astype(BF16).astype(F32)
    return high, middle, rest - middle


def norm_sq(pos):
    return pos[0] * pos[0] + pos[1] * pos[1] + pos[2] * pos[2]


def to_rows(vectors, held):
    for f, vector in enumerate(vectors):
        held[f] = vector
    return [held[0 : len(vectors), g, :] for g in range(held.shape[1])]


def put_pieces(rows, out, first, columns, order):
    for g, row in enumerate(rows):
        pieces = split3(row)
        lanes = slice(columns + g * LANES, columns + (g + 1) * LANES)
        out[first : first + len(order) * row.shape[0], lanes] = jnp.concatenate(
            [pieces[k] for k in order], axis=0
        ).astype(BF16)


def moment_rows(pos, mom, held, out, columns):
    outer = [mom[a] * pos[b] for a in range(3) for b in range(3)]
    along = outer[0] + outer[4] + outer[8]
    square = norm_sq(pos)
    mixed = [3.0 * along * pos[a] - square * mom[a] for a in range(3)]
    put_pieces(to_rows(list(mom) + outer + mixed + [along], held), out, 0, columns, (0, 1, 2))


TARGET_ORDER = (0, 1, 0, 1, 2, 0)
SOURCE_ORDER = (0, 0, 1, 1, 0, 2)


def target_rows(pos, held, out):
    one, zero = jnp.ones_like(pos[0]), jnp.zeros_like(pos[0])
    rows = list(pos) + [one, norm_sq(pos) + 1.0, zero, zero, zero]
    put_pieces(to_rows(rows, held), out, 0, 0, TARGET_ORDER)


def source_rows(pos, held, out, columns):
    one, zero = jnp.ones_like(pos[0]), jnp.zeros_like(pos[0])
    rows = [-2.0 * p for p in pos] + [norm_sq(pos), one, zero, zero, zero]
    put_pieces(to_rows(rows, held), out, 3 * FEATURES, columns, SOURCE_ORDER)


def field_from_sums(sums, held, pos, mom):
    groups = held.shape[1]
    for g in range(groups):
        lanes = slice(g * LANES, (g + 1) * LANES)
        held[0:FEATURES, g, :] = (
            sums[0:FEATURES, lanes]
            + sums[FEATURES : 2 * FEATURES, lanes]
            + sums[2 * FEATURES : 3 * FEATURES, lanes]
        )
    m = [held[a] for a in range(3)]
    outer = [[held[3 + 3 * a + b] for b in range(3)] for a in range(3)]
    trace = outer[0][0] + outer[1][1] + outer[2][2]
    scale_sq = norm_sq(pos) + 1.0
    along = m[0] * pos[0] + m[1] * pos[1] + m[2] * pos[2] - trace
    parts = []
    for a in range(3):
        by_column = outer[0][a] * pos[0] + outer[1][a] * pos[1] + outer[2][a] * pos[2]
        by_row = outer[a][0] * pos[0] + outer[a][1] * pos[1] + outer[a][2] * pos[2]
        parts.append(
            3.0 * (along * pos[a] - by_column)
            + 2.0 * by_row
            + held[12 + a]
            - scale_sq * m[a]
            + mom[a]
        )
    return parts


def pair_coefficient(radius_sq):
    inverse = lax.rsqrt(radius_sq)
    square = inverse * inverse
    fifth = square * square * inverse
    high = fifth.astype(BF16)
    return high, (fifth - high.astype(F32)).astype(BF16)


def vectors_of(ref, first, groups):
    return [ref[first + c * groups : first + (c + 1) * groups, :] for c in range(3)]


def about(pos, center):
    return [p - c for p, c in zip(pos, center)]


def field_kernel(sources, picks, with_mom, has_kept, has_before, is_last, columns, *refs):
    refs = list(refs)
    own = refs.pop(0)
    blocks = [ref.at[k] for ref in refs[:sources] for k in range(ref.shape[0])]
    blocks = [blocks[k] for k in picks]
    refs = refs[sources:]
    if with_mom:
        own_mom = refs.pop(0)
        mom_blocks = []
        while len(mom_blocks) < len(picks):
            mom_blocks += [refs[0].at[k] for k in range(refs[0].shape[0])]
            refs.pop(0)
    kept = (refs.pop(0), refs.pop(0)) if has_kept else None
    before = refs.pop(0) if has_before else None
    outs, (held, target, feats, sums) = refs[:-4], refs[-4:]
    made = outs[1:3] if len(outs) == 3 else None
    groups = held.shape[1]
    count = groups * LANES
    own_pos = vectors_of(own, 0, groups)
    center = [jnp.sum(p, keepdims=True) * (1.0 / count) for p in own_pos]
    pos = about(own_pos, center)
    if not has_kept:
        target_rows(pos, held, target)
    sums[...] = before[...] if has_before else jnp.zeros_like(sums)
    for k, there in enumerate(blocks):
        their_pos = about(vectors_of(there, 0, groups), center)
        if with_mom:
            their_mom = vectors_of(mom_blocks[k], 0, groups)
        else:
            chi = there[6 * groups : 7 * groups, :]
            their_mom = [chi * v for v in vectors_of(there, 3 * groups, groups)]
        moment_rows(their_pos, their_mom, held, feats, k * count)
        if not has_kept:
            source_rows(their_pos, held, feats, k * count)
    height, width = math.gcd(count, BLOCK), math.gcd(count, WIDTH)
    tiles = [
        (slice(a, a + height), slice(b, b + width))
        for a in range(0, len(blocks) * count, height)
        for b in range(0, count, width)
    ]

    def radius_of(tile):
        return lax.dot_general(
            feats[3 * FEATURES :, tile[0]],
            target[:, tile[1]],
            (((0,), (0,)), ((), ())),
            preferred_element_type=F32,
        )

    def add(tile, high, low):
        moments = feats[0 : 3 * FEATURES, tile[0]]
        sums[:, tile[1]] += jnp.dot(moments, high, preferred_element_type=F32) + jnp.dot(
            moments, low, preferred_element_type=F32
        )

    if has_kept:
        for a, b in tiles:
            k, at = divmod(a.start, count)
            rows = slice(picks[k] * count + at, picks[k] * count + at + height)
            add((a, b), kept[0][rows, b], kept[1][rows, b])
    else:
        radius_sq, ready = radius_of(tiles[0]), None
        for at, tile in enumerate(tiles):
            following = radius_of(tiles[at + 1]) if at + 1 < len(tiles) else None
            high, low = pair_coefficient(radius_sq)
            if made:
                made[0][tile] = high
                made[1][tile] = low
            if ready is not None:
                add(*ready)
            ready, radius_sq = (tile, high, low), following
        add(*ready)
    if not is_last:
        outs[0][...] = sums[...]
        return
    applied = vectors_of(own, 3 * groups, groups)
    chi = own[6 * groups : 7 * groups, :]
    own_now = vectors_of(own_mom, 0, groups) if with_mom else [chi * v for v in applied]
    field = field_from_sums(sums, held, pos, own_now)
    for a in range(3):
        result = chi * (applied[a] + field[a])
        rows = slice(a * groups, (a + 1) * groups)
        outs[0][rows, :] = result
        for e in range(columns):
            outs[1][e, rows, :] = result


def copy_in(inputs, held, done):
    copies = [
        pltpu.make_async_copy(src, dst, done.at[k]) for k, (src, dst) in enumerate(zip(inputs, held))
    ]
    for copy in copies:
        copy.start()
    for copy in copies:
        copy.wait()


def column_order(columns):
    return [(k + columns // 2) % columns for k in range(columns)]


def to_columns(blocks):
    return lax.all_to_all(
        blocks,
        "col",
        split_axis=0,
        concat_axis=0,
        axis_index_groups=[column_order(blocks.shape[0])],
        tiled=True,
    )


def row_pack_kernel(*refs):
    inputs, payload, (pos, field, chi, done) = refs[0:3], refs[3], refs[4:]
    copy_in(inputs, (pos, field, chi), done)
    groups = pos.shape[1] // LANES
    for g in range(groups):
        lanes = slice(g * LANES, (g + 1) * LANES)
        for c in range(3):
            payload[c * groups + g : c * groups + g + 1, :] = pos[c : c + 1, lanes]
            row = (3 + c) * groups + g
            payload[row : row + 1, :] = field[c : c + 1, lanes]
        payload[6 * groups + g : 6 * groups + g + 1, :] = chi[:, lanes]
    payload[7 * groups :, :] = jnp.zeros_like(payload[7 * groups :, :])


def column_pack_kernel(*refs):
    inputs, payload, (send, table, listed), (vel, owner, partner, counts, done) = (
        refs[0:4],
        refs[4],
        refs[5:8],
        refs[8:],
    )
    copy_in(inputs, (vel, owner, partner, counts), done)
    groups = vel.shape[1] // LANES
    slots = owner.shape[1] // LANES
    columns = owner.shape[0]
    table[0 : 3 * groups, :] = payload[0 : 3 * groups, :]
    for g in range(groups):
        for c in range(3):
            row = (3 + c) * groups + g
            table[row : row + 1, :] = vel[c : c + 1, g * LANES : (g + 1) * LANES]
    for e in range(columns):
        send[e, 0 : 6 * groups, :] = table[...]
        live = jnp.full(
            (send.shape[1] - 6 * groups - 2 * slots, LANES), counts[0, column_order(columns)[e]]
        )
        send[e, 6 * groups + 2 * slots :, :] = live.astype(F32)
        listed[2 * slots, e : e + 1, :] = live[0:1]
    for q in range(slots):
        lanes = slice(q * LANES, (q + 1) * LANES)
        for k, ref in enumerate((owner, partner)):
            half = columns // 2
            index = jnp.concatenate([ref[half:, lanes], ref[:half, lanes]], axis=0)
            send[:, 6 * groups + k * slots + q, :] = index.astype(F32)
            listed[k * slots + q] = index


def split_index(index):
    return index & (LANES - 1), index >> (LANES.bit_length() - 1)


def look_up(tables, lane, bits):
    found = [jnp.take_along_axis(t, lane, axis=1, mode="promise_in_bounds") for t in tables]
    for bit in bits:
        found = [
            jnp.where(bit, found[k + 1], found[k]) if k + 1 < len(found) else found[k]
            for k in range(0, len(found), 2)
        ]
    return found[0]


def bits_of(group, groups):
    return [(group >> k) & 1 == 1 for k in range((groups - 1).bit_length())]


def own_tables(ref, first, groups):
    return [
        jnp.broadcast_to(ref[first + g : first + g + 1, :], (SUBS, LANES)) for g in range(groups)
    ]


def their_tables(ref, rows, first, groups):
    return [ref[rows, first + g, :] for g in range(groups)]


def slot_index(listed, received, kind, rows, q, groups, slots):
    if kind:
        first = 6 * groups + q
        owner, partner, count = (
            received[rows, row, :].astype(jnp.int32)
            for row in (first, first + slots, 6 * groups + 2 * slots)
        )
    else:
        owner, partner, count = (listed[row, rows, :] for row in (q, slots + q, 2 * slots))
    live = lax.broadcasted_iota(jnp.int32, (SUBS, LANES), 1) + q * LANES < count
    return (partner, owner, live) if kind else (owner, partner, live)


def contact_blocks(columns, slots):
    return [
        (kind, slice(first, first + SUBS), q)
        for kind in range(2)
        for first in range(0, columns, SUBS)
        for q in range(slots)
    ]


def geometry_kernel(slots, table, listed, received, mom, moments, out, places, hot):
    columns = received.shape[0]
    groups = mom.shape[0] // 3
    for c in range(3):
        for g in range(groups):
            lanes = slice(g * LANES, (g + 1) * LANES)
            moments[c : c + 1, lanes] = mom[c * groups + g : c * groups + g + 1, :]
    for at, (kind, rows, q) in enumerate(contact_blocks(columns, slots)):
        mine, other, live = slot_index(listed, received, kind, rows, q, groups, slots)
        lane, group = split_index(mine)
        bits = bits_of(group, groups)
        their_lane, their_group = split_index(other)
        their_bits = bits_of(their_group, groups)
        gap = []
        for c in range(6):
            gap.append(
                look_up(own_tables(table, c * groups, groups), lane, bits)
                - look_up(
                    their_tables(received, rows, c * groups, groups), their_lane, their_bits
                )
            )
        radius_sq = gap[0] * gap[0] + gap[1] * gap[1] + gap[2] * gap[2] + 1.0
        inverse = lax.rsqrt(radius_sq)
        normal = [jnp.where(live, gap[c] * inverse, 0.0) for c in range(3)]
        speed = gap[3] * normal[0] + gap[4] * normal[1] + gap[5] * normal[2]
        own = [look_up(own_tables(mom, c * groups, groups), lane, bits) for c in range(3)]
        for c in range(3):
            out[at, c] = normal[c]
            out[at, 3 + c] = own[c]
        out[at, 6] = -0.03 * (radius_sq * inverse - 1.0) - 0.5 * speed
        out[at, 7] = own[0] * normal[0] + own[1] * normal[1] + own[2] * normal[2]
        lanes = slice(q * LANES, (q + 1) * LANES)
        places[kind, 0, rows, lanes] = group
        places[kind, 1, rows, lanes] = lane
        places[kind, 2, rows, lanes] = other
    lane_of = lax.broadcasted_iota(jnp.int32, (LANES, slots * LANES), 0)
    for kind in range(2):
        for e in range(columns):
            here = places[kind, 1, e : e + 1, :] == lane_of
            width = slots * LANES
            first = (kind * columns + e) * width
            hot[:, first : first + width] = jnp.where(here, 1.0, 0.0).astype(BF16)


def force_kernel(slots, geometry, places, hot, mom_received, forces, pieces, values):
    columns = mom_received.shape[0]
    groups = mom_received.shape[1] // 3
    for at, (kind, rows, q) in enumerate(contact_blocks(columns, slots)):
        lanes = slice(q * LANES, (q + 1) * LANES)
        their_lane, their_group = split_index(places[kind, 2, rows, lanes])
        their_bits = bits_of(their_group, groups)
        normal = [geometry[at, c] for c in range(3)]
        own = [geometry[at, 3 + c] for c in range(3)]
        along_own = geometry[at, 7]
        their = [
            look_up(their_tables(mom_received, rows, c * groups, groups), their_lane, their_bits)
            for c in range(3)
        ]
        along_their = their[0] * normal[0] + their[1] * normal[1] + their[2] * normal[2]
        product = own[0] * their[0] + own[1] * their[1] + own[2] * their[2]
        radial = 3.0 * (product - 5.0 * along_own * along_their) + geometry[at, 6]
        for c in range(3):
            force = 3.0 * (along_own * their[c] + along_their * own[c]) + radial * normal[c]
            for k, piece in enumerate(split3(force)):
                pieces[kind, k * 3 + c, rows, lanes] = piece
    width = slots * LANES
    row_of = lax.broadcasted_iota(jnp.int32, (groups, width), 0)
    for kind in range(2):
        for e in range(columns):
            here = places[kind, 0, e : e + 1, :] == row_of
            first = (kind * columns + e) * width
            values[:, first : first + width] = jnp.concatenate(
                [jnp.where(here, pieces[kind, k, e : e + 1, :], 0.0) for k in range(9)], axis=0
            ).astype(BF16)
    total = lax.dot_general(
        values[...], hot[...], (((1,), (1,)), ((), ())), preferred_element_type=F32
    )
    height = 3 * groups
    total = total[0:height] + total[height : 2 * height] + total[2 * height : 3 * height]
    for c in range(3):
        for g in range(groups):
            row = c * groups + g
            forces[c : c + 1, g * LANES : (g + 1) * LANES] = total[row : row + 1, :]


def call(kernel, name, outs, *args, specs=None, scratch=(), limit=24):
    many = isinstance(outs, tuple)
    return pl.pallas_call(
        kernel,
        out_shape=outs,
        in_specs=specs or [VMEM] * len(args),
        out_specs=tuple(VMEM for _ in outs) if many else VMEM,
        scratch_shapes=scratch,
        compiler_params=pltpu.CompilerParams(vmem_limit_bytes=limit * 2**20),
        name=name,
    )(*args)


def shape(*dims, dtype=F32):
    return jax.ShapeDtypeStruct(dims, dtype)


def flip(blocks, axis, size, bit):
    return lax.ppermute(blocks, axis, [(i, i ^ (1 << bit)) for i in range(size)])


def others(block, axis, size):
    return [lax.ppermute(block, axis, [(i, (i + k) % size) for i in range(size)])[None] for k in range(1, size)]


def exchange(block, axis, size, first=0):
    held, rounds = block[None], []
    for bit in range(first, size.bit_length() - 1):
        rounds.append(flip(held, axis, size, bit))
        if bit + 2 < size.bit_length():
            held = jnp.concatenate([held, rounds[-1]], axis=0)
    return rounds


def add_fields(payload, parts, mom, columns, keep):
    count = payload.shape[0] // SUBS * LANES
    groups = count // LANES
    sums, made = None, []
    for at, (sources, picks, moms, kept) in enumerate(parts):
        is_last = at == len(parts) - 1
        length = len(picks) * count
        args = [payload, *sources]
        if callable(moms):
            moms, sums = moms(sums)
        if mom is not None:
            args += [mom, *moms]
        args += kept
        if sums is not None:
            args.append(sums)
        if not is_last:
            outs = (shape(3 * FEATURES, count),)
        else:
            outs = (shape(3 * groups, LANES),)
            outs += (shape(columns, 3 * groups, LANES),) if columns else ()
        if keep:
            outs += (shape(length, count, dtype=BF16),) * 2
        sums, *now = call(
            functools.partial(
                field_kernel,
                len(sources),
                picks,
                mom is not None,
                bool(kept),
                sums is not None,
                is_last,
                columns,
            ),
            "field_sums",
            outs,
            *args,
            scratch=[
                pltpu.VMEM((FEATURES, groups, LANES), F32),
                pltpu.VMEM((PAIR_ROWS, count), BF16),
                pltpu.VMEM((3 * FEATURES + PAIR_ROWS, length), BF16),
                pltpu.VMEM((3 * FEATURES, count), F32),
            ],
        )
        made.append(now)
    return sums, made


def on_device(row_size, positions, velocity, applied, suscept, owner, partner, contact_count):
    count = positions.shape[1]
    columns, slot_len = owner.shape[2:]
    groups, slots = count // LANES, slot_len // LANES
    send_rows = 6 * groups + 2 * slots + 1
    send_rows += -send_rows % SUBS
    def in_hbm(*arrays):
        return [pltpu.with_memory_space_constraint(v, pltpu.HBM) for v in arrays]

    inputs = in_hbm(positions, applied, suscept.reshape(1, count))
    payload = call(
        row_pack_kernel,
        "row_pack",
        shape(8 * groups, LANES),
        *inputs,
        specs=[HBM] * 3,
        scratch=[pltpu.VMEM(v.shape, v.dtype) for v in inputs] + [pltpu.SemaphoreType.DMA((3,))],
    )
    inputs = in_hbm(
        velocity,
        owner.reshape(columns, slot_len),
        partner.reshape(columns, slot_len),
        contact_count.reshape(1, columns),
    )
    sent, table, listed = call(
        column_pack_kernel,
        "column_pack",
        (
            shape(columns, send_rows, LANES),
            shape(6 * groups, LANES),
            shape(2 * slots + 1, columns, LANES, dtype=jnp.int32),
        ),
        *inputs,
        payload,
        specs=[HBM] * 4 + [VMEM],
        scratch=[pltpu.VMEM(v.shape, v.dtype) for v in inputs[:-1]]
        + [pltpu.SMEM((1, columns), jnp.int32), pltpu.SemaphoreType.DMA((4,))],
    )
    paired = row_size > 1 and row_size & (row_size - 1) == 0
    rounds = (exchange if paired else others)(payload, "row", row_size)
    if rounds:
        first, sent = lax.optimization_barrier((rounds[0], sent))
        rounds = [first] + rounds[1:]
    received = to_columns(sent)
    keep = 4 * row_size * count * count <= KEEP_BYTES
    sources = [[payload[None]] + rounds[:1]] + [[r] for r in rounds[1:]]
    sizes = [sum(a.shape[0] for a in arrays) for arrays in sources]
    parts = [(a, tuple(range(n)), [], []) for a, n in zip(sources, sizes)]
    mom, kept = add_fields(payload, parts, None, 0, keep)
    for iteration in range(1, ITERS):
        is_last = iteration == ITERS - 1
        if paired:
            far = exchange(mom, "row", row_size, 1)
            moms = [[mom[None], flip(mom[None], "row", row_size, 0)]]
            parts = [(sources[0], (0, 1), moms[0], kept[0])]
            for k, direct in enumerate(far):
                evens, odds = tuple(range(0, sizes[k + 1], 2)), tuple(range(1, sizes[k + 1], 2))
                passed = []

                def handed_on(sums, direct=direct, passed=passed):
                    direct, sums = lax.optimization_barrier((direct, sums))
                    passed.append(flip(direct, "row", row_size, 0))
                    return [direct], sums

                parts.append((sources[k + 1], evens, handed_on, kept[k + 1]))
                parts.append((sources[k + 1], odds, lambda sums, p=passed: (p, sums), kept[k + 1]))
        else:
            moms = [[mom[None]] + others(mom, "row", row_size)[:1]]
            moms += [[r] for r in others(mom, "row", row_size)[1:]]
            parts = [(a, tuple(range(n)), m, k) for a, n, m, k in zip(sources, sizes, moms, kept)]
        mom, made = add_fields(payload, parts, mom, columns if is_last else 0, False)
    (mom_sent,) = made[-1]
    mom_received = to_columns(mom_sent)
    moments, geometry, places, hot = call(
        functools.partial(geometry_kernel, slots),
        "contact_geometry",
        (
            shape(3, count),
            shape(len(contact_blocks(columns, slots)), 8, SUBS, LANES),
            shape(2, 3, columns, slot_len, dtype=jnp.int32),
            shape(LANES, 2 * columns * slot_len, dtype=BF16),
        ),
        table,
        listed,
        received,
        mom,
    )
    forces = call(
        functools.partial(force_kernel, slots),
        "contact_force",
        shape(3, count),
        geometry,
        places,
        hot,
        mom_received,
        scratch=[
            pltpu.VMEM((2, 9, columns, slot_len), F32),
            pltpu.VMEM((9 * groups, 2 * columns * slot_len), BF16),
        ],
    )
    return (moments, forces)


def solution(mesh):
    placed = (
        P(None, ("col", "row")),
        P(None, ("col", "row")),
        P(None, ("col", "row")),
        P(("col", "row")),
        P("col", "row", None, None),
        P("col", "row", None, None),
        P("col", "row", None),
    )
    return jax.shard_map(
        functools.partial(on_device, mesh.shape["row"]),
        mesh=mesh,
        in_specs=placed,
        out_specs=(P(None, ("col", "row")), P(None, ("col", "row"))),
        check_vma=False,
    )
```

```python
import functools
import math

import jax
import jax.numpy as jnp
from jax import lax
from jax.experimental import pallas as pl
from jax.experimental.pallas import tpu as pltpu
from jax.sharding import PartitionSpec as P

ITERS = 2
LANES = 128
SUBS = 8
FEATURES = 16
PAIR_ROWS = 48
KEEP_BYTES = 20 * 2**20
BLOCK = 512
WIDTH = 256
F32 = jnp.float32
BF16 = jnp.bfloat16
VMEM = pl.BlockSpec(memory_space=pltpu.VMEM)
HBM = pl.BlockSpec(memory_space=pltpu.HBM)


def split3(value):
    high = value.astype(BF16).astype(F32)
    rest = value - high
    middle = rest.astype(BF16).astype(F32)
    return high, middle, rest - middle


def norm_sq(pos):
    return pos[0] * pos[0] + pos[1] * pos[1] + pos[2] * pos[2]


def to_rows(vectors, held):
    for f, vector in enumerate(vectors):
        held[f] = vector
    return [held[0 : len(vectors), g, :] for g in range(held.shape[1])]


def put_pieces(rows, out, first, columns, order):
    for g, row in enumerate(rows):
        pieces = split3(row)
        lanes = slice(columns + g * LANES, columns + (g + 1) * LANES)
        out[first : first + len(order) * row.shape[0], lanes] = jnp.concatenate(
            [pieces[k] for k in order], axis=0
        ).astype(BF16)


def moment_rows(pos, mom, held, out, columns):
    outer = [mom[a] * pos[b] for a in range(3) for b in range(3)]
    along = outer[0] + outer[4] + outer[8]
    square = norm_sq(pos)
    mixed = [3.0 * along * pos[a] - square * mom[a] for a in range(3)]
    put_pieces(to_rows(list(mom) + outer + mixed + [along], held), out, 0, columns, (0, 1, 2))


TARGET_ORDER = (0, 1, 0, 1, 2, 0)
SOURCE_ORDER = (0, 0, 1, 1, 0, 2)


def target_rows(pos, held, out):
    one, zero = jnp.ones_like(pos[0]), jnp.zeros_like(pos[0])
    rows = list(pos) + [one, norm_sq(pos) + 1.0, zero, zero, zero]
    put_pieces(to_rows(rows, held), out, 0, 0, TARGET_ORDER)


def source_rows(pos, held, out, columns):
    one, zero = jnp.ones_like(pos[0]), jnp.zeros_like(pos[0])
    rows = [-2.0 * p for p in pos] + [norm_sq(pos), one, zero, zero, zero]
    put_pieces(to_rows(rows, held), out, 3 * FEATURES, columns, SOURCE_ORDER)


def field_from_sums(sums, held, pos, mom):
    groups = held.shape[1]
    for g in range(groups):
        lanes = slice(g * LANES, (g + 1) * LANES)
        held[0:FEATURES, g, :] = (
            sums[0:FEATURES, lanes]
            + sums[FEATURES : 2 * FEATURES, lanes]
            + sums[2 * FEATURES : 3 * FEATURES, lanes]
        )
    m = [held[a] for a in range(3)]
    outer = [[held[3 + 3 * a + b] for b in range(3)] for a in range(3)]
    trace = outer[0][0] + outer[1][1] + outer[2][2]
    scale_sq = norm_sq(pos) + 1.0
    along = m[0] * pos[0] + m[1] * pos[1] + m[2] * pos[2] - trace
    parts = []
    for a in range(3):
        by_column = outer[0][a] * pos[0] + outer[1][a] * pos[1] + outer[2][a] * pos[2]
        by_row = outer[a][0] * pos[0] + outer[a][1] * pos[1] + outer[a][2] * pos[2]
        parts.append(
            3.0 * (along * pos[a] - by_column)
            + 2.0 * by_row
            + held[12 + a]
            - scale_sq * m[a]
            + mom[a]
        )
    return parts


def pair_coefficient(radius_sq):
    inverse = lax.rsqrt(radius_sq)
    square = inverse * inverse
    fifth = square * square * inverse
    high = fifth.astype(BF16)
    return high, (fifth - high.astype(F32)).astype(BF16)


def vectors_of(ref, first, groups):
    return [ref[first + c * groups : first + (c + 1) * groups, :] for c in range(3)]


def about(pos, center):
    return [p - c for p, c in zip(pos, center)]


def field_kernel(sources, picks, with_mom, has_kept, has_before, is_last, columns, *refs):
    refs = list(refs)
    own = refs.pop(0)
    blocks = [ref.at[k] for ref in refs[:sources] for k in range(ref.shape[0])]
    blocks = [blocks[k] for k in picks]
    refs = refs[sources:]
    if with_mom:
        own_mom = refs.pop(0)
        mom_blocks = []
        while len(mom_blocks) < len(picks):
            mom_blocks += [refs[0].at[k] for k in range(refs[0].shape[0])]
            refs.pop(0)
    kept = (refs.pop(0), refs.pop(0)) if has_kept else None
    before = refs.pop(0) if has_before else None
    outs, (held, target, feats, sums) = refs[:-4], refs[-4:]
    made = outs[1:3] if len(outs) == 3 else None
    groups = held.shape[1]
    count = groups * LANES
    own_pos = vectors_of(own, 0, groups)
    center = [jnp.sum(p, keepdims=True) * (1.0 / count) for p in own_pos]
    pos = about(own_pos, center)
    if not has_kept:
        target_rows(pos, held, target)
    sums[...] = before[...] if has_before else jnp.zeros_like(sums)
    for k, there in enumerate(blocks):
        their_pos = about(vectors_of(there, 0, groups), center)
        if with_mom:
            their_mom = vectors_of(mom_blocks[k], 0, groups)
        else:
            chi = there[6 * groups : 7 * groups, :]
            their_mom = [chi * v for v in vectors_of(there, 3 * groups, groups)]
        moment_rows(their_pos, their_mom, held, feats, k * count)
        if not has_kept:
            source_rows(their_pos, held, feats, k * count)
    height, width = math.gcd(count, BLOCK), math.gcd(count, WIDTH)
    tiles = [
        (slice(a, a + height), slice(b, b + width))
        for a in range(0, len(blocks) * count, height)
        for b in range(0, count, width)
    ]

    def radius_of(tile):
        return lax.dot_general(
            feats[3 * FEATURES :, tile[0]],
            target[:, tile[1]],
            (((0,), (0,)), ((), ())),
            preferred_element_type=F32,
        )

    def add(tile, high, low):
        moments = feats[0 : 3 * FEATURES, tile[0]]
        sums[:, tile[1]] += jnp.dot(moments, high, preferred_element_type=F32) + jnp.dot(
            moments, low, preferred_element_type=F32
        )

    if has_kept:
        for a, b in tiles:
            k, at = divmod(a.start, count)
            rows = slice(picks[k] * count + at, picks[k] * count + at + height)
            add((a, b), kept[0][rows, b], kept[1][rows, b])
    else:
        radius_sq, ready = radius_of(tiles[0]), None
        for at, tile in enumerate(tiles):
            following = radius_of(tiles[at + 1]) if at + 1 < len(tiles) else None
            high, low = pair_coefficient(radius_sq)
            if made:
                made[0][tile] = high
                made[1][tile] = low
            if ready is not None:
                add(*ready)
            ready, radius_sq = (tile, high, low), following
        add(*ready)
    if not is_last:
        outs[0][...] = sums[...]
        return
    applied = vectors_of(own, 3 * groups, groups)
    chi = own[6 * groups : 7 * groups, :]
    own_now = vectors_of(own_mom, 0, groups) if with_mom else [chi * v for v in applied]
    field = field_from_sums(sums, held, pos, own_now)
    for a in range(3):
        result = chi * (applied[a] + field[a])
        rows = slice(a * groups, (a + 1) * groups)
        outs[0][rows, :] = result
        for e in range(columns):
            outs[1][e, rows, :] = result


def copy_in(inputs, held, done):
    copies = [
        pltpu.make_async_copy(src, dst, done.at[k]) for k, (src, dst) in enumerate(zip(inputs, held))
    ]
    for copy in copies:
        copy.start()
    for copy in copies:
        copy.wait()


def column_order(columns):
    return [(k + columns // 2) % columns for k in range(columns)]


def to_columns(blocks):
    return lax.all_to_all(
        blocks,
        "col",
        split_axis=0,
        concat_axis=0,
        axis_index_groups=[column_order(blocks.shape[0])],
        tiled=True,
    )


def row_pack_kernel(*refs):
    inputs, payload, held, (pos, field, chi, done) = refs[0:7], refs[7], refs[8:12], refs[12:]
    copy_in(inputs, (pos, field, chi, *held), done)
    groups = pos.shape[1] // LANES
    for g in range(groups):
        lanes = slice(g * LANES, (g + 1) * LANES)
        for c in range(3):
            payload[c * groups + g : c * groups + g + 1, :] = pos[c : c + 1, lanes]
            row = (3 + c) * groups + g
            payload[row : row + 1, :] = field[c : c + 1, lanes]
        payload[6 * groups + g : 6 * groups + g + 1, :] = chi[:, lanes]
    payload[7 * groups :, :] = jnp.zeros_like(payload[7 * groups :, :])


def column_pack_kernel(vel, owner, partner, counts, payload, send, table, listed):
    groups = vel.shape[1] // LANES
    slots = owner.shape[1] // LANES
    columns = owner.shape[0]
    table[0 : 3 * groups, :] = payload[0 : 3 * groups, :]
    for g in range(groups):
        for c in range(3):
            row = (3 + c) * groups + g
            table[row : row + 1, :] = vel[c : c + 1, g * LANES : (g + 1) * LANES]
    order = column_order(columns)
    tail = (send.shape[1] - 6 * groups - 2 * slots, LANES)
    for e in range(columns):
        send[e, 0 : 6 * groups, :] = table[...]
        live = jnp.broadcast_to(counts[:, order[e] : order[e] + 1], tail)
        send[e, 6 * groups + 2 * slots :, :] = live.astype(F32)
        listed[2 * slots, e : e + 1, :] = live[0:1]
    for q in range(slots):
        lanes = slice(q * LANES, (q + 1) * LANES)
        for k, ref in enumerate((owner, partner)):
            half = columns // 2
            index = jnp.concatenate([ref[half:, lanes], ref[:half, lanes]], axis=0)
            send[:, 6 * groups + k * slots + q, :] = index.astype(F32)
            listed[k * slots + q] = index


def split_index(index):
    return index & (LANES - 1), index >> (LANES.bit_length() - 1)


def look_up(tables, lane, bits):
    found = [jnp.take_along_axis(t, lane, axis=1, mode="promise_in_bounds") for t in tables]
    for bit in bits:
        found = [
            jnp.where(bit, found[k + 1], found[k]) if k + 1 < len(found) else found[k]
            for k in range(0, len(found), 2)
        ]
    return found[0]


def bits_of(group, groups):
    return [(group >> k) & 1 == 1 for k in range((groups - 1).bit_length())]


def own_tables(ref, first, groups):
    return [
        jnp.broadcast_to(ref[first + g : first + g + 1, :], (SUBS, LANES)) for g in range(groups)
    ]


def their_tables(ref, rows, first, groups):
    return [ref[rows, first + g, :] for g in range(groups)]


def slot_index(listed, received, kind, rows, q, groups, slots):
    if kind:
        first = 6 * groups + q
        owner, partner, count = (
            received[rows, row, :].astype(jnp.int32)
            for row in (first, first + slots, 6 * groups + 2 * slots)
        )
    else:
        owner, partner, count = (listed[row, rows, :] for row in (q, slots + q, 2 * slots))
    live = lax.broadcasted_iota(jnp.int32, (SUBS, LANES), 1) + q * LANES < count
    return (partner, owner, live) if kind else (owner, partner, live)


def contact_blocks(columns, slots):
    return [
        (kind, slice(first, first + SUBS), q)
        for kind in range(2)
        for first in range(0, columns, SUBS)
        for q in range(slots)
    ]


def geometry_kernel(slots, table, listed, received, mom, moments, out, places, hot):
    columns = received.shape[0]
    groups = mom.shape[0] // 3
    lane_of = lax.broadcasted_iota(jnp.int32, (LANES, LANES), 1).astype(F32)
    for c in range(3):
        for g in range(groups):
            lanes = slice(g * LANES, (g + 1) * LANES)
            moments[c : c + 1, lanes] = mom[c * groups + g : c * groups + g + 1, :]
    for at, (kind, rows, q) in enumerate(contact_blocks(columns, slots)):
        mine, other, live = slot_index(listed, received, kind, rows, q, groups, slots)
        lane, group = split_index(mine)
        bits = bits_of(group, groups)
        their_lane, their_group = split_index(other)
        their_bits = bits_of(their_group, groups)
        gap = []
        for c in range(6):
            gap.append(
                look_up(own_tables(table, c * groups, groups), lane, bits)
                - look_up(
                    their_tables(received, rows, c * groups, groups), their_lane, their_bits
                )
            )
        radius_sq = gap[0] * gap[0] + gap[1] * gap[1] + gap[2] * gap[2] + 1.0
        inverse = lax.rsqrt(radius_sq)
        normal = [jnp.where(live, gap[c] * inverse, 0.0) for c in range(3)]
        speed = gap[3] * normal[0] + gap[4] * normal[1] + gap[5] * normal[2]
        own = [look_up(own_tables(mom, c * groups, groups), lane, bits) for c in range(3)]
        for c in range(3):
            out[at, c] = normal[c]
            out[at, 3 + c] = own[c]
        out[at, 6] = -0.03 * (radius_sq * inverse - 1.0) - 0.5 * speed
        out[at, 7] = own[0] * normal[0] + own[1] * normal[1] + own[2] * normal[2]
        lanes = slice(q * LANES, (q + 1) * LANES)
        places[kind, 0, rows, lanes] = group
        places[kind, 1, rows, lanes] = other
        turned = jnp.transpose(lane.astype(F32))
        for s in range(SUBS):
            first = ((kind * columns + rows.start + s) * slots + q) * LANES
            here = turned[:, s : s + 1] == lane_of
            hot[first : first + LANES, :] = jnp.where(here, 1.0, 0.0).astype(BF16)


def force_kernel(slots, geometry, places, hot, mom_received, forces, pieces, values):
    columns = mom_received.shape[0]
    groups = mom_received.shape[1] // 3
    for at, (kind, rows, q) in enumerate(contact_blocks(columns, slots)):
        lanes = slice(q * LANES, (q + 1) * LANES)
        their_lane, their_group = split_index(places[kind, 1, rows, lanes])
        their_bits = bits_of(their_group, groups)
        normal = [geometry[at, c] for c in range(3)]
        own = [geometry[at, 3 + c] for c in range(3)]
        along_own = geometry[at, 7]
        their = [
            look_up(their_tables(mom_received, rows, c * groups, groups), their_lane, their_bits)
            for c in range(3)
        ]
        along_their = their[0] * normal[0] + their[1] * normal[1] + their[2] * normal[2]
        product = own[0] * their[0] + own[1] * their[1] + own[2] * their[2]
        radial = 3.0 * (product - 5.0 * along_own * along_their) + geometry[at, 6]
        for c in range(3):
            force = 3.0 * (along_own * their[c] + along_their * own[c]) + radial * normal[c]
            for k, piece in enumerate(split3(force)):
                pieces[kind, k * 3 + c, rows, lanes] = piece
    width = slots * LANES
    row_of = lax.broadcasted_iota(jnp.int32, (groups, width), 0)
    for kind in range(2):
        for e in range(columns):
            here = places[kind, 0, e : e + 1, :] == row_of
            first = (kind * columns + e) * width
            values[:, first : first + width] = jnp.concatenate(
                [jnp.where(here, pieces[kind, k, e : e + 1, :], 0.0) for k in range(9)], axis=0
            ).astype(BF16)
    total = jnp.dot(values[...], hot[...], preferred_element_type=F32)
    height = 3 * groups
    total = total[0:height] + total[height : 2 * height] + total[2 * height : 3 * height]
    for c in range(3):
        for g in range(groups):
            row = c * groups + g
            forces[c : c + 1, g * LANES : (g + 1) * LANES] = total[row : row + 1, :]


def call(kernel, name, outs, *args, specs=None, scratch=(), limit=24):
    many = isinstance(outs, tuple)
    return pl.pallas_call(
        kernel,
        out_shape=outs,
        in_specs=specs or [VMEM] * len(args),
        out_specs=tuple(VMEM for _ in outs) if many else VMEM,
        scratch_shapes=scratch,
        compiler_params=pltpu.CompilerParams(vmem_limit_bytes=limit * 2**20),
        name=name,
    )(*args)


def shape(*dims, dtype=F32):
    return jax.ShapeDtypeStruct(dims, dtype)


def flip(blocks, axis, size, bit):
    return lax.ppermute(blocks, axis, [(i, i ^ (1 << bit)) for i in range(size)])


def others(block, axis, size):
    return [lax.ppermute(block, axis, [(i, (i + k) % size) for i in range(size)])[None] for k in range(1, size)]


def exchange(block, axis, size, first=0):
    held, rounds = block[None], []
    for bit in range(first, size.bit_length() - 1):
        rounds.append(flip(held, axis, size, bit))
        if bit + 2 < size.bit_length():
            held = jnp.concatenate([held, rounds[-1]], axis=0)
    return rounds


def add_fields(payload, parts, mom, columns, keep):
    count = payload.shape[0] // SUBS * LANES
    groups = count // LANES
    sums, made = None, []
    for at, (sources, picks, moms, kept) in enumerate(parts):
        is_last = at == len(parts) - 1
        length = len(picks) * count
        args = [payload, *sources]
        if callable(moms):
            moms, sums = moms(sums)
        if mom is not None:
            args += [mom, *moms]
        args += kept
        if sums is not None:
            args.append(sums)
        if not is_last:
            outs = (shape(3 * FEATURES, count),)
        else:
            outs = (shape(3 * groups, LANES),)
            outs += (shape(columns, 3 * groups, LANES),) if columns else ()
        if keep:
            outs += (shape(length, count, dtype=BF16),) * 2
        sums, *now = call(
            functools.partial(
                field_kernel,
                len(sources),
                picks,
                mom is not None,
                bool(kept),
                sums is not None,
                is_last,
                columns,
            ),
            "field_sums",
            outs,
            *args,
            scratch=[
                pltpu.VMEM((FEATURES, groups, LANES), F32),
                pltpu.VMEM((PAIR_ROWS, count), BF16),
                pltpu.VMEM((3 * FEATURES + PAIR_ROWS, length), BF16),
                pltpu.VMEM((3 * FEATURES, count), F32),
            ],
        )
        made.append(now)
    return sums, made


def on_device(row_size, positions, velocity, applied, suscept, owner, partner, contact_count):
    count = positions.shape[1]
    columns, slot_len = owner.shape[2:]
    groups, slots = count // LANES, slot_len // LANES
    send_rows = 6 * groups + 2 * slots + 1
    send_rows += -send_rows % SUBS
    def in_hbm(*arrays):
        return [pltpu.with_memory_space_constraint(v, pltpu.HBM) for v in arrays]

    inputs = in_hbm(
        positions,
        applied,
        suscept.reshape(1, count),
        velocity,
        owner.reshape(columns, slot_len),
        partner.reshape(columns, slot_len),
        contact_count.reshape(1, columns),
    )
    payload, *held = call(
        row_pack_kernel,
        "row_pack",
        (shape(8 * groups, LANES),) + tuple(shape(*v.shape, dtype=v.dtype) for v in inputs[3:]),
        *inputs,
        specs=[HBM] * 7,
        scratch=[pltpu.VMEM(v.shape, v.dtype) for v in inputs[:3]]
        + [pltpu.SemaphoreType.DMA((7,))],
    )
    sent, table, listed = call(
        column_pack_kernel,
        "column_pack",
        (
            shape(columns, send_rows, LANES),
            shape(6 * groups, LANES),
            shape(2 * slots + 1, columns, LANES, dtype=jnp.int32),
        ),
        *held,
        payload,
    )
    paired = row_size > 1 and row_size & (row_size - 1) == 0
    rounds = (exchange if paired else others)(payload, "row", row_size)
    if rounds:
        first, sent = lax.optimization_barrier((rounds[0], sent))
        rounds = [first] + rounds[1:]
    received = to_columns(sent)
    keep = 4 * row_size * count * count <= KEEP_BYTES
    sources = [[payload[None]] + rounds[:1]] + [[r] for r in rounds[1:]]
    sizes = [sum(a.shape[0] for a in arrays) for arrays in sources]
    parts = [(a, tuple(range(n)), [], []) for a, n in zip(sources, sizes)]
    mom, kept = add_fields(payload, parts, None, 0, keep)
    for iteration in range(1, ITERS):
        is_last = iteration == ITERS - 1
        if paired:
            far = exchange(mom, "row", row_size, 1)
            moms = [[mom[None], flip(mom[None], "row", row_size, 0)]]
            parts = [(sources[0], (0, 1), moms[0], kept[0])]
            for k, direct in enumerate(far):
                evens, odds = tuple(range(0, sizes[k + 1], 2)), tuple(range(1, sizes[k + 1], 2))
                passed = []

                def handed_on(sums, direct=direct, passed=passed):
                    direct, sums = lax.optimization_barrier((direct, sums))
                    passed.append(flip(direct, "row", row_size, 0))
                    return [direct], sums

                parts.append((sources[k + 1], evens, handed_on, kept[k + 1]))
                parts.append((sources[k + 1], odds, lambda sums, p=passed: (p, sums), kept[k + 1]))
        else:
            moms = [[mom[None]] + others(mom, "row", row_size)[:1]]
            moms += [[r] for r in others(mom, "row", row_size)[1:]]
            parts = [(a, tuple(range(n)), m, k) for a, n, m, k in zip(sources, sizes, moms, kept)]
        mom, made = add_fields(payload, parts, mom, columns if is_last else 0, False)
    (mom_sent,) = made[-1]
    mom_received = to_columns(mom_sent)
    moments, geometry, places, hot = call(
        functools.partial(geometry_kernel, slots),
        "contact_geometry",
        (
            shape(3, count),
            shape(len(contact_blocks(columns, slots)), 8, SUBS, LANES),
            shape(2, 2, columns, slot_len, dtype=jnp.int32),
            shape(2 * columns * slot_len, LANES, dtype=BF16),
        ),
        table,
        listed,
        received,
        mom,
    )
    forces = call(
        functools.partial(force_kernel, slots),
        "contact_force",
        shape(3, count),
        geometry,
        places,
        hot,
        mom_received,
        scratch=[
            pltpu.VMEM((2, 9, columns, slot_len), F32),
            pltpu.VMEM((9 * groups, 2 * columns * slot_len), BF16),
        ],
    )
    return (moments, forces)


def solution(mesh):
    placed = (
        P(None, ("col", "row")),
        P(None, ("col", "row")),
        P(None, ("col", "row")),
        P(("col", "row")),
        P("col", "row", None, None),
        P("col", "row", None, None),
        P("col", "row", None),
    )
    return jax.shard_map(
        functools.partial(on_device, mesh.shape["row"]),
        mesh=mesh,
        in_specs=placed,
        out_specs=(P(None, ("col", "row")), P(None, ("col", "row"))),
        check_vma=False,
    )
```

```python
import functools
import math

import jax
import jax.numpy as jnp
from jax import lax
from jax.experimental import pallas as pl
from jax.experimental.pallas import tpu as pltpu
from jax.sharding import PartitionSpec as P

ITERS = 2
LANES = 128
SUBS = 8
FEATURES = 16
PAIR_ROWS = 48
KEEP_BYTES = 20 * 2**20
BLOCK = 512
WIDTH = 256
F32 = jnp.float32
BF16 = jnp.bfloat16
VMEM = pl.BlockSpec(memory_space=pltpu.VMEM)
HBM = pl.BlockSpec(memory_space=pltpu.HBM)


def split3(value):
    high = value.astype(BF16).astype(F32)
    rest = value - high
    middle = rest.astype(BF16).astype(F32)
    return high, middle, rest - middle


def norm_sq(pos):
    return pos[0] * pos[0] + pos[1] * pos[1] + pos[2] * pos[2]


def to_rows(vectors, held):
    for f, vector in enumerate(vectors):
        held[f] = vector
    return [held[0 : len(vectors), g, :] for g in range(held.shape[1])]


def put_pieces(rows, out, first, columns, order):
    for g, row in enumerate(rows):
        pieces = split3(row)
        lanes = slice(columns + g * LANES, columns + (g + 1) * LANES)
        out[first : first + len(order) * row.shape[0], lanes] = jnp.concatenate(
            [pieces[k] for k in order], axis=0
        ).astype(BF16)


def moment_rows(pos, mom, held, out, columns):
    outer = [mom[a] * pos[b] for a in range(3) for b in range(3)]
    along = outer[0] + outer[4] + outer[8]
    square = norm_sq(pos)
    mixed = [3.0 * along * pos[a] - square * mom[a] for a in range(3)]
    put_pieces(to_rows(list(mom) + outer + mixed + [along], held), out, 0, columns, (0, 1, 2))


TARGET_ORDER = (0, 1, 0, 1, 2, 0)
SOURCE_ORDER = (0, 0, 1, 1, 0, 2)


def target_rows(pos, held, out):
    one, zero = jnp.ones_like(pos[0]), jnp.zeros_like(pos[0])
    rows = list(pos) + [one, norm_sq(pos) + 1.0, zero, zero, zero]
    put_pieces(to_rows(rows, held), out, 0, 0, TARGET_ORDER)


def source_rows(pos, held, out, columns):
    one, zero = jnp.ones_like(pos[0]), jnp.zeros_like(pos[0])
    rows = [-2.0 * p for p in pos] + [norm_sq(pos), one, zero, zero, zero]
    put_pieces(to_rows(rows, held), out, 3 * FEATURES, columns, SOURCE_ORDER)


def field_from_sums(sums, held, pos, mom):
    groups = held.shape[1]
    for g in range(groups):
        lanes = slice(g * LANES, (g + 1) * LANES)
        held[0:FEATURES, g, :] = (
            sums[0:FEATURES, lanes]
            + sums[FEATURES : 2 * FEATURES, lanes]
            + sums[2 * FEATURES : 3 * FEATURES, lanes]
        )
    m = [held[a] for a in range(3)]
    outer = [[held[3 + 3 * a + b] for b in range(3)] for a in range(3)]
    trace = outer[0][0] + outer[1][1] + outer[2][2]
    scale_sq = norm_sq(pos) + 1.0
    along = m[0] * pos[0] + m[1] * pos[1] + m[2] * pos[2] - trace
    parts = []
    for a in range(3):
        by_column = outer[0][a] * pos[0] + outer[1][a] * pos[1] + outer[2][a] * pos[2]
        by_row = outer[a][0] * pos[0] + outer[a][1] * pos[1] + outer[a][2] * pos[2]
        parts.append(
            3.0 * (along * pos[a] - by_column)
            + 2.0 * by_row
            + held[12 + a]
            - scale_sq * m[a]
            + mom[a]
        )
    return parts


def pair_coefficient(radius_sq):
    inverse = lax.rsqrt(radius_sq)
    square = inverse * inverse
    fifth = square * square * inverse
    high = fifth.astype(BF16)
    return high, (fifth - high.astype(F32)).astype(BF16)


def vectors_of(ref, first, groups):
    return [ref[first + c * groups : first + (c + 1) * groups, :] for c in range(3)]


def about(pos, center):
    return [p - c for p, c in zip(pos, center)]


def field_kernel(sources, picks, with_mom, has_kept, has_before, is_last, columns, *refs):
    refs = list(refs)
    own = refs.pop(0)
    blocks = [ref.at[k] for ref in refs[:sources] for k in range(ref.shape[0])]
    blocks = [blocks[k] for k in picks]
    refs = refs[sources:]
    if with_mom:
        own_mom = refs.pop(0)
        mom_blocks = []
        while len(mom_blocks) < len(picks):
            mom_blocks += [refs[0].at[k] for k in range(refs[0].shape[0])]
            refs.pop(0)
    kept = (refs.pop(0), refs.pop(0)) if has_kept else None
    before = refs.pop(0) if has_before else None
    outs, (held, target, feats, sums) = refs[:-4], refs[-4:]
    made = outs[1:3] if len(outs) == 3 else None
    groups = held.shape[1]
    count = groups * LANES
    own_pos = vectors_of(own, 0, groups)
    center = [jnp.sum(p, keepdims=True) * (1.0 / count) for p in own_pos]
    pos = about(own_pos, center)
    if not has_kept:
        target_rows(pos, held, target)
    sums[...] = before[...] if has_before else jnp.zeros_like(sums)
    for k, there in enumerate(blocks):
        their_pos = about(vectors_of(there, 0, groups), center)
        if with_mom:
            their_mom = vectors_of(mom_blocks[k], 0, groups)
        else:
            chi = there[6 * groups : 7 * groups, :]
            their_mom = [chi * v for v in vectors_of(there, 3 * groups, groups)]
        moment_rows(their_pos, their_mom, held, feats, k * count)
        if not has_kept:
            source_rows(their_pos, held, feats, k * count)
    height, width = math.gcd(count, BLOCK), math.gcd(count, WIDTH)
    tiles = [
        (slice(a, a + height), slice(b, b + width))
        for a in range(0, len(blocks) * count, height)
        for b in range(0, count, width)
    ]

    def radius_of(tile):
        return lax.dot_general(
            feats[3 * FEATURES :, tile[0]],
            target[:, tile[1]],
            (((0,), (0,)), ((), ())),
            preferred_element_type=F32,
        )

    def add(tile, high, low):
        moments = feats[0 : 3 * FEATURES, tile[0]]
        sums[:, tile[1]] += jnp.dot(moments, high, preferred_element_type=F32) + jnp.dot(
            moments, low, preferred_element_type=F32
        )

    if has_kept:
        for a, b in tiles:
            k, at = divmod(a.start, count)
            rows = slice(picks[k] * count + at, picks[k] * count + at + height)
            add((a, b), kept[0][rows, b], kept[1][rows, b])
    else:
        radius_sq, ready = radius_of(tiles[0]), None
        for at, tile in enumerate(tiles):
            following = radius_of(tiles[at + 1]) if at + 1 < len(tiles) else None
            high, low = pair_coefficient(radius_sq)
            if made:
                made[0][tile] = high
                made[1][tile] = low
            if ready is not None:
                add(*ready)
            ready, radius_sq = (tile, high, low), following
        add(*ready)
    if not is_last:
        outs[0][...] = sums[...]
        return
    applied = vectors_of(own, 3 * groups, groups)
    chi = own[6 * groups : 7 * groups, :]
    own_now = vectors_of(own_mom, 0, groups) if with_mom else [chi * v for v in applied]
    field = field_from_sums(sums, held, pos, own_now)
    for a in range(3):
        result = chi * (applied[a] + field[a])
        rows = slice(a * groups, (a + 1) * groups)
        outs[0][rows, :] = result
        for e in range(columns):
            outs[1][e, rows, :] = result


def copy_in(inputs, held, done):
    copies = [
        pltpu.make_async_copy(src, dst, done.at[k]) for k, (src, dst) in enumerate(zip(inputs, held))
    ]
    for copy in copies:
        copy.start()
    for copy in copies:
        copy.wait()


def column_order(columns):
    first = (columns // 2 + 1) % columns
    return [first] + [k for k in range(columns) if k != first]


def to_columns(blocks):
    return lax.all_to_all(
        blocks,
        "col",
        split_axis=0,
        concat_axis=0,
        axis_index_groups=[column_order(blocks.shape[0])],
        tiled=True,
    )


def row_pack_kernel(*refs):
    inputs, payload, held, (pos, field, chi, done) = refs[0:7], refs[7], refs[8:12], refs[12:]
    copy_in(inputs, (pos, field, chi, *held), done)
    groups = pos.shape[1] // LANES
    for g in range(groups):
        lanes = slice(g * LANES, (g + 1) * LANES)
        for c in range(3):
            payload[c * groups + g : c * groups + g + 1, :] = pos[c : c + 1, lanes]
            row = (3 + c) * groups + g
            payload[row : row + 1, :] = field[c : c + 1, lanes]
        payload[6 * groups + g : 6 * groups + g + 1, :] = chi[:, lanes]
    payload[7 * groups :, :] = jnp.zeros_like(payload[7 * groups :, :])


def column_pack_kernel(vel, owner, partner, counts, payload, send, table, listed):
    groups = vel.shape[1] // LANES
    slots = owner.shape[1] // LANES
    columns = owner.shape[0]
    table[0 : 3 * groups, :] = payload[0 : 3 * groups, :]
    for g in range(groups):
        for c in range(3):
            row = (3 + c) * groups + g
            table[row : row + 1, :] = vel[c : c + 1, g * LANES : (g + 1) * LANES]
    order = column_order(columns)
    tail = (send.shape[1] - 6 * groups - 2 * slots, LANES)
    for e in range(columns):
        send[e, 0 : 6 * groups, :] = table[...]
        live = jnp.broadcast_to(counts[:, order[e] : order[e] + 1], tail)
        send[e, 6 * groups + 2 * slots :, :] = live.astype(F32)
        listed[2 * slots, e : e + 1, :] = live[0:1]
    for q in range(slots):
        lanes = slice(q * LANES, (q + 1) * LANES)
        for k, ref in enumerate((owner, partner)):
            index = jnp.concatenate([ref[e : e + 1, lanes] for e in order], axis=0)
            send[:, 6 * groups + k * slots + q, :] = index.astype(F32)
            listed[k * slots + q] = index


def split_index(index):
    return index & (LANES - 1), index >> (LANES.bit_length() - 1)


def look_up(tables, lane, bits):
    found = [jnp.take_along_axis(t, lane, axis=1, mode="promise_in_bounds") for t in tables]
    for bit in bits:
        found = [
            jnp.where(bit, found[k + 1], found[k]) if k + 1 < len(found) else found[k]
            for k in range(0, len(found), 2)
        ]
    return found[0]


def bits_of(group, groups):
    return [(group >> k) & 1 == 1 for k in range((groups - 1).bit_length())]


def own_tables(ref, first, groups):
    return [
        jnp.broadcast_to(ref[first + g : first + g + 1, :], (SUBS, LANES)) for g in range(groups)
    ]


def their_tables(ref, rows, first, groups):
    return [ref[rows, first + g, :] for g in range(groups)]


def slot_index(listed, received, kind, rows, q, groups, slots):
    if kind:
        first = 6 * groups + q
        owner, partner, count = (
            received[rows, row, :].astype(jnp.int32)
            for row in (first, first + slots, 6 * groups + 2 * slots)
        )
    else:
        owner, partner, count = (listed[row, rows, :] for row in (q, slots + q, 2 * slots))
    live = lax.broadcasted_iota(jnp.int32, (SUBS, LANES), 1) + q * LANES < count
    return (partner, owner, live) if kind else (owner, partner, live)


def contact_blocks(columns, slots):
    return [
        (kind, slice(first, first + SUBS), q)
        for kind in range(2)
        for first in range(0, columns, SUBS)
        for q in range(slots)
    ]


def geometry_kernel(slots, table, listed, received, mom, moments, out, places, hot):
    columns = received.shape[0]
    groups = mom.shape[0] // 3
    lane_of = lax.broadcasted_iota(jnp.int32, (LANES, LANES), 1).astype(F32)
    for c in range(3):
        for g in range(groups):
            lanes = slice(g * LANES, (g + 1) * LANES)
            moments[c : c + 1, lanes] = mom[c * groups + g : c * groups + g + 1, :]
    for at, (kind, rows, q) in enumerate(contact_blocks(columns, slots)):
        mine, other, live = slot_index(listed, received, kind, rows, q, groups, slots)
        lane, group = split_index(mine)
        bits = bits_of(group, groups)
        their_lane, their_group = split_index(other)
        their_bits = bits_of(their_group, groups)
        gap = []
        for c in range(6):
            gap.append(
                look_up(own_tables(table, c * groups, groups), lane, bits)
                - look_up(
                    their_tables(received, rows, c * groups, groups), their_lane, their_bits
                )
            )
        radius_sq = gap[0] * gap[0] + gap[1] * gap[1] + gap[2] * gap[2] + 1.0
        inverse = lax.rsqrt(radius_sq)
        normal = [jnp.where(live, gap[c] * inverse, 0.0) for c in range(3)]
        speed = gap[3] * normal[0] + gap[4] * normal[1] + gap[5] * normal[2]
        own = [look_up(own_tables(mom, c * groups, groups), lane, bits) for c in range(3)]
        for c in range(3):
            out[at, c] = normal[c]
            out[at, 3 + c] = own[c]
        out[at, 6] = -0.03 * (radius_sq * inverse - 1.0) - 0.5 * speed
        out[at, 7] = own[0] * normal[0] + own[1] * normal[1] + own[2] * normal[2]
        lanes = slice(q * LANES, (q + 1) * LANES)
        places[kind, 0, rows, lanes] = group
        places[kind, 1, rows, lanes] = other
        turned = jnp.transpose(lane.astype(F32))
        for s in range(SUBS):
            first = ((kind * columns + rows.start + s) * slots + q) * LANES
            here = turned[:, s : s + 1] == lane_of
            hot[first : first + LANES, :] = jnp.where(here, 1.0, 0.0).astype(BF16)


def force_kernel(slots, geometry, places, hot, mom_received, forces, pieces, values):
    columns = mom_received.shape[0]
    groups = mom_received.shape[1] // 3
    for at, (kind, rows, q) in enumerate(contact_blocks(columns, slots)):
        lanes = slice(q * LANES, (q + 1) * LANES)
        their_lane, their_group = split_index(places[kind, 1, rows, lanes])
        their_bits = bits_of(their_group, groups)
        normal = [geometry[at, c] for c in range(3)]
        own = [geometry[at, 3 + c] for c in range(3)]
        along_own = geometry[at, 7]
        their = [
            look_up(their_tables(mom_received, rows, c * groups, groups), their_lane, their_bits)
            for c in range(3)
        ]
        along_their = their[0] * normal[0] + their[1] * normal[1] + their[2] * normal[2]
        product = own[0] * their[0] + own[1] * their[1] + own[2] * their[2]
        radial = 3.0 * (product - 5.0 * along_own * along_their) + geometry[at, 6]
        for c in range(3):
            force = 3.0 * (along_own * their[c] + along_their * own[c]) + radial * normal[c]
            for k, piece in enumerate(split3(force)):
                pieces[kind, k * 3 + c, rows, lanes] = piece
    width = slots * LANES
    row_of = lax.broadcasted_iota(jnp.int32, (groups, width), 0)
    for kind in range(2):
        for e in range(columns):
            here = places[kind, 0, e : e + 1, :] == row_of
            first = (kind * columns + e) * width
            values[:, first : first + width] = jnp.concatenate(
                [jnp.where(here, pieces[kind, k, e : e + 1, :], 0.0) for k in range(9)], axis=0
            ).astype(BF16)
    total = jnp.dot(values[...], hot[...], preferred_element_type=F32)
    height = 3 * groups
    total = total[0:height] + total[height : 2 * height] + total[2 * height : 3 * height]
    for c in range(3):
        for g in range(groups):
            row = c * groups + g
            forces[c : c + 1, g * LANES : (g + 1) * LANES] = total[row : row + 1, :]


def call(kernel, name, outs, *args, specs=None, scratch=(), limit=24):
    many = isinstance(outs, tuple)
    return pl.pallas_call(
        kernel,
        out_shape=outs,
        in_specs=specs or [VMEM] * len(args),
        out_specs=tuple(VMEM for _ in outs) if many else VMEM,
        scratch_shapes=scratch,
        compiler_params=pltpu.CompilerParams(vmem_limit_bytes=limit * 2**20),
        name=name,
    )(*args)


def shape(*dims, dtype=F32):
    return jax.ShapeDtypeStruct(dims, dtype)


def flip(blocks, axis, size, bit):
    return lax.ppermute(blocks, axis, [(i, i ^ (1 << bit)) for i in range(size)])


def others(block, axis, size):
    return [lax.ppermute(block, axis, [(i, (i + k) % size) for i in range(size)])[None] for k in range(1, size)]


def exchange(block, axis, size, first=0):
    held, rounds = block[None], []
    for bit in range(first, size.bit_length() - 1):
        rounds.append(flip(held, axis, size, bit))
        if bit + 2 < size.bit_length():
            held = jnp.concatenate([held, rounds[-1]], axis=0)
    return rounds


def add_fields(payload, parts, mom, columns, keep):
    count = payload.shape[0] // SUBS * LANES
    groups = count // LANES
    sums, made = None, []
    for at, (sources, picks, moms, kept) in enumerate(parts):
        is_last = at == len(parts) - 1
        length = len(picks) * count
        args = [payload, *sources]
        if callable(moms):
            moms, sums = moms(sums)
        if mom is not None:
            args += [mom, *moms]
        args += kept
        if sums is not None:
            args.append(sums)
        if not is_last:
            outs = (shape(3 * FEATURES, count),)
        else:
            outs = (shape(3 * groups, LANES),)
            outs += (shape(columns, 3 * groups, LANES),) if columns else ()
        if keep:
            outs += (shape(length, count, dtype=BF16),) * 2
        sums, *now = call(
            functools.partial(
                field_kernel,
                len(sources),
                picks,
                mom is not None,
                bool(kept),
                sums is not None,
                is_last,
                columns,
            ),
            "field_sums",
            outs,
            *args,
            scratch=[
                pltpu.VMEM((FEATURES, groups, LANES), F32),
                pltpu.VMEM((PAIR_ROWS, count), BF16),
                pltpu.VMEM((3 * FEATURES + PAIR_ROWS, length), BF16),
                pltpu.VMEM((3 * FEATURES, count), F32),
            ],
        )
        made.append(now)
    return sums, made


def on_device(row_size, positions, velocity, applied, suscept, owner, partner, contact_count):
    count = positions.shape[1]
    columns, slot_len = owner.shape[2:]
    groups, slots = count // LANES, slot_len // LANES
    send_rows = 6 * groups + 2 * slots + 1
    send_rows += -send_rows % SUBS
    def in_hbm(*arrays):
        return [pltpu.with_memory_space_constraint(v, pltpu.HBM) for v in arrays]

    inputs = in_hbm(
        positions,
        applied,
        suscept.reshape(1, count),
        velocity,
        owner.reshape(columns, slot_len),
        partner.reshape(columns, slot_len),
        contact_count.reshape(1, columns),
    )
    payload, *held = call(
        row_pack_kernel,
        "row_pack",
        (shape(8 * groups, LANES),) + tuple(shape(*v.shape, dtype=v.dtype) for v in inputs[3:]),
        *inputs,
        specs=[HBM] * 7,
        scratch=[pltpu.VMEM(v.shape, v.dtype) for v in inputs[:3]]
        + [pltpu.SemaphoreType.DMA((7,))],
    )
    sent, table, listed = call(
        column_pack_kernel,
        "column_pack",
        (
            shape(columns, send_rows, LANES),
            shape(6 * groups, LANES),
            shape(2 * slots + 1, columns, LANES, dtype=jnp.int32),
        ),
        *held,
        payload,
    )
    paired = row_size > 1 and row_size & (row_size - 1) == 0
    rounds = (exchange if paired else others)(payload, "row", row_size)
    if rounds:
        first, sent = lax.optimization_barrier((rounds[0], sent))
        rounds = [first] + rounds[1:]
    received = to_columns(sent)
    keep = 4 * row_size * count * count <= KEEP_BYTES
    sources = [[payload[None]] + rounds[:1]] + [[r] for r in rounds[1:]]
    sizes = [sum(a.shape[0] for a in arrays) for arrays in sources]
    parts = [(a, tuple(range(n)), [], []) for a, n in zip(sources, sizes)]
    mom, kept = add_fields(payload, parts, None, 0, keep)
    for iteration in range(1, ITERS):
        is_last = iteration == ITERS - 1
        if paired:
            far = exchange(mom, "row", row_size, 1)
            moms = [[mom[None], flip(mom[None], "row", row_size, 0)]]
            parts = [(sources[0], (0, 1), moms[0], kept[0])]
            for k, direct in enumerate(far):
                evens, odds = tuple(range(0, sizes[k + 1], 2)), tuple(range(1, sizes[k + 1], 2))
                passed = []

                def handed_on(sums, direct=direct, passed=passed):
                    direct, sums = lax.optimization_barrier((direct, sums))
                    passed.append(flip(direct, "row", row_size, 0))
                    return [direct], sums

                parts.append((sources[k + 1], evens, handed_on, kept[k + 1]))
                parts.append((sources[k + 1], odds, lambda sums, p=passed: (p, sums), kept[k + 1]))
        else:
            moms = [[mom[None]] + others(mom, "row", row_size)[:1]]
            moms += [[r] for r in others(mom, "row", row_size)[1:]]
            parts = [(a, tuple(range(n)), m, k) for a, n, m, k in zip(sources, sizes, moms, kept)]
        mom, made = add_fields(payload, parts, mom, columns if is_last else 0, False)
    (mom_sent,) = made[-1]
    mom_received = to_columns(mom_sent)
    moments, geometry, places, hot = call(
        functools.partial(geometry_kernel, slots),
        "contact_geometry",
        (
            shape(3, count),
            shape(len(contact_blocks(columns, slots)), 8, SUBS, LANES),
            shape(2, 2, columns, slot_len, dtype=jnp.int32),
            shape(2 * columns * slot_len, LANES, dtype=BF16),
        ),
        table,
        listed,
        received,
        mom,
    )
    forces = call(
        functools.partial(force_kernel, slots),
        "contact_force",
        shape(3, count),
        geometry,
        places,
        hot,
        mom_received,
        scratch=[
            pltpu.VMEM((2, 9, columns, slot_len), F32),
            pltpu.VMEM((9 * groups, 2 * columns * slot_len), BF16),
        ],
    )
    return (moments, forces)


def solution(mesh):
    placed = (
        P(None, ("col", "row")),
        P(None, ("col", "row")),
        P(None, ("col", "row")),
        P(("col", "row")),
        P("col", "row", None, None),
        P("col", "row", None, None),
        P("col", "row", None),
    )
    return jax.shard_map(
        functools.partial(on_device, mesh.shape["row"]),
        mesh=mesh,
        in_specs=placed,
        out_specs=(P(None, ("col", "row")), P(None, ("col", "row"))),
        check_vma=False,
    )
```

```python
import functools
import math

import jax
import jax.numpy as jnp
from jax import lax
from jax.experimental import pallas as pl
from jax.experimental.pallas import tpu as pltpu
from jax.sharding import PartitionSpec as P

ITERS = 2
PIECES = 2
LANES = 128
SUBS = 8
FEATURES = 16
PAIR_ROWS = 48
KEEP_BYTES = 20 * 2**20
BLOCK = 512
WIDTH = 256
F32 = jnp.float32
BF16 = jnp.bfloat16
VMEM = pl.BlockSpec(memory_space=pltpu.VMEM)
HBM = pl.BlockSpec(memory_space=pltpu.HBM)


def split3(value):
    high = value.astype(BF16).astype(F32)
    rest = value - high
    middle = rest.astype(BF16).astype(F32)
    return high, middle, rest - middle


def norm_sq(pos):
    return pos[0] * pos[0] + pos[1] * pos[1] + pos[2] * pos[2]


def to_rows(vectors, held):
    for f, vector in enumerate(vectors):
        held[f] = vector
    return [held[0 : len(vectors), g, :] for g in range(held.shape[1])]


def put_pieces(rows, out, first, columns, order):
    for g, row in enumerate(rows):
        pieces = split3(row)
        lanes = slice(columns + g * LANES, columns + (g + 1) * LANES)
        out[first : first + len(order) * row.shape[0], lanes] = jnp.concatenate(
            [pieces[k] for k in order], axis=0
        ).astype(BF16)


def moment_rows(pos, mom, held, out, columns):
    outer = [mom[a] * pos[b] for a in range(3) for b in range(3)]
    along = outer[0] + outer[4] + outer[8]
    square = norm_sq(pos)
    mixed = [3.0 * along * pos[a] - square * mom[a] for a in range(3)]
    put_pieces(to_rows(list(mom) + outer + mixed + [along], held), out, 0, columns, (0, 1, 2))


TARGET_ORDER = (0, 1, 0, 1, 2, 0)
SOURCE_ORDER = (0, 0, 1, 1, 0, 2)


def target_rows(pos, held, out):
    one, zero = jnp.ones_like(pos[0]), jnp.zeros_like(pos[0])
    rows = list(pos) + [one, norm_sq(pos) + 1.0, zero, zero, zero]
    put_pieces(to_rows(rows, held), out, 0, 0, TARGET_ORDER)


def source_rows(pos, held, out, columns):
    one, zero = jnp.ones_like(pos[0]), jnp.zeros_like(pos[0])
    rows = [-2.0 * p for p in pos] + [norm_sq(pos), one, zero, zero, zero]
    put_pieces(to_rows(rows, held), out, 3 * FEATURES, columns, SOURCE_ORDER)


def field_from_sums(sums, held, pos, mom):
    groups = held.shape[1]
    for g in range(groups):
        lanes = slice(g * LANES, (g + 1) * LANES)
        held[0:FEATURES, g, :] = (
            sums[0:FEATURES, lanes]
            + sums[FEATURES : 2 * FEATURES, lanes]
            + sums[2 * FEATURES : 3 * FEATURES, lanes]
        )
    m = [held[a] for a in range(3)]
    outer = [[held[3 + 3 * a + b] for b in range(3)] for a in range(3)]
    trace = outer[0][0] + outer[1][1] + outer[2][2]
    scale_sq = norm_sq(pos) + 1.0
    along = m[0] * pos[0] + m[1] * pos[1] + m[2] * pos[2] - trace
    parts = []
    for a in range(3):
        by_column = outer[0][a] * pos[0] + outer[1][a] * pos[1] + outer[2][a] * pos[2]
        by_row = outer[a][0] * pos[0] + outer[a][1] * pos[1] + outer[a][2] * pos[2]
        parts.append(
            3.0 * (along * pos[a] - by_column)
            + 2.0 * by_row
            + held[12 + a]
            - scale_sq * m[a]
            + mom[a]
        )
    return parts


def pair_coefficient(radius_sq):
    inverse = lax.rsqrt(radius_sq)
    square = inverse * inverse
    fifth = square * square * inverse
    high = fifth.astype(BF16)
    return high, (fifth - high.astype(F32)).astype(BF16)


def vectors_of(ref, first, groups):
    return [ref[first + c * groups : first + (c + 1) * groups, :] for c in range(3)]


def about(pos, center):
    return [p - c for p, c in zip(pos, center)]


def field_kernel(sources, picks, with_mom, has_kept, has_before, is_last, columns, *refs):
    refs = list(refs)
    own = refs.pop(0)
    blocks = [ref.at[k] for ref in refs[:sources] for k in range(ref.shape[0])]
    blocks = [blocks[k] for k in picks]
    refs = refs[sources:]
    if with_mom:
        own_mom = refs.pop(0)
        mom_blocks = []
        while len(mom_blocks) < len(picks):
            mom_blocks += [refs[0].at[k] for k in range(refs[0].shape[0])]
            refs.pop(0)
    kept = (refs.pop(0), refs.pop(0)) if has_kept else None
    before = refs.pop(0) if has_before else None
    outs, (stages, target, feats, sums) = refs[:-4], refs[-4:]
    held = stages.at[0]
    made = outs[1:3] if len(outs) == 3 else None
    groups = held.shape[1]
    count = groups * LANES
    own_pos = vectors_of(own, 0, groups)
    center = [jnp.sum(p, keepdims=True) * (1.0 / count) for p in own_pos]
    pos = about(own_pos, center)
    if not has_kept:
        target_rows(pos, stages.at[1], target)
    sums[...] = before[...] if has_before else jnp.zeros_like(sums)

    def place(k):
        their_pos = about(vectors_of(blocks[k], 0, groups), center)
        source_rows(their_pos, stages.at[2 * k + 3], feats, k * count)

    def weigh(k):
        there = blocks[k]
        their_pos = about(vectors_of(there, 0, groups), center)
        if with_mom:
            their_mom = vectors_of(mom_blocks[k], 0, groups)
        else:
            chi = there[6 * groups : 7 * groups, :]
            their_mom = [chi * v for v in vectors_of(there, 3 * groups, groups)]
        moment_rows(their_pos, their_mom, stages.at[2 * k + 2], feats, k * count)

    height, width = math.gcd(count, BLOCK), math.gcd(count, WIDTH)
    tiles = [
        (slice(a, a + height), slice(b, b + width))
        for a in range(0, len(blocks) * count, height)
        for b in range(0, count, width)
    ]

    def radius_of(tile):
        return lax.dot_general(
            feats[3 * FEATURES :, tile[0]],
            target[:, tile[1]],
            (((0,), (0,)), ((), ())),
            preferred_element_type=F32,
        )

    def add(tile, high, low):
        moments = feats[0 : 3 * FEATURES, tile[0]]
        sums[:, tile[1]] += jnp.dot(moments, high, preferred_element_type=F32) + jnp.dot(
            moments, low, preferred_element_type=F32
        )

    each = len(tiles) // len(blocks)
    if has_kept:
        for k in range(len(blocks)):
            weigh(k)
        for a, b in tiles:
            k, at = divmod(a.start, count)
            rows = slice(picks[k] * count + at, picks[k] * count + at + height)
            add((a, b), kept[0][rows, b], kept[1][rows, b])
    else:
        place(0)
        radius_sq, ready = radius_of(tiles[0]), None
        weigh(0)
        for at, tile in enumerate(tiles):
            k, step = at // each + 1, at % each
            if k < len(blocks) and step == each // 4:
                place(k)
            if k < len(blocks) and step == each // 2:
                weigh(k)
            following = radius_of(tiles[at + 1]) if at + 1 < len(tiles) else None
            if ready is not None:
                add(*ready)
            high, low = pair_coefficient(radius_sq)
            if made:
                made[0][tile] = high
                made[1][tile] = low
            ready, radius_sq = (tile, high, low), following
        add(*ready)
    if not is_last:
        outs[0][...] = sums[...]
        return
    applied = vectors_of(own, 3 * groups, groups)
    chi = own[6 * groups : 7 * groups, :]
    own_now = vectors_of(own_mom, 0, groups) if with_mom else [chi * v for v in applied]
    field = field_from_sums(sums, held, pos, own_now)
    for a in range(3):
        result = chi * (applied[a] + field[a])
        rows = slice(a * groups, (a + 1) * groups)
        outs[0][rows, :] = result
        for e in range(columns):
            outs[1][e, rows, :] = result


def copy_in(inputs, held, done):
    copies = [
        pltpu.make_async_copy(src, dst, done.at[k]) for k, (src, dst) in enumerate(zip(inputs, held))
    ]
    for copy in copies:
        copy.start()
    for copy in copies:
        copy.wait()


def column_order(columns):
    first = (columns // 2 + 1) % columns
    return [first] + [k for k in range(columns) if k != first]


def to_columns(blocks):
    return lax.all_to_all(
        blocks,
        "col",
        split_axis=0,
        concat_axis=0,
        axis_index_groups=[column_order(blocks.shape[0])],
        tiled=True,
    )


def row_pack_kernel(*refs):
    inputs, payload, held, (pos, field, chi, done) = refs[0:7], refs[7], refs[8:12], refs[12:]
    copy_in(inputs, (pos, field, chi, *held), done)
    groups = pos.shape[1] // LANES
    for g in range(groups):
        lanes = slice(g * LANES, (g + 1) * LANES)
        for c in range(3):
            payload[c * groups + g : c * groups + g + 1, :] = pos[c : c + 1, lanes]
            row = (3 + c) * groups + g
            payload[row : row + 1, :] = field[c : c + 1, lanes]
        payload[6 * groups + g : 6 * groups + g + 1, :] = chi[:, lanes]
    payload[7 * groups :, :] = jnp.zeros_like(payload[7 * groups :, :])


def column_pack_kernel(vel, owner, partner, counts, payload, send, table, listed):
    groups = vel.shape[1] // LANES
    slots = owner.shape[1] // LANES
    columns = owner.shape[0]
    table[0 : 3 * groups, :] = payload[0 : 3 * groups, :]
    for g in range(groups):
        for c in range(3):
            row = (3 + c) * groups + g
            table[row : row + 1, :] = vel[c : c + 1, g * LANES : (g + 1) * LANES]
    order = column_order(columns)
    tail = (send.shape[1] - 6 * groups - 2 * slots, LANES)
    for e in range(columns):
        send[e, 0 : 6 * groups, :] = table[...]
        live = jnp.broadcast_to(counts[:, order[e] : order[e] + 1], tail)
        send[e, 6 * groups + 2 * slots :, :] = live.astype(F32)
        listed[2 * slots, e : e + 1, :] = live[0:1]
    for q in range(slots):
        lanes = slice(q * LANES, (q + 1) * LANES)
        for k, ref in enumerate((owner, partner)):
            index = jnp.concatenate([ref[e : e + 1, lanes] for e in order], axis=0)
            send[:, 6 * groups + k * slots + q, :] = index.astype(F32)
            listed[k * slots + q] = index


def split_index(index):
    return index & (LANES - 1), index >> (LANES.bit_length() - 1)


def look_up(tables, lane, bits):
    found = [jnp.take_along_axis(t, lane, axis=1, mode="promise_in_bounds") for t in tables]
    for bit in bits:
        found = [
            jnp.where(bit, found[k + 1], found[k]) if k + 1 < len(found) else found[k]
            for k in range(0, len(found), 2)
        ]
    return found[0]


def bits_of(group, groups):
    return [(group >> k) & 1 == 1 for k in range((groups - 1).bit_length())]


def own_tables(ref, first, groups):
    return [
        jnp.broadcast_to(ref[first + g : first + g + 1, :], (SUBS, LANES)) for g in range(groups)
    ]


def their_tables(ref, rows, first, groups):
    return [ref[rows, first + g, :] for g in range(groups)]


def slot_index(listed, received, kind, rows, q, groups, slots):
    if kind:
        first = 6 * groups + q
        owner, partner, count = (
            received[rows, row, :].astype(jnp.int32)
            for row in (first, first + slots, 6 * groups + 2 * slots)
        )
    else:
        owner, partner, count = (listed[row, rows, :] for row in (q, slots + q, 2 * slots))
    live = lax.broadcasted_iota(jnp.int32, (SUBS, LANES), 1) + q * LANES < count
    return (partner, owner, live) if kind else (owner, partner, live)


def contact_blocks(columns, slots):
    return [
        (kind, slice(first, first + SUBS), q)
        for kind in range(2)
        for first in range(0, columns, SUBS)
        for q in range(slots)
    ]


def geometry_kernel(slots, table, listed, received, mom, moments, out, places, hot):
    columns = received.shape[0]
    groups = mom.shape[0] // 3
    lane_of = lax.broadcasted_iota(jnp.int32, (LANES, LANES), 1).astype(F32)
    for c in range(3):
        for g in range(groups):
            lanes = slice(g * LANES, (g + 1) * LANES)
            moments[c : c + 1, lanes] = mom[c * groups + g : c * groups + g + 1, :]
    for at, (kind, rows, q) in enumerate(contact_blocks(columns, slots)):
        mine, other, live = slot_index(listed, received, kind, rows, q, groups, slots)
        lane, group = split_index(mine)
        bits = bits_of(group, groups)
        their_lane, their_group = split_index(other)
        their_bits = bits_of(their_group, groups)
        gap = []
        for c in range(6):
            gap.append(
                look_up(own_tables(table, c * groups, groups), lane, bits)
                - look_up(
                    their_tables(received, rows, c * groups, groups), their_lane, their_bits
                )
            )
        radius_sq = gap[0] * gap[0] + gap[1] * gap[1] + gap[2] * gap[2] + 1.0
        inverse = lax.rsqrt(radius_sq)
        normal = [jnp.where(live, gap[c] * inverse, 0.0) for c in range(3)]
        speed = gap[3] * normal[0] + gap[4] * normal[1] + gap[5] * normal[2]
        own = [look_up(own_tables(mom, c * groups, groups), lane, bits) for c in range(3)]
        for c in range(3):
            out[at, c] = normal[c]
            out[at, 3 + c] = own[c]
        out[at, 6] = -0.03 * (radius_sq * inverse - 1.0) - 0.5 * speed
        out[at, 7] = own[0] * normal[0] + own[1] * normal[1] + own[2] * normal[2]
        lanes = slice(q * LANES, (q + 1) * LANES)
        places[kind, 0, rows, lanes] = group
        places[kind, 1, rows, lanes] = other
        turned = jnp.transpose(lane.astype(F32))
        for s in range(SUBS):
            first = ((kind * columns + rows.start + s) * slots + q) * LANES
            here = turned[:, s : s + 1] == lane_of
            hot[first : first + LANES, :] = jnp.where(here, 1.0, 0.0).astype(BF16)


def force_kernel(slots, geometry, places, hot, mom_received, forces, pieces, values):
    columns = mom_received.shape[0]
    groups = mom_received.shape[1] // 3
    width = slots * LANES
    height = 3 * groups
    row_of = lax.broadcasted_iota(jnp.int32, (groups, width), 0)
    order = list(enumerate(contact_blocks(columns, slots)))
    total = None
    for first in range(0, len(order), slots):
        for at, (kind, rows, q) in order[first : first + slots]:
            lanes = slice(q * LANES, (q + 1) * LANES)
            their_lane, their_group = split_index(places[kind, 1, rows, lanes])
            their_bits = bits_of(their_group, groups)
            normal = [geometry[at, c] for c in range(3)]
            own = [geometry[at, 3 + c] for c in range(3)]
            along_own = geometry[at, 7]
            their = [
                look_up(their_tables(mom_received, rows, c * groups, groups), their_lane, their_bits)
                for c in range(3)
            ]
            along_their = their[0] * normal[0] + their[1] * normal[1] + their[2] * normal[2]
            product = own[0] * their[0] + own[1] * their[1] + own[2] * their[2]
            radial = 3.0 * (product - 5.0 * along_own * along_their) + geometry[at, 6]
            for c in range(3):
                force = 3.0 * (along_own * their[c] + along_their * own[c]) + radial * normal[c]
                for k, piece in enumerate(split3(force)[:PIECES]):
                    pieces[kind, k * 3 + c, rows, lanes] = piece
        for e in range(rows.start, rows.stop):
            here = places[kind, 0, e : e + 1, :] == row_of
            start = (kind * columns + e) * width
            values[:, start : start + width] = jnp.concatenate(
                [jnp.where(here, pieces[kind, k, e : e + 1, :], 0.0) for k in range(3 * PIECES)],
                axis=0,
            ).astype(BF16)
        span = slice((kind * columns + rows.start) * width, (kind * columns + rows.stop) * width)
        summed = jnp.dot(values[:, span], hot[span, :], preferred_element_type=F32)
        total = summed if total is None else total + summed
    total = sum(total[k * height : (k + 1) * height] for k in range(PIECES))
    for c in range(3):
        for g in range(groups):
            row = c * groups + g
            forces[c : c + 1, g * LANES : (g + 1) * LANES] = total[row : row + 1, :]


def call(kernel, name, outs, *args, specs=None, scratch=(), limit=24):
    many = isinstance(outs, tuple)
    return pl.pallas_call(
        kernel,
        out_shape=outs,
        in_specs=specs or [VMEM] * len(args),
        out_specs=tuple(VMEM for _ in outs) if many else VMEM,
        scratch_shapes=scratch,
        compiler_params=pltpu.CompilerParams(vmem_limit_bytes=limit * 2**20),
        name=name,
    )(*args)


def shape(*dims, dtype=F32):
    return jax.ShapeDtypeStruct(dims, dtype)


def flip(blocks, axis, size, bit):
    return lax.ppermute(blocks, axis, [(i, i ^ (1 << bit)) for i in range(size)])


def others(block, axis, size):
    return [lax.ppermute(block, axis, [(i, (i + k) % size) for i in range(size)])[None] for k in range(1, size)]


def exchange(block, axis, size, first=0):
    held, rounds = block[None], []
    for bit in range(first, size.bit_length() - 1):
        rounds.append(flip(held, axis, size, bit))
        if bit + 2 < size.bit_length():
            held = jnp.concatenate([held, rounds[-1]], axis=0)
    return rounds


def add_fields(payload, parts, mom, columns, keep):
    count = payload.shape[0] // SUBS * LANES
    groups = count // LANES
    sums, made = None, []
    for at, (sources, picks, moms, kept) in enumerate(parts):
        is_last = at == len(parts) - 1
        length = len(picks) * count
        args = [payload, *sources]
        if callable(moms):
            moms, sums = moms(sums)
        if mom is not None:
            args += [mom, *moms]
        args += kept
        if sums is not None:
            args.append(sums)
        if not is_last:
            outs = (shape(3 * FEATURES, count),)
        else:
            outs = (shape(3 * groups, LANES),)
            outs += (shape(columns, 3 * groups, LANES),) if columns else ()
        if keep:
            outs += (shape(length, count, dtype=BF16),) * 2
        sums, *now = call(
            functools.partial(
                field_kernel,
                len(sources),
                picks,
                mom is not None,
                bool(kept),
                sums is not None,
                is_last,
                columns,
            ),
            "field_sums",
            outs,
            *args,
            scratch=[
                pltpu.VMEM((2 * len(picks) + 2, FEATURES, groups, LANES), F32),
                pltpu.VMEM((PAIR_ROWS, count), BF16),
                pltpu.VMEM((3 * FEATURES + PAIR_ROWS, length), BF16),
                pltpu.VMEM((3 * FEATURES, count), F32),
            ],
        )
        made.append(now)
    return sums, made


def on_device(row_size, positions, velocity, applied, suscept, owner, partner, contact_count):
    count = positions.shape[1]
    columns, slot_len = owner.shape[2:]
    groups, slots = count // LANES, slot_len // LANES
    send_rows = 6 * groups + 2 * slots + 1
    send_rows += -send_rows % SUBS
    def in_hbm(*arrays):
        return [pltpu.with_memory_space_constraint(v, pltpu.HBM) for v in arrays]

    inputs = in_hbm(
        positions,
        applied,
        suscept.reshape(1, count),
        velocity,
        owner.reshape(columns, slot_len),
        partner.reshape(columns, slot_len),
        contact_count.reshape(1, columns),
    )
    payload, *held = call(
        row_pack_kernel,
        "row_pack",
        (shape(8 * groups, LANES),) + tuple(shape(*v.shape, dtype=v.dtype) for v in inputs[3:]),
        *inputs,
        specs=[HBM] * 7,
        scratch=[pltpu.VMEM(v.shape, v.dtype) for v in inputs[:3]]
        + [pltpu.SemaphoreType.DMA((7,))],
    )
    sent, table, listed = call(
        column_pack_kernel,
        "column_pack",
        (
            shape(columns, send_rows, LANES),
            shape(6 * groups, LANES),
            shape(2 * slots + 1, columns, LANES, dtype=jnp.int32),
        ),
        *held,
        payload,
    )
    paired = row_size > 1 and row_size & (row_size - 1) == 0
    rounds = (exchange if paired else others)(payload, "row", row_size)
    if rounds:
        first, sent = lax.optimization_barrier((rounds[0], sent))
        rounds = [first] + rounds[1:]
    received = to_columns(sent)
    keep = 4 * row_size * count * count <= KEEP_BYTES
    sources = [[payload[None]] + rounds[:1]] + [[r] for r in rounds[1:]]
    sizes = [sum(a.shape[0] for a in arrays) for arrays in sources]
    parts = [(a, tuple(range(n)), [], []) for a, n in zip(sources, sizes)]
    mom, kept = add_fields(payload, parts, None, 0, keep)
    for iteration in range(1, ITERS):
        is_last = iteration == ITERS - 1
        if paired:
            far = exchange(mom, "row", row_size, 1)
            moms = [[mom[None], flip(mom[None], "row", row_size, 0)]]
            parts = [(sources[0], (0, 1), moms[0], kept[0])]
            for k, direct in enumerate(far):
                evens, odds = tuple(range(0, sizes[k + 1], 2)), tuple(range(1, sizes[k + 1], 2))
                passed = []

                def handed_on(sums, direct=direct, passed=passed):
                    direct, sums = lax.optimization_barrier((direct, sums))
                    passed.append(flip(direct, "row", row_size, 0))
                    return [direct], sums

                parts.append((sources[k + 1], evens, handed_on, kept[k + 1]))
                parts.append((sources[k + 1], odds, lambda sums, p=passed: (p, sums), kept[k + 1]))
        else:
            moms = [[mom[None]] + others(mom, "row", row_size)[:1]]
            moms += [[r] for r in others(mom, "row", row_size)[1:]]
            parts = [(a, tuple(range(n)), m, k) for a, n, m, k in zip(sources, sizes, moms, kept)]
        mom, made = add_fields(payload, parts, mom, columns if is_last else 0, False)
    (mom_sent,) = made[-1]
    mom_received = to_columns(mom_sent)
    moments, geometry, places, hot = call(
        functools.partial(geometry_kernel, slots),
        "contact_geometry",
        (
            shape(3, count),
            shape(len(contact_blocks(columns, slots)), 8, SUBS, LANES),
            shape(2, 2, columns, slot_len, dtype=jnp.int32),
            shape(2 * columns * slot_len, LANES, dtype=BF16),
        ),
        table,
        listed,
        received,
        mom,
    )
    forces = call(
        functools.partial(force_kernel, slots),
        "contact_force",
        shape(3, count),
        geometry,
        places,
        hot,
        mom_received,
        scratch=[
            pltpu.VMEM((2, 3 * PIECES, columns, slot_len), F32),
            pltpu.VMEM((3 * PIECES * groups, 2 * columns * slot_len), BF16),
        ],
    )
    return (moments, forces)


def solution(mesh):
    placed = (
        P(None, ("col", "row")),
        P(None, ("col", "row")),
        P(None, ("col", "row")),
        P(("col", "row")),
        P("col", "row", None, None),
        P("col", "row", None, None),
        P("col", "row", None),
    )
    return jax.shard_map(
        functools.partial(on_device, mesh.shape["row"]),
        mesh=mesh,
        in_specs=placed,
        out_specs=(P(None, ("col", "row")), P(None, ("col", "row"))),
        check_vma=False,
    )
```

```python
import functools
import math

import jax
import jax.numpy as jnp
from jax import lax
from jax.experimental import pallas as pl
from jax.experimental.pallas import tpu as pltpu
from jax.sharding import PartitionSpec as P

ITERS = 2
PIECES = 2
LANES = 128
SUBS = 8
FEATURES = 16
PAIR_ROWS = 48
KEEP_BYTES = 20 * 2**20
BLOCK = 512
WIDTH = 256
F32 = jnp.float32
BF16 = jnp.bfloat16
VMEM = pl.BlockSpec(memory_space=pltpu.VMEM)
HBM = pl.BlockSpec(memory_space=pltpu.HBM)


def split3(value):
    high = value.astype(BF16).astype(F32)
    rest = value - high
    middle = rest.astype(BF16).astype(F32)
    return high, middle, rest - middle


def norm_sq(pos):
    return pos[0] * pos[0] + pos[1] * pos[1] + pos[2] * pos[2]


def to_rows(vectors, held):
    for f, vector in enumerate(vectors):
        held[f] = vector
    return [held[0 : len(vectors), g, :] for g in range(held.shape[1])]


def put_pieces(rows, out, first, columns, order):
    for g, row in enumerate(rows):
        pieces = split3(row)
        lanes = slice(columns + g * LANES, columns + (g + 1) * LANES)
        out[first : first + len(order) * row.shape[0], lanes] = jnp.concatenate(
            [pieces[k] for k in order], axis=0
        ).astype(BF16)


def moment_rows(pos, mom, held, out, columns):
    outer = [mom[a] * pos[b] for a in range(3) for b in range(3)]
    along = outer[0] + outer[4] + outer[8]
    square = norm_sq(pos)
    mixed = [3.0 * along * pos[a] - square * mom[a] for a in range(3)]
    put_pieces(to_rows(list(mom) + outer + mixed + [along], held), out, 0, columns, (0, 1, 2))


TARGET_ORDER = (0, 1, 0, 1, 2, 0)
SOURCE_ORDER = (0, 0, 1, 1, 0, 2)


def target_rows(pos, held, out):
    one, zero = jnp.ones_like(pos[0]), jnp.zeros_like(pos[0])
    rows = list(pos) + [one, norm_sq(pos) + 1.0, zero, zero, zero]
    put_pieces(to_rows(rows, held), out, 0, 0, TARGET_ORDER)


def source_rows(pos, held, out, columns):
    one, zero = jnp.ones_like(pos[0]), jnp.zeros_like(pos[0])
    rows = [-2.0 * p for p in pos] + [norm_sq(pos), one, zero, zero, zero]
    put_pieces(to_rows(rows, held), out, 3 * FEATURES, columns, SOURCE_ORDER)


def field_from_sums(sums, held, pos, mom):
    groups = held.shape[1]
    for g in range(groups):
        lanes = slice(g * LANES, (g + 1) * LANES)
        held[0:FEATURES, g, :] = (
            sums[0:FEATURES, lanes]
            + sums[FEATURES : 2 * FEATURES, lanes]
            + sums[2 * FEATURES : 3 * FEATURES, lanes]
        )
    m = [held[a] for a in range(3)]
    outer = [[held[3 + 3 * a + b] for b in range(3)] for a in range(3)]
    trace = outer[0][0] + outer[1][1] + outer[2][2]
    scale_sq = norm_sq(pos) + 1.0
    along = m[0] * pos[0] + m[1] * pos[1] + m[2] * pos[2] - trace
    parts = []
    for a in range(3):
        by_column = outer[0][a] * pos[0] + outer[1][a] * pos[1] + outer[2][a] * pos[2]
        by_row = outer[a][0] * pos[0] + outer[a][1] * pos[1] + outer[a][2] * pos[2]
        parts.append(
            3.0 * (along * pos[a] - by_column)
            + 2.0 * by_row
            + held[12 + a]
            - scale_sq * m[a]
            + mom[a]
        )
    return parts


def pair_coefficient(radius_sq):
    inverse = lax.rsqrt(radius_sq)
    square = inverse * inverse
    fifth = square * square * inverse
    high = fifth.astype(BF16)
    return high, (fifth - high.astype(F32)).astype(BF16)


def vectors_of(ref, first, groups):
    return [ref[first + c * groups : first + (c + 1) * groups, :] for c in range(3)]


def about(pos, center):
    return [p - c for p, c in zip(pos, center)]


def field_kernel(sources, picks, with_mom, has_kept, has_before, is_last, columns, *refs):
    refs = list(refs)
    own = refs.pop(0)
    blocks = [ref.at[k] for ref in refs[:sources] for k in range(ref.shape[0])]
    blocks = [blocks[k] for k in picks]
    refs = refs[sources:]
    if with_mom:
        own_mom = refs.pop(0)
        mom_blocks = []
        while len(mom_blocks) < len(picks):
            mom_blocks += [refs[0].at[k] for k in range(refs[0].shape[0])]
            refs.pop(0)
    kept = (refs.pop(0), refs.pop(0)) if has_kept else None
    before = refs.pop(0) if has_before else None
    outs, (stages, target, feats, sums) = refs[:-4], refs[-4:]
    held = stages.at[0]
    made = outs[1:3] if len(outs) == 3 else None
    groups = held.shape[1]
    count = groups * LANES
    own_pos = vectors_of(own, 0, groups)
    center = [jnp.sum(p, keepdims=True) * (1.0 / count) for p in own_pos]
    pos = about(own_pos, center)
    if not has_kept:
        target_rows(pos, stages.at[1], target)
    sums[...] = before[...] if has_before else jnp.zeros_like(sums)

    def place(k):
        their_pos = about(vectors_of(blocks[k], 0, groups), center)
        source_rows(their_pos, stages.at[2 * k + 3], feats, k * count)

    def weigh(k):
        there = blocks[k]
        their_pos = about(vectors_of(there, 0, groups), center)
        if with_mom:
            their_mom = vectors_of(mom_blocks[k], 0, groups)
        else:
            chi = there[6 * groups : 7 * groups, :]
            their_mom = [chi * v for v in vectors_of(there, 3 * groups, groups)]
        moment_rows(their_pos, their_mom, stages.at[2 * k + 2], feats, k * count)

    height, width = math.gcd(count, BLOCK), math.gcd(count, WIDTH)
    tiles = [
        (slice(a, a + height), slice(b, b + width))
        for a in range(0, len(blocks) * count, height)
        for b in range(0, count, width)
    ]

    def radius_of(tile):
        return lax.dot_general(
            feats[3 * FEATURES :, tile[0]],
            target[:, tile[1]],
            (((0,), (0,)), ((), ())),
            preferred_element_type=F32,
        )

    def add(tile, high, low):
        moments = feats[0 : 3 * FEATURES, tile[0]]
        sums[:, tile[1]] += jnp.dot(moments, high, preferred_element_type=F32) + jnp.dot(
            moments, low, preferred_element_type=F32
        )

    each = len(tiles) // len(blocks)
    if has_kept:
        for k in range(len(blocks)):
            weigh(k)
        for a, b in tiles:
            k, at = divmod(a.start, count)
            rows = slice(picks[k] * count + at, picks[k] * count + at + height)
            add((a, b), kept[0][rows, b], kept[1][rows, b])
    else:
        place(0)
        radius_sq, ready = radius_of(tiles[0]), None
        weigh(0)
        for at, tile in enumerate(tiles):
            k, step = at // each + 1, at % each
            if k < len(blocks) and step == each // 4:
                place(k)
            if k < len(blocks) and step == each // 2:
                weigh(k)
            following = radius_of(tiles[at + 1]) if at + 1 < len(tiles) else None
            if ready is not None:
                add(*ready)
            high, low = pair_coefficient(radius_sq)
            if made:
                made[0][tile] = high
                made[1][tile] = low
            ready, radius_sq = (tile, high, low), following
        add(*ready)
    if not is_last:
        outs[0][...] = sums[...]
        return
    applied = vectors_of(own, 3 * groups, groups)
    chi = own[6 * groups : 7 * groups, :]
    own_now = vectors_of(own_mom, 0, groups) if with_mom else [chi * v for v in applied]
    field = field_from_sums(sums, held, pos, own_now)
    for a in range(3):
        result = chi * (applied[a] + field[a])
        rows = slice(a * groups, (a + 1) * groups)
        outs[0][rows, :] = result
        for e in range(columns):
            outs[1][e, rows, :] = result


def copy_in(inputs, held, done):
    copies = [
        pltpu.make_async_copy(src, dst, done.at[k]) for k, (src, dst) in enumerate(zip(inputs, held))
    ]
    for copy in copies:
        copy.start()
    return copies


def column_order(columns):
    first = (columns // 2 + 1) % columns
    return [first] + [k for k in range(columns) if k != first]


def to_columns(blocks):
    return lax.all_to_all(
        blocks,
        "col",
        split_axis=0,
        concat_axis=0,
        axis_index_groups=[column_order(blocks.shape[0])],
        tiled=True,
    )


def row_pack_kernel(*refs):
    inputs, payload, held, (pos, field, chi, done) = refs[0:7], refs[7], refs[8:12], refs[12:]
    copies = copy_in(inputs, (pos, field, chi, *held), done)
    for copy in copies[:3]:
        copy.wait()
    groups = pos.shape[1] // LANES
    for g in range(groups):
        lanes = slice(g * LANES, (g + 1) * LANES)
        for c in range(3):
            payload[c * groups + g : c * groups + g + 1, :] = pos[c : c + 1, lanes]
            row = (3 + c) * groups + g
            payload[row : row + 1, :] = field[c : c + 1, lanes]
        payload[6 * groups + g : 6 * groups + g + 1, :] = chi[:, lanes]
    payload[7 * groups :, :] = jnp.zeros_like(payload[7 * groups :, :])
    for copy in copies[3:]:
        copy.wait()


def column_pack_kernel(vel, owner, partner, counts, payload, send, table, listed):
    groups = vel.shape[1] // LANES
    slots = owner.shape[1] // LANES
    columns = owner.shape[0]
    table[0 : 3 * groups, :] = payload[0 : 3 * groups, :]
    for g in range(groups):
        for c in range(3):
            row = (3 + c) * groups + g
            table[row : row + 1, :] = vel[c : c + 1, g * LANES : (g + 1) * LANES]
    order = column_order(columns)
    tail = (send.shape[1] - 6 * groups - 2 * slots, LANES)
    for e in range(columns):
        send[e, 0 : 6 * groups, :] = table[...]
        live = jnp.broadcast_to(counts[:, order[e] : order[e] + 1], tail)
        send[e, 6 * groups + 2 * slots :, :] = live.astype(F32)
        listed[2 * slots, e : e + 1, :] = live[0:1]
    for q in range(slots):
        lanes = slice(q * LANES, (q + 1) * LANES)
        for k, ref in enumerate((owner, partner)):
            index = jnp.concatenate([ref[e : e + 1, lanes] for e in order], axis=0)
            send[:, 6 * groups + k * slots + q, :] = index.astype(F32)
            listed[k * slots + q] = index


def split_index(index):
    return index & (LANES - 1), index >> (LANES.bit_length() - 1)


def look_up(tables, lane, bits):
    found = [jnp.take_along_axis(t, lane, axis=1, mode="promise_in_bounds") for t in tables]
    for bit in bits:
        found = [
            jnp.where(bit, found[k + 1], found[k]) if k + 1 < len(found) else found[k]
            for k in range(0, len(found), 2)
        ]
    return found[0]


def bits_of(group, groups):
    return [(group >> k) & 1 == 1 for k in range((groups - 1).bit_length())]


def own_tables(ref, first, groups):
    return [
        jnp.broadcast_to(ref[first + g : first + g + 1, :], (SUBS, LANES)) for g in range(groups)
    ]


def their_tables(ref, rows, first, groups):
    return [ref[rows, first + g, :] for g in range(groups)]


def slot_index(listed, received, kind, rows, q, groups, slots):
    if kind:
        first = 6 * groups + q
        owner, partner, count = (
            received[rows, row, :].astype(jnp.int32)
            for row in (first, first + slots, 6 * groups + 2 * slots)
        )
    else:
        owner, partner, count = (listed[row, rows, :] for row in (q, slots + q, 2 * slots))
    live = lax.broadcasted_iota(jnp.int32, (SUBS, LANES), 1) + q * LANES < count
    return (partner, owner, live) if kind else (owner, partner, live)


def contact_blocks(columns, slots):
    return [
        (kind, slice(first, first + SUBS), q)
        for kind in range(2)
        for first in range(0, columns, SUBS)
        for q in range(slots)
    ]


def geometry_kernel(slots, table, listed, received, mom, moments, out, places, hot):
    columns = received.shape[0]
    groups = mom.shape[0] // 3
    lane_of = lax.broadcasted_iota(jnp.int32, (LANES, LANES), 1).astype(F32)
    for c in range(3):
        for g in range(groups):
            lanes = slice(g * LANES, (g + 1) * LANES)
            moments[c : c + 1, lanes] = mom[c * groups + g : c * groups + g + 1, :]
    for at, (kind, rows, q) in enumerate(contact_blocks(columns, slots)):
        mine, other, live = slot_index(listed, received, kind, rows, q, groups, slots)
        lane, group = split_index(mine)
        bits = bits_of(group, groups)
        their_lane, their_group = split_index(other)
        their_bits = bits_of(their_group, groups)
        gap = []
        for c in range(6):
            gap.append(
                look_up(own_tables(table, c * groups, groups), lane, bits)
                - look_up(
                    their_tables(received, rows, c * groups, groups), their_lane, their_bits
                )
            )
        radius_sq = gap[0] * gap[0] + gap[1] * gap[1] + gap[2] * gap[2] + 1.0
        inverse = lax.rsqrt(radius_sq)
        normal = [jnp.where(live, gap[c] * inverse, 0.0) for c in range(3)]
        speed = gap[3] * normal[0] + gap[4] * normal[1] + gap[5] * normal[2]
        own = [look_up(own_tables(mom, c * groups, groups), lane, bits) for c in range(3)]
        for c in range(3):
            out[at, c] = normal[c]
            out[at, 3 + c] = own[c]
        out[at, 6] = -0.03 * (radius_sq * inverse - 1.0) - 0.5 * speed
        out[at, 7] = own[0] * normal[0] + own[1] * normal[1] + own[2] * normal[2]
        lanes = slice(q * LANES, (q + 1) * LANES)
        places[kind, 0, rows, lanes] = group
        places[kind, 1, rows, lanes] = other
        turned = jnp.transpose(lane.astype(F32))
        for s in range(SUBS):
            first = ((kind * columns + rows.start + s) * slots + q) * LANES
            here = turned[:, s : s + 1] == lane_of
            hot[first : first + LANES, :] = jnp.where(here, 1.0, 0.0).astype(BF16)


def force_kernel(slots, geometry, places, hot, mom_received, forces, pieces, values):
    columns = mom_received.shape[0]
    groups = mom_received.shape[1] // 3
    width = slots * LANES
    height = 3 * groups
    row_of = lax.broadcasted_iota(jnp.int32, (groups, width), 0)
    order = list(enumerate(contact_blocks(columns, slots)))
    total = None
    for first in range(0, len(order), slots):
        for at, (kind, rows, q) in order[first : first + slots]:
            lanes = slice(q * LANES, (q + 1) * LANES)
            their_lane, their_group = split_index(places[kind, 1, rows, lanes])
            their_bits = bits_of(their_group, groups)
            normal = [geometry[at, c] for c in range(3)]
            own = [geometry[at, 3 + c] for c in range(3)]
            along_own = geometry[at, 7]
            their = [
                look_up(their_tables(mom_received, rows, c * groups, groups), their_lane, their_bits)
                for c in range(3)
            ]
            along_their = their[0] * normal[0] + their[1] * normal[1] + their[2] * normal[2]
            product = own[0] * their[0] + own[1] * their[1] + own[2] * their[2]
            radial = 3.0 * (product - 5.0 * along_own * along_their) + geometry[at, 6]
            for c in range(3):
                force = 3.0 * (along_own * their[c] + along_their * own[c]) + radial * normal[c]
                for k, piece in enumerate(split3(force)[:PIECES]):
                    pieces[kind, k * 3 + c, rows, lanes] = piece
        for e in range(rows.start, rows.stop):
            here = places[kind, 0, e : e + 1, :] == row_of
            start = (kind * columns + e) * width
            values[:, start : start + width] = jnp.concatenate(
                [jnp.where(here, pieces[kind, k, e : e + 1, :], 0.0) for k in range(3 * PIECES)],
                axis=0,
            ).astype(BF16)
        span = slice((kind * columns + rows.start) * width, (kind * columns + rows.stop) * width)
        summed = jnp.dot(values[:, span], hot[span, :], preferred_element_type=F32)
        total = summed if total is None else total + summed
    total = sum(total[k * height : (k + 1) * height] for k in range(PIECES))
    for c in range(3):
        for g in range(groups):
            row = c * groups + g
            forces[c : c + 1, g * LANES : (g + 1) * LANES] = total[row : row + 1, :]


def call(kernel, name, outs, *args, specs=None, scratch=(), limit=24):
    many = isinstance(outs, tuple)
    return pl.pallas_call(
        kernel,
        out_shape=outs,
        in_specs=specs or [VMEM] * len(args),
        out_specs=tuple(VMEM for _ in outs) if many else VMEM,
        scratch_shapes=scratch,
        compiler_params=pltpu.CompilerParams(vmem_limit_bytes=limit * 2**20),
        name=name,
    )(*args)


def shape(*dims, dtype=F32):
    return jax.ShapeDtypeStruct(dims, dtype)


def flip(blocks, axis, size, bit):
    return lax.ppermute(blocks, axis, [(i, i ^ (1 << bit)) for i in range(size)])


def others(block, axis, size):
    return [lax.ppermute(block, axis, [(i, (i + k) % size) for i in range(size)])[None] for k in range(1, size)]


def exchange(block, axis, size, first=0):
    held, rounds = block[None], []
    for bit in range(first, size.bit_length() - 1):
        rounds.append(flip(held, axis, size, bit))
        if bit + 2 < size.bit_length():
            held = jnp.concatenate([held, rounds[-1]], axis=0)
    return rounds


def add_fields(payload, parts, mom, columns, keep):
    count = payload.shape[0] // SUBS * LANES
    groups = count // LANES
    sums, made = None, []
    for at, (sources, picks, moms, kept) in enumerate(parts):
        is_last = at == len(parts) - 1
        length = len(picks) * count
        args = [payload, *sources]
        if callable(moms):
            moms, sums = moms(sums)
        if mom is not None:
            args += [mom, *moms]
        args += kept
        if sums is not None:
            args.append(sums)
        if not is_last:
            outs = (shape(3 * FEATURES, count),)
        else:
            outs = (shape(3 * groups, LANES),)
            outs += (shape(columns, 3 * groups, LANES),) if columns else ()
        if keep:
            outs += (shape(length, count, dtype=BF16),) * 2
        sums, *now = call(
            functools.partial(
                field_kernel,
                len(sources),
                picks,
                mom is not None,
                bool(kept),
                sums is not None,
                is_last,
                columns,
            ),
            "field_sums",
            outs,
            *args,
            scratch=[
                pltpu.VMEM((2 * len(picks) + 2, FEATURES, groups, LANES), F32),
                pltpu.VMEM((PAIR_ROWS, count), BF16),
                pltpu.VMEM((3 * FEATURES + PAIR_ROWS, length), BF16),
                pltpu.VMEM((3 * FEATURES, count), F32),
            ],
        )
        made.append(now)
    return sums, made


def on_device(row_size, positions, velocity, applied, suscept, owner, partner, contact_count):
    count = positions.shape[1]
    columns, slot_len = owner.shape[2:]
    groups, slots = count // LANES, slot_len // LANES
    send_rows = 6 * groups + 2 * slots + 1
    send_rows += -send_rows % SUBS
    def in_hbm(*arrays):
        return [pltpu.with_memory_space_constraint(v, pltpu.HBM) for v in arrays]

    inputs = in_hbm(
        positions,
        applied,
        suscept.reshape(1, count),
        velocity,
        owner.reshape(columns, slot_len),
        partner.reshape(columns, slot_len),
        contact_count.reshape(1, columns),
    )
    payload, *held = call(
        row_pack_kernel,
        "row_pack",
        (shape(8 * groups, LANES),) + tuple(shape(*v.shape, dtype=v.dtype) for v in inputs[3:]),
        *inputs,
        specs=[HBM] * 7,
        scratch=[pltpu.VMEM(v.shape, v.dtype) for v in inputs[:3]]
        + [pltpu.SemaphoreType.DMA((7,))],
    )
    sent, table, listed = call(
        column_pack_kernel,
        "column_pack",
        (
            shape(columns, send_rows, LANES),
            shape(6 * groups, LANES),
            shape(2 * slots + 1, columns, LANES, dtype=jnp.int32),
        ),
        *held,
        payload,
    )
    paired = row_size > 1 and row_size & (row_size - 1) == 0
    rounds = (exchange if paired else others)(payload, "row", row_size)
    if rounds:
        first, sent = lax.optimization_barrier((rounds[0], sent))
        rounds = [first] + rounds[1:]
    received = to_columns(sent)
    keep = 4 * row_size * count * count <= KEEP_BYTES
    sources = [[payload[None]] + rounds[:1]] + [[r] for r in rounds[1:]]
    sizes = [sum(a.shape[0] for a in arrays) for arrays in sources]
    parts = [(a, tuple(range(n)), [], []) for a, n in zip(sources, sizes)]
    mom, kept = add_fields(payload, parts, None, 0, keep)
    for iteration in range(1, ITERS):
        is_last = iteration == ITERS - 1
        if paired:
            far = exchange(mom, "row", row_size, 1)
            moms = [[mom[None], flip(mom[None], "row", row_size, 0)]]
            parts = [(sources[0], (0, 1), moms[0], kept[0])]
            for k, direct in enumerate(far):
                evens, odds = tuple(range(0, sizes[k + 1], 2)), tuple(range(1, sizes[k + 1], 2))
                passed = []

                def handed_on(sums, direct=direct, passed=passed):
                    direct, sums = lax.optimization_barrier((direct, sums))
                    passed.append(flip(direct, "row", row_size, 0))
                    return [direct], sums

                parts.append((sources[k + 1], evens, handed_on, kept[k + 1]))
                parts.append((sources[k + 1], odds, lambda sums, p=passed: (p, sums), kept[k + 1]))
        else:
            moms = [[mom[None]] + others(mom, "row", row_size)[:1]]
            moms += [[r] for r in others(mom, "row", row_size)[1:]]
            parts = [(a, tuple(range(n)), m, k) for a, n, m, k in zip(sources, sizes, moms, kept)]
        mom, made = add_fields(payload, parts, mom, columns if is_last else 0, False)
    (mom_sent,) = made[-1]
    mom_received = to_columns(mom_sent)
    moments, geometry, places, hot = call(
        functools.partial(geometry_kernel, slots),
        "contact_geometry",
        (
            shape(3, count),
            shape(len(contact_blocks(columns, slots)), 8, SUBS, LANES),
            shape(2, 2, columns, slot_len, dtype=jnp.int32),
            shape(2 * columns * slot_len, LANES, dtype=BF16),
        ),
        table,
        listed,
        received,
        mom,
    )
    forces = call(
        functools.partial(force_kernel, slots),
        "contact_force",
        shape(3, count),
        geometry,
        places,
        hot,
        mom_received,
        scratch=[
            pltpu.VMEM((2, 3 * PIECES, columns, slot_len), F32),
            pltpu.VMEM((3 * PIECES * groups, 2 * columns * slot_len), BF16),
        ],
    )
    return (moments, forces)


def solution(mesh):
    placed = (
        P(None, ("col", "row")),
        P(None, ("col", "row")),
        P(None, ("col", "row")),
        P(("col", "row")),
        P("col", "row", None, None),
        P("col", "row", None, None),
        P("col", "row", None),
    )
    return jax.shard_map(
        functools.partial(on_device, mesh.shape["row"]),
        mesh=mesh,
        in_specs=placed,
        out_specs=(P(None, ("col", "row")), P(None, ("col", "row"))),
        check_vma=False,
    )
```
